32 devices in a mesh: seq: 8 (over y, x, core), head: 4 (over z).
Axes of the slice: x: 2, y: 2, z: 4, core: 2. Of those that a mesh axis runs over, the one named last changes fastest.
Arguments:
- queries: bfloat16 [512, 8192], P('seq', 'head'), may hold values from -6 to 6
- keys: bfloat16 [512, 1024], P('seq'), may hold values from -6 to 6
- values: bfloat16 [512, 1024], P('seq'), may hold values from -6 to 6
- vertical: int32 [64, 8], replicated, may hold values from -1 to 7, as said below
- slash: int32 [64, 8], replicated, may hold values from -1 to 7, as said below
- plan: int32 [64], replicated, may hold values from 0 to 63, each once
Outputs:
- attended: bfloat16 [512, 8192], P('seq', 'head')
The draws below stay inside these ranges and needn't reach their ends.
Inputs may be any that keep to these rules, and one draw needn't show every extreme that they name: `vertical`: entries of 0 or more name key blocks of 64 positions; -1 marks an unused entry, and every row has at least one used entry. `slash`: entries of 0 or more are offsets back from a query's own block; -1 marks an unused entry; the first entry of every row is 0. `plan`: A permutation of the query heads.
All inputs are finite; a program needn't handle non-finite values.
Results may differ from the reference program's by a relative error of at most 0.0044.
Values may be sent and summed in bfloat16 or wider, within the bound.
No kernel may reach another device: no remote copies, remote signals or barrier semaphores. Data moves between devices by JAX's collectives and lax.ppermute only.
A program may use at most 64 MiB of HBM per device.

```python
import jax
import jax.numpy as jnp
from jax import lax

HD = 128
QH = 64
KVH = 8
BLK = 64
NV = 8
NS = 8
TOKENS = 512


def draw_queries(key, part):
    key = jax.random.fold_in(key, 3)
    return jax.random.normal(key, (TOKENS, QH * HD), jnp.float32).astype(jnp.bfloat16)


def draw_keys(key, part):
    key = jax.random.fold_in(key, 5)
    return jax.random.normal(key, (TOKENS, KVH * HD), jnp.float32).astype(jnp.bfloat16)


def draw_vertical(key, part):
    key = jax.random.fold_in(key, 7)
    block_count = TOKENS // BLK
    count_key, entry_key, head_key = jax.random.split(key, 3)
    counts = jax.random.randint(count_key, (QH,), 1, NV)
    entries = jax.random.randint(entry_key, (QH, NV), 0, block_count)
    in_use = jnp.arange(NV)[None, :] < counts[:, None]
    listing = jnp.where(in_use, entries, -1)
    forced_head = jax.random.randint(head_key, (), 0, QH)
    return listing.at[forced_head, 0].set(block_count - 1).astype(jnp.int32)


def draw_slash(key, part):
    key = jax.random.fold_in(key, 9)
    block_count = TOKENS // BLK
    count_key, entry_key, head_key = jax.random.split(key, 3)
    counts = jax.random.randint(count_key, (QH,), 2, NS)
    entries = jax.random.randint(entry_key, (QH, NS), 0, block_count)
    in_use = jnp.arange(NS)[None, :] < counts[:, None]
    listing = jnp.where(in_use, entries, -1)
    listing = listing.at[:, 0].set(0)
    forced_head = jax.random.randint(head_key, (), 0, QH)
    return listing.at[forced_head, 1].set(block_count - 1).astype(jnp.int32)


def level_of(own_key, shape, shards, least, high):
    factor_of = 1.0
    for dim, shards_of in shards:
        steps = jax.random.uniform(jax.random.fold_in(jax.random.fold_in(own_key, 6), dim), (shards_of,), jnp.float32, least / len(shards), high / len(shards))
        factor_of = factor_of * jnp.repeat(jnp.exp(steps), shape[dim] // shards_of).reshape((-1,) + (1,) * (len(shape) - 1 - dim))
    return factor_of


def normal_values(key, dims, spread, most, cuts=(), kind=jnp.bfloat16):
    level = level_of(key, dims, cuts, -0.22, 0.18) if cuts else 1.0
    values = jax.random.normal(key, dims, jnp.float32) * spread * level
    return jnp.minimum(jnp.maximum(values, -most), most).astype(kind)


def setup_inputs(seed: int = 0) -> dict:
    key_of = jax.random.split(jax.random.key(seed), 7)
    queries = draw_queries(jax.random.fold_in(key_of[6], 71), 0)
    keys = draw_keys(jax.random.fold_in(key_of[6], 71), 0)
    values = normal_values(key_of[2], (TOKENS, KVH * HD), 1.0, 6.0, ((0, 8),))
    vertical = draw_vertical(jax.random.fold_in(key_of[6], 71), 0)
    slash = draw_slash(jax.random.fold_in(key_of[6], 71), 0)
    plan = jax.random.permutation(key_of[5], QH).astype(jnp.int32)
    return dict(queries=queries, keys=keys, values=values, vertical=vertical, slash=slash, plan=plan)


def head_attention(queries3, keys3, values3, head_id, vertical_row, slash_row):
    kv_head = head_id * KVH // QH
    query_rows = jnp.take(queries3, head_id, axis=1).astype(jnp.float32)
    key_rows = jnp.take(keys3, kv_head, axis=1).astype(jnp.float32)
    value_rows = jnp.take(values3, kv_head, axis=1).astype(jnp.float32)
    block_count = TOKENS // BLK
    own_blocks = jnp.arange(block_count, dtype=jnp.int32)
    slash_blocks = own_blocks[:, None] - slash_row[None, :]
    vert_blocks = jnp.broadcast_to(vertical_row[None, :], (block_count, NV))
    candidate = jnp.concatenate([vert_blocks, slash_blocks], axis=1)
    usable = jnp.concatenate([vert_blocks >= 0, (slash_row[None, :] >= 0) & (slash_blocks >= 0)], axis=1)
    list_width = NV + NS
    earlier = jnp.arange(list_width)[:, None] > jnp.arange(list_width)[None, :]
    repeated = jnp.any(earlier[None] & usable[:, None, :] & (candidate[:, :, None] == candidate[:, None, :]), axis=2)
    usable = usable & jnp.logical_not(repeated)
    clipped = jnp.clip(candidate, 0, block_count - 1).astype(jnp.int32)
    key_blocks = key_rows.reshape(block_count, BLK, HD)[clipped]
    value_blocks = value_rows.reshape(block_count, BLK, HD)[clipped]
    query_blocks = query_rows.reshape(block_count, BLK, HD)
    scores = jnp.einsum("bqh,bckh->bqck", query_blocks, key_blocks) * (HD ** -0.5)
    query_pos = own_blocks[:, None] * BLK + jnp.arange(BLK, dtype=jnp.int32)[None, :]
    key_pos = clipped[:, :, None] * BLK + jnp.arange(BLK, dtype=jnp.int32)[None, None, :]
    allowed = usable[:, None, :, None] & (key_pos[:, None, :, :] <= query_pos[:, :, None, None])
    masked = jnp.where(allowed, scores, -1e30)
    row_max = jnp.max(masked, axis=(2, 3), keepdims=True)
    weights = jnp.where(allowed, jnp.exp(masked - row_max), 0.0)
    totals = jnp.sum(weights, axis=(2, 3))
    rounded = lax.optimization_barrier(weights.astype(jnp.bfloat16)).astype(jnp.float32)
    mixture = jnp.einsum("bqck,bckh->bqh", rounded, value_blocks)
    return (mixture / totals[:, :, None]).reshape(TOKENS, HD)


def reference(queries, keys, values, vertical, slash, plan):
    queries3 = queries.reshape(TOKENS, QH, HD)
    keys3 = keys.reshape(TOKENS, KVH, HD)
    values3 = values.reshape(TOKENS, KVH, HD)

    def one_slot(slot_id):
        head_id = plan[slot_id]
        return head_attention(queries3, keys3, values3, head_id, vertical[head_id], slash[head_id])

    results = lax.map(one_slot, jnp.arange(QH, dtype=jnp.int32))
    return jnp.transpose(results, (1, 0, 2)).reshape(TOKENS, QH * HD).astype(jnp.bfloat16)
```

```python
import functools

import jax
import jax.numpy as jnp
from jax import lax
from jax.experimental import pallas as pl
from jax.experimental.pallas import tpu as pltpu
from jax.sharding import PartitionSpec as P

HD = 128
QH = 64
KVH = 8
BLK = 64
GROUP = QH // KVH

floor_value = -1e30


def entry_bits(table, row):
    bits = jnp.int32(0)
    for entry in range(table.shape[1]):
        named = table[row, entry]
        bits = bits | jnp.where(named >= 0, jnp.int32(1) << jnp.maximum(named, 0), 0)
    return bits


def attention_kernel(seq_size, head_size, slot_count, plan, vertical, slash, *refs):
    query_refs = refs[:head_size]
    kv_refs = refs[head_size : head_size + seq_size]
    out_ref = refs[-1]
    query_len = out_ref.shape[0]
    key_len = kv_refs[0].shape[0]
    held_heads = query_refs[0].shape[1] // HD
    own_seq = lax.axis_index("seq")
    own_head = lax.axis_index("head")

    back = lax.broadcasted_iota(jnp.int32, (1, seq_size * key_len), 1) // key_len
    block = own_seq - back
    block_shift = jnp.maximum(block, 0)
    row = lax.broadcasted_iota(jnp.int32, (query_len, seq_size * key_len), 0)
    column = lax.broadcasted_iota(jnp.int32, (query_len, seq_size * key_len), 1)
    causal = (column <= row) | (column >= key_len)
    score_scale = HD ** (-0.5)

    def slot(j):
        head = plan[own_head * slot_count + j]
        owner = head // held_heads
        held_at = pl.multiple_of((head - owner * held_heads) * HD, HD)
        steps = own_head - owner
        steps = jnp.where(steps < 0, steps + head_size, steps)
        query = query_refs[0][:, pl.ds(held_at, HD)]
        for d in range(1, head_size):
            query = jnp.where(steps == d, query_refs[d][:, pl.ds(held_at, HD)], query)
        kv_head = head // GROUP
        key_at = pl.multiple_of(kv_head * HD, HD)
        value_at = pl.multiple_of((kv_head + KVH) * HD, HD)
        key = jnp.concatenate([ref[:, pl.ds(key_at, HD)] for ref in kv_refs], axis=0)
        value = jnp.concatenate([ref[:, pl.ds(value_at, HD)] for ref in kv_refs], axis=0)
        vertical_bits = entry_bits(vertical, head)
        slash_bits = entry_bits(slash, head)
        hit = ((vertical_bits >> block_shift) | (slash_bits >> back)) & 1
        listed = (hit == 1) & (block >= 0)
        scores = lax.dot_general(
            query, key, (((1,), (1,)), ((), ())), preferred_element_type=jnp.float32
        )
        masked = jnp.where(causal & listed, scores, floor_value)
        row_max = jnp.max(masked, axis=1, keepdims=True)
        weights = jnp.exp((masked - row_max) * score_scale)
        totals = jnp.sum(weights, axis=1, keepdims=True)
        mixture = jnp.dot(
            weights.astype(jnp.bfloat16), value, preferred_element_type=jnp.float32
        )
        out_ref[:, pl.ds(pl.multiple_of(j * HD, HD), HD)] = (mixture / totals).astype(out_ref.dtype)

    for j in range(slot_count):
        slot(j)


def per_device(queries, keys, values, vertical, slash, plan):
    seq_size = lax.axis_size("seq")
    head_size = lax.axis_size("head")
    slot_count = plan.shape[0] // head_size
    query_len = queries.shape[0]
    assert query_len == BLK

    kv = jnp.concatenate([keys, values], axis=1)
    query_pieces = [queries]
    for d in range(1, head_size):
        query_pieces.append(
            lax.ppermute(queries, "head", [(i, (i + d) % head_size) for i in range(head_size)])
        )
    kv_pieces = [kv]
    for d in range(1, seq_size):
        kv_pieces.append(lax.ppermute(kv, "seq", [(i, i + d) for i in range(seq_size - d)]))

    smem = pl.BlockSpec(memory_space=pltpu.SMEM)
    vmem = pl.BlockSpec(memory_space=pltpu.VMEM)
    return pl.pallas_call(
        functools.partial(attention_kernel, seq_size, head_size, slot_count),
        out_shape=jax.ShapeDtypeStruct((query_len, slot_count * HD), jnp.bfloat16),
        in_specs=[smem] * 3 + [vmem] * (head_size + seq_size),
        out_specs=vmem,
        compiler_params=pltpu.CompilerParams(vmem_limit_bytes=40 * 1024 * 1024),
        name="attention",
    )(plan, vertical, slash, *query_pieces, *kv_pieces)


def solution(mesh):
    in_specs = (P("seq", "head"), P("seq", None), P("seq", None), P(), P(), P())
    out_specs = P("seq", "head")
    return jax.shard_map(
        per_device, mesh=mesh, in_specs=in_specs, out_specs=out_specs, check_vma=False
    )
```

```python
import functools

import jax
import jax.numpy as jnp
from jax import lax
from jax.experimental import pallas as pl
from jax.experimental.pallas import tpu as pltpu
from jax.sharding import PartitionSpec as P

HD = 128
QH = 64
KVH = 8
BLK = 64
GROUP = QH // KVH
SLOTS_AT_ONCE = 4

floor_value = -1e30


def entry_bits(table, row):
    bits = jnp.int32(0)
    for entry in range(table.shape[1]):
        named = table[row, entry]
        bits = bits | jnp.where(named >= 0, jnp.int32(1) << jnp.maximum(named, 0), 0)
    return bits


def attention_kernel(seq_size, head_size, slot_count, plan, vertical, slash, *refs):
    kv_refs = refs[:seq_size]
    query_ref = refs[seq_size]
    out_ref = refs[-1]
    query_len = out_ref.shape[0]
    key_len = kv_refs[0].shape[0]
    held_heads = query_ref.shape[2] // HD
    own_seq = lax.axis_index("seq")
    own_head = lax.axis_index("head")
    chips = seq_size // 2

    piece = lax.broadcasted_iota(jnp.int32, (1, seq_size * key_len), 1) // key_len
    first_block = jnp.where(piece < chips, own_seq, own_seq + 1 - 2 * (own_seq % 2))
    block = first_block - 2 * (piece % chips)
    back = own_seq - block
    present = (block >= 0) & (back >= 0)
    block_shift = jnp.maximum(block, 0)
    back_shift = jnp.maximum(back, 0)
    row = lax.broadcasted_iota(jnp.int32, (query_len, seq_size * key_len), 0)
    column = lax.broadcasted_iota(jnp.int32, (query_len, seq_size * key_len), 1)
    causal = (column <= row) | (column >= key_len)
    score_scale = HD ** (-0.5)

    for lead in range(0, slot_count, SLOTS_AT_ONCE):
        slots = range(lead, min(lead + SLOTS_AT_ONCE, slot_count))
        heads = [plan[own_head * slot_count + j] for j in slots]
        masked = []
        for head in heads:
            owner = head // held_heads
            held_at = pl.multiple_of((head - owner * held_heads) * HD, HD)
            query = query_ref[owner, :, pl.ds(held_at, HD)]
            key_at = pl.multiple_of(head // GROUP * HD, HD)
            key = jnp.concatenate([ref[:, pl.ds(key_at, HD)] for ref in kv_refs], axis=0)
            scores = lax.dot_general(
                query, key, (((1,), (1,)), ((), ())), preferred_element_type=jnp.float32
            )
            vertical_bits = entry_bits(vertical, head)
            slash_bits = entry_bits(slash, head)
            hit = ((vertical_bits >> block_shift) | (slash_bits >> back_shift)) & 1
            listed = (hit == 1) & present
            masked.append(jnp.where(causal & listed, scores, floor_value))
        row_max = [jnp.max(m, axis=1, keepdims=True) for m in masked]
        weights = [jnp.exp((m - top) * score_scale) for m, top in zip(masked, row_max)]
        totals = [jnp.sum(w, axis=1, keepdims=True) for w in weights]
        mixture = []
        for head, w in zip(heads, weights):
            value_at = pl.multiple_of((head // GROUP + KVH) * HD, HD)
            value = jnp.concatenate([ref[:, pl.ds(value_at, HD)] for ref in kv_refs], axis=0)
            mixture.append(
                jnp.dot(w.astype(jnp.bfloat16), value, preferred_element_type=jnp.float32)
            )
        for j, mix, total in zip(slots, mixture, totals):
            out_ref[:, j * HD : (j + 1) * HD] = (mix / total).astype(out_ref.dtype)


def per_device(queries, keys, values, vertical, slash, plan):
    seq_size = lax.axis_size("seq")
    head_size = lax.axis_size("head")
    slot_count = plan.shape[0] // head_size
    query_len = queries.shape[0]
    assert query_len == BLK and seq_size % 2 == 0

    all_queries = lax.all_to_all(
        jnp.broadcast_to(queries[None], (head_size,) + queries.shape), "head", 0, 0
    )
    kv = jnp.concatenate([keys, values], axis=1)
    same_core = [kv]
    for e in range(1, seq_size // 2):
        same_core.append(lax.ppermute(kv, "seq", [(i, i + 2 * e) for i in range(seq_size - 2 * e)]))
    other_core = [lax.ppermute(kv, "seq", [(i, i + 1) for i in range(0, seq_size, 2)])]
    for e in range(1, seq_size // 2):
        pairs = [(i, i ^ 1) for i in range(2 * e, seq_size)]
        other_core.append(lax.ppermute(same_core[e], "seq", pairs))

    smem = pl.BlockSpec(memory_space=pltpu.SMEM)
    vmem = pl.BlockSpec(memory_space=pltpu.VMEM)
    return pl.pallas_call(
        functools.partial(attention_kernel, seq_size, head_size, slot_count),
        out_shape=jax.ShapeDtypeStruct((query_len, slot_count * HD), jnp.bfloat16),
        in_specs=[smem] * 3 + [vmem] * (seq_size + 1),
        out_specs=vmem,
        compiler_params=pltpu.CompilerParams(vmem_limit_bytes=40 * 1024 * 1024),
        name="attention",
    )(plan, vertical, slash, *same_core, *other_core, all_queries)


def solution(mesh):
    in_specs = (P("seq", "head"), P("seq", None), P("seq", None), P(), P(), P())
    out_specs = P("seq", "head")
    return jax.shard_map(
        per_device, mesh=mesh, in_specs=in_specs, out_specs=out_specs, check_vma=False
    )
```

```python
import functools

import jax
import jax.numpy as jnp
from jax import lax
from jax.experimental import pallas as pl
from jax.experimental.pallas import tpu as pltpu
from jax.sharding import PartitionSpec as P

HD = 128
QH = 64
KVH = 8
BLK = 64
GROUP = QH // KVH
HEADS_AT_ONCE = 4

floor_value = -1e30

SMEM = pl.BlockSpec(memory_space=pltpu.SMEM)
VMEM = pl.BlockSpec(memory_space=pltpu.VMEM)


def shift_of(size):
    assert size & (size - 1) == 0
    return size.bit_length() - 1


def route_kernel(head_size, held, plan, send, receive, most, counts):
    own = lax.axis_index("head")
    for pair in range(head_size * head_size):
        counts[pair] = 0
    largest = jnp.int32(0)
    for slot in range(plan.shape[0]):
        target = slot // held
        head = plan[slot]
        owner = head >> shift_of(held)
        pair = owner * head_size + target
        rank = counts[pair]
        counts[pair] = rank + 1
        largest = jnp.maximum(largest, jnp.where(owner == target, 0, rank + 1))
        place = ((target - owner) & (head_size - 1)) * held + rank
        send[jnp.where(owner == own, head & (held - 1), held)] = place
        receive[jnp.where(own == target, slot % held, held)] = place
    most[0] = largest


def entry_bits(table, row):
    bits = jnp.int32(0)
    for entry in range(table.shape[1]):
        named = table[row, entry]
        bits = bits | jnp.where(named >= 0, jnp.int32(1) << jnp.maximum(named, 0), 0)
    return bits


def attention_kernel(seq_size, held, kv_heads, send, vertical, slash, kv_own, kv_other, query_ref, out_ref):
    query_len = query_ref.shape[0]
    key_len = query_len
    own_seq = lax.axis_index("seq")
    own_head = lax.axis_index("head")
    chips = seq_size // 2
    half = chips * key_len

    piece = lax.broadcasted_iota(jnp.int32, (1, 2 * half), 1) // key_len
    core = jnp.where(piece < chips, own_seq & 1, 1 - (own_seq & 1))
    block = ((own_seq >> 1) ^ (piece & (chips - 1))) * 2 + core
    back = own_seq - block
    present = back >= 0
    back_shift = jnp.maximum(back, 0)
    row = lax.broadcasted_iota(jnp.int32, (query_len, 2 * half), 0)
    column = lax.broadcasted_iota(jnp.int32, (query_len, 2 * half), 1)
    causal = (column <= row) | (column >= key_len)
    score_scale = HD ** (-0.5)
    per_kv = held // kv_heads

    for lead in range(0, held, HEADS_AT_ONCE):
        heads = range(lead, min(lead + HEADS_AT_ONCE, held))
        kv_head = lead // per_kv
        key_at = kv_head * HD
        value_at = (kv_head + kv_heads) * HD
        key = jnp.concatenate([kv_own[:, key_at : key_at + HD], kv_other[:, key_at : key_at + HD]], axis=0)
        value = jnp.concatenate(
            [kv_own[:, value_at : value_at + HD], kv_other[:, value_at : value_at + HD]], axis=0
        )
        query = jnp.concatenate([query_ref[:, i * HD : (i + 1) * HD] for i in heads], axis=0)
        scores = lax.dot_general(
            query, key, (((1,), (1,)), ((), ())), preferred_element_type=jnp.float32
        )
        weights = []
        totals = []
        for at, i in enumerate(heads):
            head = own_head * held + i
            vertical_bits = entry_bits(vertical, head)
            slash_bits = entry_bits(slash, head)
            hit = ((vertical_bits >> block) | (slash_bits >> back_shift)) & 1
            listed = (hit == 1) & present
            own_scores = scores[at * query_len : (at + 1) * query_len]
            masked = jnp.where(causal & listed, own_scores, floor_value)
            row_max = jnp.max(masked, axis=1, keepdims=True)
            weight = jnp.exp((masked - row_max) * score_scale)
            totals.append(jnp.sum(weight, axis=1, keepdims=True))
            weights.append(weight.astype(jnp.bfloat16))
        mixture = jnp.dot(
            jnp.concatenate(weights, axis=0), value, preferred_element_type=jnp.float32
        )
        for at, i in enumerate(heads):
            mix = mixture[at * query_len : (at + 1) * query_len]
            out_ref[send[i]] = (mix / totals[at]).astype(out_ref.dtype)


def place_kernel(held, receive, kept, *refs):
    arrived = refs[:-1]
    out_ref = refs[-1]
    capacity = arrived[0].shape[0]
    for t in range(out_ref.shape[1] // HD):
        place = receive[t]
        distance = place >> shift_of(held)
        rank = place & (held - 1)
        rows = kept[rank]
        rank_sent = jnp.minimum(rank, capacity - 1)
        for d, ref in enumerate(arrived):
            rows = jnp.where(distance == d + 1, ref[rank_sent], rows)
        out_ref[:, t * HD : (t + 1) * HD] = rows


def exchange(head_size, held, capacity, packed, receive):
    arrived = []
    for d in range(1, head_size):
        arrived.append(
            lax.ppermute(
                packed[d * held : d * held + capacity],
                "head",
                [(i, (i + d) % head_size) for i in range(head_size)],
            )
        )
    query_len = packed.shape[1]
    return pl.pallas_call(
        functools.partial(place_kernel, held),
        out_shape=jax.ShapeDtypeStruct((query_len, held * HD), packed.dtype),
        in_specs=[SMEM] + [VMEM] * head_size,
        out_specs=VMEM,
        name="place",
    )(receive, packed[:held], *arrived)


def per_device(queries, keys, values, vertical, slash, plan):
    seq_size = lax.axis_size("seq")
    head_size = lax.axis_size("head")
    query_len = queries.shape[0]
    held = queries.shape[1] // HD
    kv_heads = max(1, held // GROUP)
    chips = seq_size // 2
    assert query_len == BLK and plan.shape[0] == held * head_size and chips & (chips - 1) == 0

    send, receive, most = pl.pallas_call(
        functools.partial(route_kernel, head_size, held),
        out_shape=[
            jax.ShapeDtypeStruct((held + 1,), jnp.int32),
            jax.ShapeDtypeStruct((held + 1,), jnp.int32),
            jax.ShapeDtypeStruct((1,), jnp.int32),
        ],
        in_specs=[SMEM],
        out_specs=[SMEM] * 3,
        scratch_shapes=[pltpu.SMEM((head_size * head_size,), jnp.int32)],
        name="route",
    )(plan)

    kv_at = lax.axis_index("head") * held // GROUP * HD
    kv = jnp.concatenate(
        [lax.dynamic_slice_in_dim(rows, kv_at, kv_heads * HD, axis=1) for rows in (keys, values)], axis=1
    )
    pieces = [kv]
    for m in range(1, chips):
        pairs = [(i, i ^ (2 * m)) for i in range(seq_size) if i < i ^ (2 * m)]
        pieces.append(lax.ppermute(kv, "seq", pairs))
    kv_own = jnp.concatenate(pieces, axis=0)
    kv_other = lax.ppermute(kv_own, "seq", [(i, i ^ 1) for i in range(seq_size)])

    packed = pl.pallas_call(
        functools.partial(attention_kernel, seq_size, held, kv_heads),
        out_shape=jax.ShapeDtypeStruct((head_size * held, query_len, HD), jnp.bfloat16),
        in_specs=[SMEM] * 3 + [VMEM] * 3,
        out_specs=VMEM,
        compiler_params=pltpu.CompilerParams(vmem_limit_bytes=40 * 1024 * 1024),
        name="attention",
    )(send, vertical, slash, kv_own, kv_other, queries)

    capacities = sorted({c for c in (held * 3 // 8, held // 2) if c} | {held})
    level = jnp.int32(0)
    for capacity in capacities[:-1]:
        level = level + (most[0] > capacity).astype(jnp.int32)
    return lax.switch(
        level,
        [functools.partial(exchange, head_size, held, capacity) for capacity in capacities],
        packed,
        receive,
    )


def solution(mesh):
    in_specs = (P("seq", "head"), P("seq", None), P("seq", None), P(), P(), P())
    out_specs = P("seq", "head")
    return jax.shard_map(
        per_device, mesh=mesh, in_specs=in_specs, out_specs=out_specs, check_vma=False
    )
```

```python
import functools
import math

import jax
import jax.numpy as jnp
from jax import lax
from jax.experimental import pallas as pl
from jax.experimental.pallas import tpu as pltpu
from jax.sharding import PartitionSpec as P

HD = 128
QH = 64
KVH = 8
BLK = 64
GROUP = QH // KVH
HEADS_AT_ONCE = 4
LANES = 128

floor_value = -1e30

SMEM = pl.BlockSpec(memory_space=pltpu.SMEM)
VMEM = pl.BlockSpec(memory_space=pltpu.VMEM)
ANY = pl.BlockSpec(memory_space=pl.ANY)
SMALL = 1024 * 1024


def shift_of(size):
    assert size & (size - 1) == 0
    return size.bit_length() - 1


def entry_bits(table, row):
    bits = jnp.int32(0)
    for entry in range(table.shape[0]):
        named = table[entry, row]
        bits = bits | jnp.where(named >= 0, jnp.int32(1) << jnp.maximum(named, 0), 0)
    return bits


def route_kernel(head_size, held, capacities, plan, vertical, slash, send, receive, level, counts):
    own = lax.axis_index("head")
    for pair in range(head_size * head_size):
        counts[pair] = 0
    largest = jnp.int32(0)
    for slot in range(plan.shape[0]):
        target = slot // held
        head = plan[slot]
        owner = head >> shift_of(held)
        pair = owner * head_size + target
        rank = counts[pair]
        counts[pair] = rank + 1
        largest = jnp.maximum(largest, jnp.where(owner == target, 0, rank + 1))
        place = ((target - owner) & (head_size - 1)) * held + rank
        send[jnp.where(owner == own, head & (held - 1), held)] = place
        receive[jnp.where(own == target, slot % held, held)] = place
    chosen = jnp.int32(0)
    for capacity in capacities[:-1]:
        chosen = chosen + (largest > capacity).astype(jnp.int32)
    level[0] = chosen
    for i in range(held):
        send[held + 1 + i] = entry_bits(vertical, own * held + i)
        send[2 * held + 1 + i] = entry_bits(slash, own * held + i)


def attention_kernel(seq_size, held, kv_heads, send, kv_own, kv_other, query_ref, out_ref):
    query_len = query_ref.shape[0]
    key_len = query_len
    own_seq = lax.axis_index("seq")
    chips = seq_size // 2
    half = chips * key_len

    piece = lax.broadcasted_iota(jnp.int32, (1, 2 * half), 1) // key_len
    core = jnp.where(piece < chips, own_seq & 1, 1 - (own_seq & 1))
    block = ((own_seq >> 1) ^ (piece & (chips - 1))) * 2 + core
    back = own_seq - block
    present = back >= 0
    back_shift = jnp.maximum(back, 0)
    row = lax.broadcasted_iota(jnp.int32, (query_len, LANES), 0)
    column = lax.broadcasted_iota(jnp.int32, (query_len, LANES), 1)
    causal = (column <= row) | (column >= key_len)
    score_scale = HD ** (-0.5) * math.log2(math.e)
    per_kv = held // kv_heads

    def scores_of(lead):
        heads = range(lead, min(lead + HEADS_AT_ONCE, held))
        key_at = lead // per_kv * HD
        key = jnp.concatenate([kv_own[:, key_at : key_at + HD], kv_other[:, key_at : key_at + HD]], axis=0)
        query = jnp.concatenate([query_ref[:, i * HD : (i + 1) * HD] for i in heads], axis=0)
        return lax.dot_general(
            query, key, (((1,), (1,)), ((), ())), preferred_element_type=jnp.float32
        )

    following = scores_of(0)
    for lead in range(0, held, HEADS_AT_ONCE):
        heads = range(lead, min(lead + HEADS_AT_ONCE, held))
        scores = following
        if lead + HEADS_AT_ONCE < held:
            following = scores_of(lead + HEADS_AT_ONCE)
        value_at = (lead // per_kv + kv_heads) * HD
        value = jnp.concatenate(
            [kv_own[:, value_at : value_at + HD], kv_other[:, value_at : value_at + HD]], axis=0
        )
        weights = []
        totals = []
        for at, i in enumerate(heads):
            hit = ((send[held + 1 + i] >> block) | (send[2 * held + 1 + i] >> back_shift)) & 1
            bias = jnp.where((hit == 1) & present, 0.0, floor_value)
            masked = scores[at * query_len : (at + 1) * query_len] + bias
            masked = jnp.concatenate(
                [jnp.where(causal, masked[:, :LANES], floor_value), masked[:, LANES:]], axis=1
            )
            row_max = jnp.max(masked, axis=1, keepdims=True)
            weight = jnp.exp2((masked - row_max) * score_scale)
            totals.append(1.0 / jnp.sum(weight, axis=1, keepdims=True))
            weights.append(weight.astype(jnp.bfloat16))
        mixture = jnp.dot(
            jnp.concatenate(weights, axis=0), value, preferred_element_type=jnp.float32
        )
        for at, i in enumerate(heads):
            mix = mixture[at * query_len : (at + 1) * query_len]
            out_ref[send[i]] = (mix * totals[at]).astype(out_ref.dtype)


def place_kernel(held, receive, packed, *refs):
    arrived = refs[:-2]
    out_ref, done = refs[-2:]
    slots = out_ref.shape[1] // HD
    for t in range(slots):
        place = receive[t]
        distance = place >> shift_of(held)
        rank = place & (held - 1)
        for d, ref in enumerate((packed,) + arrived):

            @pl.when(distance == d)
            def _(ref=ref):
                pltpu.make_async_copy(ref.at[rank], out_ref.at[:, pl.ds(t * HD, HD)], done.at[t]).start()

    for t in range(slots):
        pltpu.make_async_copy(packed.at[0], out_ref.at[:, pl.ds(t * HD, HD)], done.at[t]).wait()


def exchange(head_size, held, capacity, packed, receive):
    arrived = []
    for d in range(1, head_size):
        arrived.append(
            lax.ppermute(
                packed[d * held : d * held + capacity],
                "head",
                [(i, (i + d) % head_size) for i in range(head_size)],
            )
        )
    return pl.pallas_call(
        functools.partial(place_kernel, held),
        out_shape=jax.ShapeDtypeStruct((packed.shape[1], held * HD), packed.dtype),
        in_specs=[SMEM] + [ANY] * head_size,
        out_specs=ANY,
        scratch_shapes=[pltpu.SemaphoreType.DMA((held,))],
        compiler_params=pltpu.CompilerParams(vmem_limit_bytes=SMALL),
        name="place",
    )(receive, packed, *arrived)


def per_device(queries, keys, values, vertical, slash, plan):
    seq_size = lax.axis_size("seq")
    head_size = lax.axis_size("head")
    query_len = queries.shape[0]
    held = queries.shape[1] // HD
    kv_heads = max(1, held // GROUP)
    chips = seq_size // 2
    assert query_len == BLK and plan.shape[0] == held * head_size and chips & (chips - 1) == 0

    capacities = sorted({held * c // 16 for c in (5, 6, 7, 8, 16)} - {0})
    send, receive, level = pl.pallas_call(
        functools.partial(route_kernel, head_size, held, capacities),
        out_shape=[
            jax.ShapeDtypeStruct((3 * held + 1,), jnp.int32),
            jax.ShapeDtypeStruct((held + 1,), jnp.int32),
            jax.ShapeDtypeStruct((1,), jnp.int32),
        ],
        in_specs=[SMEM] * 3,
        out_specs=[SMEM] * 3,
        scratch_shapes=[pltpu.SMEM((head_size * head_size,), jnp.int32)],
        compiler_params=pltpu.CompilerParams(vmem_limit_bytes=SMALL),
        name="route",
    )(plan, vertical.T, slash.T)

    kv_at = lax.axis_index("head") * held // GROUP * HD
    kv = jnp.concatenate(
        [lax.dynamic_slice_in_dim(rows, kv_at, kv_heads * HD, axis=1) for rows in (keys, values)], axis=1
    )
    pieces = [kv]
    for m in range(1, chips):
        pairs = [(i, i ^ (2 * m)) for i in range(seq_size)]
        pieces.append(lax.ppermute(kv, "seq", pairs))
    kv_own = jnp.concatenate(pieces, axis=0)
    kv_other = lax.ppermute(kv_own, "seq", [(i, i ^ 1) for i in range(seq_size)])

    packed = pl.pallas_call(
        functools.partial(attention_kernel, seq_size, held, kv_heads),
        out_shape=jax.ShapeDtypeStruct((head_size * held, query_len, HD), jnp.bfloat16),
        in_specs=[SMEM] + [VMEM] * 3,
        out_specs=VMEM,
        compiler_params=pltpu.CompilerParams(vmem_limit_bytes=40 * 1024 * 1024),
        name="attention",
    )(send, kv_own, kv_other, queries)

    return lax.switch(
        level[0],
        [functools.partial(exchange, head_size, held, capacity) for capacity in capacities],
        packed,
        receive,
    )


def solution(mesh):
    in_specs = (P("seq", "head"), P("seq", None), P("seq", None), P(), P(), P())
    out_specs = P("seq", "head")
    return jax.shard_map(
        per_device, mesh=mesh, in_specs=in_specs, out_specs=out_specs, check_vma=False
    )
```

```python
import functools
import math

import jax
import jax.numpy as jnp
from jax import lax
from jax.experimental import pallas as pl
from jax.experimental.pallas import tpu as pltpu
from jax.sharding import PartitionSpec as P

HD = 128
QH = 64
KVH = 8
BLK = 64
GROUP = QH // KVH
HEADS_AT_ONCE = 4
LANES = 128

floor_value = -1e30

SMEM = pl.BlockSpec(memory_space=pltpu.SMEM)
VMEM = pl.BlockSpec(memory_space=pltpu.VMEM)
ANY = pl.BlockSpec(memory_space=pl.ANY)
SMALL = 1024 * 1024


def shift_of(size):
    assert size & (size - 1) == 0
    return size.bit_length() - 1


def entry_bits(table, row):
    bits = jnp.int32(0)
    for entry in range(table.shape[0]):
        named = table[entry, row]
        bits = bits | jnp.where(named >= 0, jnp.int32(1) << jnp.maximum(named, 0), 0)
    return bits


def route_kernel(head_size, held, levels, plan, vertical, slash, send, receive, level, counts, most):
    own = lax.axis_index("head")
    for pair in range(head_size * head_size):
        counts[pair] = 0
    for distance in range(head_size):
        most[distance] = 0
    for slot in range(plan.shape[0]):
        target = slot // held
        head = plan[slot]
        owner = head >> shift_of(held)
        pair = owner * head_size + target
        rank = counts[pair]
        counts[pair] = rank + 1
        distance = owner ^ target
        most[distance] = jnp.maximum(most[distance], rank + 1)
        place = distance * held + rank
        send[jnp.where(owner == own, head & (held - 1), held)] = place
        receive[jnp.where(own == target, slot % held, held)] = place
    chosen = jnp.int32(len(levels) - 1)
    for index in reversed(range(len(levels) - 1)):
        fits = most[1] <= levels[index][1]
        for distance in range(2, head_size):
            fits = fits & (most[distance] <= levels[index][distance])
        chosen = jnp.where(fits, index, chosen)
    level[0] = chosen
    for i in range(held):
        send[held + 1 + i] = entry_bits(vertical, own * held + i)
        send[2 * held + 1 + i] = entry_bits(slash, own * held + i)


def attention_kernel(seq_size, held, kv_heads, send, kv_own, kv_other, query_ref, out_ref):
    query_len = query_ref.shape[0]
    key_len = query_len
    own_seq = lax.axis_index("seq")
    chips = seq_size // 2
    half = chips * key_len

    piece = lax.broadcasted_iota(jnp.int32, (1, 2 * half), 1) // key_len
    core = jnp.where(piece < chips, own_seq & 1, 1 - (own_seq & 1))
    block = ((own_seq >> 1) ^ (piece & (chips - 1))) * 2 + core
    back = own_seq - block
    present = back >= 0
    back_shift = jnp.maximum(back, 0)
    row = lax.broadcasted_iota(jnp.int32, (query_len, LANES), 0)
    column = lax.broadcasted_iota(jnp.int32, (query_len, LANES), 1)
    causal = (column <= row) | (column >= key_len)
    score_scale = HD ** (-0.5) * math.log2(math.e)
    per_kv = held // kv_heads

    def scores_of(lead):
        heads = range(lead, min(lead + HEADS_AT_ONCE, held))
        key_at = lead // per_kv * HD
        key = jnp.concatenate([kv_own[:, key_at : key_at + HD], kv_other[:, key_at : key_at + HD]], axis=0)
        query = jnp.concatenate([query_ref[:, i * HD : (i + 1) * HD] for i in heads], axis=0)
        return lax.dot_general(
            query, key, (((1,), (1,)), ((), ())), preferred_element_type=jnp.float32
        )

    following = scores_of(0)
    for lead in range(0, held, HEADS_AT_ONCE):
        heads = range(lead, min(lead + HEADS_AT_ONCE, held))
        scores = following
        if lead + HEADS_AT_ONCE < held:
            following = scores_of(lead + HEADS_AT_ONCE)
        value_at = (lead // per_kv + kv_heads) * HD
        value = jnp.concatenate(
            [kv_own[:, value_at : value_at + HD], kv_other[:, value_at : value_at + HD]], axis=0
        )
        weights = []
        totals = []
        for at, i in enumerate(heads):
            hit = ((send[held + 1 + i] >> block) | (send[2 * held + 1 + i] >> back_shift)) & 1
            bias = jnp.where((hit == 1) & present, 0.0, floor_value)
            masked = scores[at * query_len : (at + 1) * query_len] + bias
            masked = jnp.concatenate(
                [jnp.where(causal, masked[:, :LANES], floor_value), masked[:, LANES:]], axis=1
            )
            row_max = jnp.max(masked, axis=1, keepdims=True)
            weight = jnp.exp2((masked - row_max) * score_scale)
            totals.append(1.0 / jnp.sum(weight, axis=1, keepdims=True))
            weights.append(weight.astype(jnp.bfloat16))
        mixture = jnp.dot(
            jnp.concatenate(weights, axis=0), value, preferred_element_type=jnp.float32
        )
        for at, i in enumerate(heads):
            mix = mixture[at * query_len : (at + 1) * query_len]
            out_ref[send[i]] = (mix * totals[at]).astype(out_ref.dtype)


def place_kernel(held, order, receive, packed, *refs):
    arrived = refs[:-2]
    out_ref, done = refs[-2:]
    slots = out_ref.shape[1] // HD
    for t in range(slots):
        place = receive[t]
        distance = place >> shift_of(held)
        rank = place & (held - 1)
        for m, ref in zip([0] + order, (packed,) + arrived):

            @pl.when(distance == m)
            def _(ref=ref):
                pltpu.make_async_copy(ref.at[rank], out_ref.at[:, pl.ds(t * HD, HD)], done.at[t]).start()

    for t in range(slots):
        pltpu.make_async_copy(packed.at[0], out_ref.at[:, pl.ds(t * HD, HD)], done.at[t]).wait()


def capacity_levels(head_size, held):
    near = max(1, held * 9 // 16)
    steps = sorted({max(1, held * c // 16) for c in (5, 6, 7, 8)})
    even_odd = sorted(((b, c) for b in steps for c in steps), key=sum)
    levels = [
        tuple(near if m < head_size // 2 else far[m % 2] for m in range(head_size)) for far in even_odd
    ]
    return levels + [(max(1, held * 10 // 16),) * head_size, (held,) * head_size]


def exchange(head_size, held, capacities, packed, receive):
    order = sorted(range(1, head_size), key=lambda m: (m >= head_size // 2, -m))
    arrived = {}
    for m in order:
        arrived[m] = lax.ppermute(
            packed[m * held : m * held + capacities[m]],
            "head",
            [(i, i ^ m) for i in range(head_size)],
        )
    return pl.pallas_call(
        functools.partial(place_kernel, held, order),
        out_shape=pltpu.HBM((packed.shape[1], held * HD), packed.dtype),
        in_specs=[SMEM] + [ANY] * head_size,
        out_specs=pl.BlockSpec(memory_space=pltpu.HBM),
        scratch_shapes=[pltpu.SemaphoreType.DMA((held,))],
        compiler_params=pltpu.CompilerParams(vmem_limit_bytes=SMALL),
        name="place",
    )(receive, packed, *(arrived[m] for m in order))


def per_device(queries, keys, values, vertical, slash, plan):
    seq_size = lax.axis_size("seq")
    head_size = lax.axis_size("head")
    query_len = queries.shape[0]
    held = queries.shape[1] // HD
    kv_heads = max(1, held // GROUP)
    chips = seq_size // 2
    assert query_len == BLK and plan.shape[0] == held * head_size and chips & (chips - 1) == 0

    levels = capacity_levels(head_size, held)
    send, receive, level = pl.pallas_call(
        functools.partial(route_kernel, head_size, held, levels),
        out_shape=[
            jax.ShapeDtypeStruct((3 * held + 1,), jnp.int32),
            jax.ShapeDtypeStruct((held + 1,), jnp.int32),
            jax.ShapeDtypeStruct((1,), jnp.int32),
        ],
        in_specs=[SMEM] * 3,
        out_specs=[SMEM] * 3,
        scratch_shapes=[
            pltpu.SMEM((head_size * head_size,), jnp.int32),
            pltpu.SMEM((head_size,), jnp.int32),
        ],
        compiler_params=pltpu.CompilerParams(vmem_limit_bytes=SMALL),
        name="route",
    )(plan, vertical.T, slash.T)

    kv_at = lax.axis_index("head") * held // GROUP * HD
    kv = jnp.concatenate(
        [lax.dynamic_slice_in_dim(rows, kv_at, kv_heads * HD, axis=1) for rows in (keys, values)], axis=1
    )
    pieces = [kv]
    for m in range(1, chips):
        pairs = [(i, i ^ (2 * m)) for i in range(seq_size)]
        pieces.append(lax.ppermute(kv, "seq", pairs))
    pieces, send, receive, level = lax.optimization_barrier((pieces, send, receive, level))
    kv_own = jnp.concatenate(pieces, axis=0)
    kv_other = lax.ppermute(kv_own, "seq", [(i, i ^ 1) for i in range(seq_size)])

    packed = pl.pallas_call(
        functools.partial(attention_kernel, seq_size, held, kv_heads),
        out_shape=jax.ShapeDtypeStruct((head_size * held, query_len, HD), jnp.bfloat16),
        in_specs=[SMEM] + [VMEM] * 3,
        out_specs=VMEM,
        compiler_params=pltpu.CompilerParams(vmem_limit_bytes=40 * 1024 * 1024),
        name="attention",
    )(send, kv_own, kv_other, queries)

    return lax.switch(
        level[0],
        [functools.partial(exchange, head_size, held, capacities) for capacities in levels],
        packed,
        receive,
    )


def solution(mesh):
    in_specs = (P("seq", "head"), P("seq", None), P("seq", None), P(), P(), P())
    out_specs = P("seq", "head")
    return jax.shard_map(
        per_device, mesh=mesh, in_specs=in_specs, out_specs=out_specs, check_vma=False
    )
```

```python
import functools
import math

import jax
import jax.numpy as jnp
from jax import lax
from jax.experimental import pallas as pl
from jax.experimental.pallas import tpu as pltpu
from jax.sharding import PartitionSpec as P

HD = 128
QH = 64
KVH = 8
BLK = 64
GROUP = QH // KVH
HEADS_AT_ONCE = 4
LANES = 128

floor_value = -1e30

SMEM = pl.BlockSpec(memory_space=pltpu.SMEM)
VMEM = pl.BlockSpec(memory_space=pltpu.VMEM)
ANY = pl.BlockSpec(memory_space=pl.ANY)
SMALL = 1024 * 1024


def shift_of(size):
    assert size & (size - 1) == 0
    return size.bit_length() - 1


def entry_bits(table):
    bits = jnp.zeros((1, table.shape[1]), jnp.int32)
    for entry in range(table.shape[0]):
        named = table[entry : entry + 1, :]
        bits = bits | jnp.where(named >= 0, jnp.int32(1) << jnp.maximum(named, 0), 0)
    return bits


class Tally:
    def __init__(self, head_size, held):
        self.width = shift_of(held) + 1
        self.per_word = 31 // self.width
        self.words = [jnp.int32(0)] * -(-head_size // self.per_word)

    def rank_and_count(self, owner):
        if len(self.words) == 1:
            at = owner * self.width
            rank = self.words[0] >> at
            self.words[0] = self.words[0] + (jnp.int32(1) << at)
        else:
            word = owner // self.per_word
            at = (owner - word * self.per_word) * self.width
            held_word = self.words[0]
            for index in range(1, len(self.words)):
                held_word = jnp.where(word == index, self.words[index], held_word)
            rank = held_word >> at
            one = jnp.int32(1) << at
            self.words = [w + jnp.where(word == index, one, 0) for index, w in enumerate(self.words)]
        return rank & ((1 << self.width) - 1)

    def count(self, owner):
        word = self.words[owner // self.per_word]
        return (word >> (owner % self.per_word * self.width)) & ((1 << self.width) - 1)


def route_kernel(head_size, held, levels, plan, vertical, slash, send, slots, level, bits):
    own = lax.axis_index("head")
    most = [jnp.int32(0)] * head_size
    for target in range(head_size):
        tally = Tally(head_size, held)
        for t in range(held):
            head = plan[target * held + t]
            owner = head >> shift_of(held)
            rank = tally.rank_and_count(owner)
            send[jnp.where(owner == own, head & (held - 1), held)] = ((owner ^ target) << shift_of(held)) + rank
        for owner in range(head_size):
            most[owner ^ target] = jnp.maximum(most[owner ^ target], tally.count(owner))
    tally = Tally(head_size, held)
    for distance in range(head_size):
        slots[head_size * held + distance] = 0
    for t in range(held):
        owner = plan[own * held + t] >> shift_of(held)
        rank = tally.rank_and_count(owner)
        distance = owner ^ own
        slots[(distance << shift_of(held)) + rank] = t
        slots[head_size * held + distance] = rank + 1
    chosen = jnp.int32(len(levels) - 1)
    for index in reversed(range(len(levels) - 1)):
        fits = most[1] <= levels[index][1]
        for distance in range(2, head_size):
            fits = fits & (most[distance] <= levels[index][distance])
        chosen = jnp.where(fits, index, chosen)
    level[0] = chosen
    bits[0:1, :] = entry_bits(vertical)
    bits[1:2, :] = entry_bits(slash)


def attention_kernel(seq_size, held, kv_heads, send, bits, kv_own, kv_other, query_ref, out_ref):
    query_len = query_ref.shape[0]
    key_len = query_len
    own_seq = lax.axis_index("seq")
    own_head = lax.axis_index("head")
    chips = seq_size // 2
    half = chips * key_len

    piece = lax.broadcasted_iota(jnp.int32, (1, 2 * half), 1) // key_len
    core = jnp.where(piece < chips, own_seq & 1, 1 - (own_seq & 1))
    block = ((own_seq >> 1) ^ (piece & (chips - 1))) * 2 + core
    back = own_seq - block
    present = back >= 0
    back_shift = jnp.maximum(back, 0)
    row = lax.broadcasted_iota(jnp.int32, (query_len, LANES), 0)
    column = lax.broadcasted_iota(jnp.int32, (query_len, LANES), 1)
    causal = (column <= row) | (column >= key_len)
    score_scale = HD ** (-0.5) * math.log2(math.e)
    per_kv = held // kv_heads

    def scores_of(lead):
        heads = range(lead, min(lead + HEADS_AT_ONCE, held))
        key_at = lead // per_kv * HD
        key = jnp.concatenate([kv_own[:, key_at : key_at + HD], kv_other[:, key_at : key_at + HD]], axis=0)
        query = jnp.concatenate([query_ref[:, i * HD : (i + 1) * HD] for i in heads], axis=0)
        return lax.dot_general(
            query, key, (((1,), (1,)), ((), ())), preferred_element_type=jnp.float32
        )

    following = scores_of(0)
    for lead in range(0, held, HEADS_AT_ONCE):
        heads = range(lead, min(lead + HEADS_AT_ONCE, held))
        scores = following
        if lead + HEADS_AT_ONCE < held:
            following = scores_of(lead + HEADS_AT_ONCE)
        value_at = (lead // per_kv + kv_heads) * HD
        value = jnp.concatenate(
            [kv_own[:, value_at : value_at + HD], kv_other[:, value_at : value_at + HD]], axis=0
        )
        weights = []
        totals = []
        for at, i in enumerate(heads):
            head = own_head * held + i
            hit = ((bits[0, head] >> block) | (bits[1, head] >> back_shift)) & 1
            bias = jnp.where((hit == 1) & present, 0.0, floor_value)
            masked = scores[at * query_len : (at + 1) * query_len] + bias
            masked = jnp.concatenate(
                [jnp.where(causal, masked[:, :LANES], floor_value), masked[:, LANES:]], axis=1
            )
            row_max = jnp.max(masked, axis=1, keepdims=True)
            weight = jnp.exp2((masked - row_max) * score_scale)
            totals.append(1.0 / jnp.sum(weight, axis=1, keepdims=True))
            weights.append(weight.astype(jnp.bfloat16))
        mixture = jnp.dot(
            jnp.concatenate(weights, axis=0), value, preferred_element_type=jnp.float32
        )
        for at, i in enumerate(heads):
            mix = mixture[at * query_len : (at + 1) * query_len]
            out_ref[send[i]] = (mix * totals[at]).astype(out_ref.dtype)


def place_kernel(head_size, held, chunks, slots, *refs):
    out_ref, done = refs[-2:]
    for (distance, first, count), ref in zip(chunks, refs):
        arriving = slots[head_size * held + distance]
        for rank in range(first, first + count):

            @pl.when(rank < arriving)
            def _(ref=ref, rank=rank, first=first, distance=distance):
                at = pl.multiple_of(slots[distance * held + rank] * HD, HD)
                pltpu.make_async_copy(ref.at[rank - first], out_ref.at[:, pl.ds(at, HD)], done).start()

    pltpu.make_async_copy(out_ref, out_ref, done).wait()


def capacity_levels(head_size, held):
    near = max(1, held * 8 // 16)
    steps = sorted({max(1, held * c // 16) for c in (5, 6, 7, 8)})
    even_odd = sorted(((b, c) for b in steps for c in steps), key=sum)
    levels = [
        tuple(near if m < head_size // 2 else far[m % 2] for m in range(head_size)) for far in even_odd
    ]
    return levels + [(max(1, held * 10 // 16),) * head_size, (held,) * head_size]


def exchange(head_size, held, capacities, packed, slots):
    chunks = []
    for m in range(1, head_size):
        cut = capacities[m] // 2 if m < head_size // 2 else 0
        chunks += [(m, first, count) for first, count in ((0, cut), (cut, capacities[m] - cut)) if count]
    arrived = [
        lax.ppermute(
            packed[m * held + first : m * held + first + count],
            "head",
            [(i, i ^ m) for i in range(head_size)],
        )
        for m, first, count in chunks
    ]
    return pl.pallas_call(
        functools.partial(place_kernel, head_size, held, [(0, 0, held)] + chunks),
        out_shape=pltpu.HBM((packed.shape[1], held * HD), packed.dtype),
        in_specs=[SMEM] + [ANY] * (1 + len(chunks)),
        out_specs=pl.BlockSpec(memory_space=pltpu.HBM),
        scratch_shapes=[pltpu.SemaphoreType.DMA],
        compiler_params=pltpu.CompilerParams(vmem_limit_bytes=SMALL),
        name="place",
    )(slots, packed, *arrived)


def per_device(queries, keys, values, vertical, slash, plan):
    seq_size = lax.axis_size("seq")
    head_size = lax.axis_size("head")
    query_len = queries.shape[0]
    held = queries.shape[1] // HD
    kv_heads = max(1, held // GROUP)
    chips = seq_size // 2
    assert query_len == BLK and plan.shape[0] == held * head_size and chips & (chips - 1) == 0

    levels = capacity_levels(head_size, held)
    send, slots, level, bits = pl.pallas_call(
        functools.partial(route_kernel, head_size, held, levels),
        out_shape=[
            jax.ShapeDtypeStruct((held + 1,), jnp.int32),
            jax.ShapeDtypeStruct((head_size * held + head_size,), jnp.int32),
            jax.ShapeDtypeStruct((1,), jnp.int32),
            jax.ShapeDtypeStruct((2, vertical.shape[0]), jnp.int32),
        ],
        in_specs=[SMEM, VMEM, VMEM],
        out_specs=[SMEM] * 3 + [VMEM],
        compiler_params=pltpu.CompilerParams(vmem_limit_bytes=SMALL),
        name="route",
    )(plan, vertical.T, slash.T)

    kv_at = lax.axis_index("head") * held // GROUP * HD
    kv = jnp.concatenate(
        [lax.dynamic_slice_in_dim(rows, kv_at, kv_heads * HD, axis=1) for rows in (keys, values)], axis=1
    )
    pieces = [kv]
    for m in range(1, chips):
        pairs = [(i, i ^ (2 * m)) for i in range(seq_size)]
        pieces.append(lax.ppermute(kv, "seq", pairs))
    pieces, send, slots, level, bits = lax.optimization_barrier((pieces, send, slots, level, bits))
    kv_own = jnp.concatenate(pieces, axis=0)
    kv_other = lax.ppermute(kv_own, "seq", [(i, i ^ 1) for i in range(seq_size)])

    packed = pl.pallas_call(
        functools.partial(attention_kernel, seq_size, held, kv_heads),
        out_shape=jax.ShapeDtypeStruct((head_size * held, query_len, HD), jnp.bfloat16),
        in_specs=[SMEM] * 2 + [VMEM] * 3,
        out_specs=VMEM,
        compiler_params=pltpu.CompilerParams(vmem_limit_bytes=40 * 1024 * 1024),
        name="attention",
    )(send, bits, kv_own, kv_other, queries)

    return lax.switch(
        level[0],
        [functools.partial(exchange, head_size, held, capacities) for capacities in levels],
        packed,
        slots,
    )


def solution(mesh):
    in_specs = (P("seq", "head"), P("seq", None), P("seq", None), P(), P(), P())
    out_specs = P("seq", "head")
    return jax.shard_map(
        per_device, mesh=mesh, in_specs=in_specs, out_specs=out_specs, check_vma=False
    )
```

```python
import functools
import math

import jax
import jax.numpy as jnp
from jax import lax
from jax.experimental import pallas as pl
from jax.experimental.pallas import tpu as pltpu
from jax.sharding import PartitionSpec as P

HD = 128
QH = 64
KVH = 8
BLK = 64
GROUP = QH // KVH
HEADS_AT_ONCE = 4
LANES = 128

floor_value = -1e30

SMEM = pl.BlockSpec(memory_space=pltpu.SMEM)
VMEM = pl.BlockSpec(memory_space=pltpu.VMEM)
ANY = pl.BlockSpec(memory_space=pl.ANY)
SMALL = 1024 * 1024


def shift_of(size):
    assert size & (size - 1) == 0
    return size.bit_length() - 1


def entry_bits(table):
    bits = jnp.zeros((1, table.shape[1]), jnp.int32)
    for entry in range(table.shape[0]):
        named = table[entry : entry + 1, :]
        bits = bits | jnp.where(named >= 0, jnp.int32(1) << jnp.maximum(named, 0), 0)
    return bits


class Tally:
    def __init__(self, sources, most):
        self.width = shift_of(most) + 1
        self.per_word = 31 // self.width
        self.words = [jnp.int32(0)] * -(-sources // self.per_word)

    def rank_and_count(self, source):
        if len(self.words) == 1:
            at = source * self.width
            rank = self.words[0] >> at
            self.words[0] = self.words[0] + (jnp.int32(1) << at)
        else:
            word = source // self.per_word
            at = (source - word * self.per_word) * self.width
            held_word = self.words[0]
            for index in range(1, len(self.words)):
                held_word = jnp.where(word == index, self.words[index], held_word)
            rank = held_word >> at
            one = jnp.int32(1) << at
            self.words = [w + jnp.where(word == index, one, 0) for index, w in enumerate(self.words)]
        return rank & ((1 << self.width) - 1)


def route_kernel(half, held, plan, vertical, slash, send, slots, bits):
    own = lax.axis_index("head")
    lead = own & half
    for i in range(2 * held):
        send[i] = half * held
    for distance in range(half):
        slots[half * held + distance] = 0
    for target in range(half):
        tally = Tally(half, held)
        for t in range(held):
            head = plan[(lead + target) * held + t]
            owner = head >> shift_of(held)
            source = owner & (half - 1)
            rank = tally.rank_and_count(source)
            place = ((source ^ target) << shift_of(held)) + rank
            candidate = (head & (held - 1)) + jnp.where(owner == own, 0, held)
            send[jnp.where(source == own - lead, candidate, 2 * held)] = place
    tally = Tally(half, held)
    for t in range(held):
        source = (plan[own * held + t] >> shift_of(held)) & (half - 1)
        rank = tally.rank_and_count(source)
        distance = source ^ (own - lead)
        slots[(distance << shift_of(held)) + rank] = t
        slots[half * held + distance] = rank + 1
    bits[0:1, :] = entry_bits(vertical)
    bits[1:2, :] = entry_bits(slash)


def attention_kernel(seq_size, half, held, kv_heads, send, bits, kv_own, kv_other, near, far, out_ref):
    query_len = near.shape[0]
    key_len = query_len
    own_seq = lax.axis_index("seq")
    own_head = lax.axis_index("head")
    chips = seq_size // 2
    chip_rows = chips * key_len

    piece = lax.broadcasted_iota(jnp.int32, (1, 2 * chip_rows), 1) // key_len
    core = jnp.where(piece < chips, own_seq & 1, 1 - (own_seq & 1))
    block = ((own_seq >> 1) ^ (piece & (chips - 1))) * 2 + core
    back = own_seq - block
    present = back >= 0
    back_shift = jnp.maximum(back, 0)
    row = lax.broadcasted_iota(jnp.int32, (query_len, LANES), 0)
    column = lax.broadcasted_iota(jnp.int32, (query_len, LANES), 1)
    causal = (column <= row) | (column >= key_len)
    score_scale = HD ** (-0.5) * math.log2(math.e)
    per_kv = held // kv_heads

    def rows_of(at):
        return jnp.concatenate([kv_own[:, at : at + HD], kv_other[:, at : at + HD]], axis=0)

    def scores_of(candidates):
        key = rows_of(candidates[0] // per_kv * HD)
        query = jnp.concatenate(
            [(near if i < held else far)[:, i % held * HD : (i % held + 1) * HD] for i in candidates], axis=0
        )
        return lax.dot_general(
            query, key, (((1,), (1,)), ((), ())), preferred_element_type=jnp.float32
        )

    together = min(HEADS_AT_ONCE, per_kv)
    groups = [range(lead, lead + together) for lead in range(0, 2 * held, together)]
    following = scores_of(groups[0])
    for index, candidates in enumerate(groups):
        scores = following
        if index + 1 < len(groups):
            following = scores_of(groups[index + 1])
        value = rows_of((candidates[0] // per_kv + 2 * kv_heads) * HD)
        weights = []
        totals = []
        for at, i in enumerate(candidates):
            head = (own_head if i < held else own_head ^ half) * held + i % held
            hit = ((bits[0, head] >> block) | (bits[1, head] >> back_shift)) & 1
            bias = jnp.where((hit == 1) & present, 0.0, floor_value)
            masked = scores[at * query_len : (at + 1) * query_len] + bias
            masked = jnp.concatenate(
                [jnp.where(causal, masked[:, :LANES], floor_value), masked[:, LANES:]], axis=1
            )
            row_max = jnp.max(masked, axis=1, keepdims=True)
            weight = jnp.exp2((masked - row_max) * score_scale)
            totals.append(1.0 / jnp.sum(weight, axis=1, keepdims=True))
            weights.append(weight.astype(jnp.bfloat16))
        mixture = jnp.dot(
            jnp.concatenate(weights, axis=0), value, preferred_element_type=jnp.float32
        )
        for at, i in enumerate(candidates):
            mix = mixture[at * query_len : (at + 1) * query_len]
            out_ref[send[i]] = (mix * totals[at]).astype(out_ref.dtype)


def place_kernel(half, held, slots, *refs):
    out_ref, done = refs[-2:]
    for distance, ref in enumerate(refs[:-2]):
        arriving = slots[half * held + distance]
        for rank in range(held):

            @pl.when(rank < arriving)
            def _(ref=ref, rank=rank, distance=distance):
                at = pl.multiple_of(slots[distance * held + rank] * HD, HD)
                pltpu.make_async_copy(ref.at[rank], out_ref.at[:, pl.ds(at, HD)], done).start()

    pltpu.make_async_copy(out_ref, out_ref, done).wait()


def per_device(queries, keys, values, vertical, slash, plan):
    seq_size = lax.axis_size("seq")
    head_size = lax.axis_size("head")
    half = head_size // 2
    query_len = queries.shape[0]
    held = queries.shape[1] // HD
    kv_heads = max(1, held // GROUP)
    chips = seq_size // 2
    assert query_len == BLK and plan.shape[0] == held * head_size and chips & (chips - 1) == 0

    far_queries = lax.ppermute(queries, "head", [(i, i ^ half) for i in range(head_size)])

    send, slots, bits = pl.pallas_call(
        functools.partial(route_kernel, half, held),
        out_shape=[
            jax.ShapeDtypeStruct((2 * held + 1,), jnp.int32),
            jax.ShapeDtypeStruct((half * held + half,), jnp.int32),
            jax.ShapeDtypeStruct((2, vertical.shape[0]), jnp.int32),
        ],
        in_specs=[SMEM, VMEM, VMEM],
        out_specs=[SMEM] * 2 + [VMEM],
        compiler_params=pltpu.CompilerParams(vmem_limit_bytes=SMALL),
        name="route",
    )(plan, vertical.T, slash.T)

    own_head = lax.axis_index("head")
    kv = jnp.concatenate(
        [
            lax.dynamic_slice_in_dim(rows, holder * held // GROUP * HD, kv_heads * HD, axis=1)
            for rows in (keys, values)
            for holder in (own_head, own_head ^ half)
        ],
        axis=1,
    )
    pieces = [kv]
    for m in range(1, chips):
        pieces.append(lax.ppermute(kv, "seq", [(i, i ^ (2 * m)) for i in range(seq_size)]))
    pieces, far_queries, send, slots, bits = lax.optimization_barrier(
        (pieces, far_queries, send, slots, bits)
    )
    kv_own = jnp.concatenate(pieces, axis=0)
    kv_other = lax.ppermute(kv_own, "seq", [(i, i ^ 1) for i in range(seq_size)])

    packed = pl.pallas_call(
        functools.partial(attention_kernel, seq_size, half, held, kv_heads),
        out_shape=jax.ShapeDtypeStruct((half * held + 1, query_len, HD), jnp.bfloat16),
        in_specs=[SMEM] * 2 + [VMEM] * 4,
        out_specs=VMEM,
        compiler_params=pltpu.CompilerParams(vmem_limit_bytes=40 * 1024 * 1024),
        name="attention",
    )(send, bits, kv_own, kv_other, queries, far_queries)

    arrived = [
        lax.ppermute(packed[m * held : (m + 1) * held], "head", [(i, i ^ m) for i in range(head_size)])
        for m in range(1, half)
    ]
    return pl.pallas_call(
        functools.partial(place_kernel, half, held),
        out_shape=pltpu.HBM((query_len, held * HD), packed.dtype),
        in_specs=[SMEM] + [ANY] * half,
        out_specs=pl.BlockSpec(memory_space=pltpu.HBM),
        scratch_shapes=[pltpu.SemaphoreType.DMA],
        compiler_params=pltpu.CompilerParams(vmem_limit_bytes=SMALL),
        name="place",
    )(slots, packed, *arrived)


def solution(mesh):
    in_specs = (P("seq", "head"), P("seq", None), P("seq", None), P(), P(), P())
    out_specs = P("seq", "head")
    return jax.shard_map(
        per_device, mesh=mesh, in_specs=in_specs, out_specs=out_specs, check_vma=False
    )
```

```python
import functools
import math

import jax
import jax.numpy as jnp
from jax import lax
from jax.experimental import pallas as pl
from jax.experimental.pallas import tpu as pltpu
from jax.sharding import PartitionSpec as P

HD = 128
QH = 64
KVH = 8
BLK = 64
GROUP = QH // KVH
HEADS_AT_ONCE = 4
LANES = 128
EXCHANGE_PIECES = 4

floor_value = -1e30

SMEM = pl.BlockSpec(memory_space=pltpu.SMEM)
VMEM = pl.BlockSpec(memory_space=pltpu.VMEM)
ANY = pl.BlockSpec(memory_space=pl.ANY)
SMALL = 1024 * 1024


def shift_of(size):
    assert size & (size - 1) == 0
    return size.bit_length() - 1


def entry_bits(table):
    bits = jnp.zeros((1, table.shape[1]), jnp.int32)
    for entry in range(table.shape[0]):
        named = table[entry : entry + 1, :]
        bits = bits | jnp.where(named >= 0, jnp.int32(1) << jnp.maximum(named, 0), 0)
    return bits


class Tally:
    def __init__(self, sources, most):
        self.width = shift_of(most) + 1
        self.per_word = 31 // self.width
        self.words = [jnp.int32(0)] * -(-sources // self.per_word)

    def rank_and_count(self, source):
        if len(self.words) == 1:
            at = source * self.width
            rank = self.words[0] >> at
            self.words[0] = self.words[0] + (jnp.int32(1) << at)
        else:
            word = source // self.per_word
            at = (source - word * self.per_word) * self.width
            held_word = self.words[0]
            for index in range(1, len(self.words)):
                held_word = jnp.where(word == index, self.words[index], held_word)
            rank = held_word >> at
            one = jnp.int32(1) << at
            self.words = [w + jnp.where(word == index, one, 0) for index, w in enumerate(self.words)]
        return rank & ((1 << self.width) - 1)


def route_kernel(half, held, plan, vertical, slash, send, slots, bits):
    own = lax.axis_index("head")
    lead = own & half
    for i in range(2 * held):
        send[i] = half * held
    for distance in range(half):
        slots[half * held + distance] = 0
    for target in range(half):
        tally = Tally(half, held)
        for t in range(held):
            head = plan[(lead + target) * held + t]
            owner = head >> shift_of(held)
            source = owner & (half - 1)
            rank = tally.rank_and_count(source)
            place = ((source ^ target) << shift_of(held)) + rank
            candidate = (head & (held - 1)) + jnp.where(owner == own, 0, held)
            send[jnp.where(source == own - lead, candidate, 2 * held)] = place
    tally = Tally(half, held)
    for t in range(held):
        source = (plan[own * held + t] >> shift_of(held)) & (half - 1)
        rank = tally.rank_and_count(source)
        distance = source ^ (own - lead)
        slots[(distance << shift_of(held)) + rank] = t
        slots[half * held + distance] = rank + 1
    bits[0:1, :] = entry_bits(vertical)
    bits[1:2, :] = entry_bits(slash)


def attention_kernel(seq_size, half, held, kv_heads, send, bits, kv_own, kv_other, *refs):
    query_refs, out_ref = refs[:-1], refs[-1]
    query_len = query_refs[0].shape[0]
    key_len = query_len
    own_seq = lax.axis_index("seq")
    own_head = lax.axis_index("head")
    chips = seq_size // 2
    chip_rows = chips * key_len

    piece = lax.broadcasted_iota(jnp.int32, (1, 2 * chip_rows), 1) // key_len
    core = jnp.where(piece < chips, own_seq & 1, 1 - (own_seq & 1))
    block = ((own_seq >> 1) ^ (piece & (chips - 1))) * 2 + core
    back = own_seq - block
    present = back >= 0
    back_shift = jnp.maximum(back, 0)
    row = lax.broadcasted_iota(jnp.int32, (query_len, LANES), 0)
    column = lax.broadcasted_iota(jnp.int32, (query_len, LANES), 1)
    causal = (column <= row) | (column >= key_len)
    score_scale = HD ** (-0.5) * math.log2(math.e)
    per_kv = held // kv_heads

    query_at = [(ref, at) for ref in query_refs for at in range(0, ref.shape[1], HD)]

    def rows_of(at):
        return jnp.concatenate([kv_own[:, at : at + HD], kv_other[:, at : at + HD]], axis=0)

    def scores_of(candidates):
        key = rows_of(candidates[0] // per_kv * HD)
        query = jnp.concatenate([ref[:, at : at + HD] for ref, at in (query_at[i] for i in candidates)], axis=0)
        return lax.dot_general(
            query, key, (((1,), (1,)), ((), ())), preferred_element_type=jnp.float32
        )

    together = min(HEADS_AT_ONCE, per_kv)
    groups = [range(lead, lead + together) for lead in range(0, 2 * held, together)]
    following = scores_of(groups[0])
    for index, candidates in enumerate(groups):
        scores = following
        if index + 1 < len(groups):
            following = scores_of(groups[index + 1])
        value = rows_of((candidates[0] // per_kv + 2 * kv_heads) * HD)
        weights = []
        totals = []
        for at, i in enumerate(candidates):
            head = (own_head if i < held else own_head ^ half) * held + i % held
            hit = ((bits[0, head] >> block) | (bits[1, head] >> back_shift)) & 1
            bias = jnp.where((hit == 1) & present, 0.0, floor_value)
            masked = scores[at * query_len : (at + 1) * query_len] + bias
            masked = jnp.concatenate(
                [jnp.where(causal, masked[:, :LANES], floor_value), masked[:, LANES:]], axis=1
            )
            row_max = jnp.max(masked, axis=1, keepdims=True)
            weight = jnp.exp2((masked - row_max) * score_scale)
            totals.append(1.0 / jnp.sum(weight, axis=1, keepdims=True))
            weights.append(weight.astype(jnp.bfloat16))
        mixture = jnp.dot(
            jnp.concatenate(weights, axis=0), value, preferred_element_type=jnp.float32
        )
        for at, i in enumerate(candidates):
            mix = mixture[at * query_len : (at + 1) * query_len]
            out_ref[send[i]] = (mix * totals[at]).astype(out_ref.dtype)


def place_kernel(half, held, chunks, slots, *refs):
    out_ref, done = refs[-2:]
    for (distance, first, count), ref in zip(chunks, refs):
        arriving = slots[half * held + distance]
        for rank in range(first, first + count):

            @pl.when(rank < arriving)
            def _(ref=ref, rank=rank, first=first, distance=distance):
                at = pl.multiple_of(slots[distance * held + rank] * HD, HD)
                pltpu.make_async_copy(ref.at[rank - first], out_ref.at[:, pl.ds(at, HD)], done).start()

    pltpu.make_async_copy(out_ref, out_ref, done).wait()


def per_device(queries, keys, values, vertical, slash, plan):
    seq_size = lax.axis_size("seq")
    head_size = lax.axis_size("head")
    half = head_size // 2
    query_len = queries.shape[0]
    held = queries.shape[1] // HD
    kv_heads = max(1, held // GROUP)
    chips = seq_size // 2
    assert query_len == BLK and plan.shape[0] == held * head_size and chips & (chips - 1) == 0

    send, slots, bits = pl.pallas_call(
        functools.partial(route_kernel, half, held),
        out_shape=[
            jax.ShapeDtypeStruct((2 * held + 1,), jnp.int32),
            jax.ShapeDtypeStruct((half * held + half,), jnp.int32),
            jax.ShapeDtypeStruct((2, vertical.shape[0]), jnp.int32),
        ],
        in_specs=[SMEM, VMEM, VMEM],
        out_specs=[SMEM] * 2 + [VMEM],
        compiler_params=pltpu.CompilerParams(vmem_limit_bytes=SMALL),
        name="route",
    )(plan, vertical.T, slash.T)

    own_head = lax.axis_index("head")
    kv = jnp.concatenate(
        [
            lax.dynamic_slice_in_dim(rows, holder * held // GROUP * HD, kv_heads * HD, axis=1)
            for rows in (keys, values)
            for holder in (own_head, own_head ^ half)
        ],
        axis=1,
    )
    pieces = [kv]
    for m in range(1, chips):
        pieces.append(lax.ppermute(kv, "seq", [(i, i ^ (2 * m)) for i in range(seq_size)]))
    swap = [(i, i ^ half) for i in range(head_size)]
    cut = held * 10 // 16
    far_queries = [
        lax.ppermute(queries[:, first * HD : last * HD], "head", swap) for first, last in ((0, cut), (cut, held))
    ]
    pieces, far_queries, send, slots, bits = lax.optimization_barrier(
        (pieces, far_queries, send, slots, bits)
    )
    kv_own = jnp.concatenate(pieces, axis=0)
    kv_other = lax.ppermute(kv_own, "seq", [(i, i ^ 1) for i in range(seq_size)])

    packed = pl.pallas_call(
        functools.partial(attention_kernel, seq_size, half, held, kv_heads),
        out_shape=jax.ShapeDtypeStruct((half * held + 1, query_len, HD), jnp.bfloat16),
        in_specs=[SMEM] * 2 + [VMEM] * (3 + len(far_queries)),
        out_specs=VMEM,
        compiler_params=pltpu.CompilerParams(vmem_limit_bytes=40 * 1024 * 1024),
        name="attention",
    )(send, bits, kv_own, kv_other, queries, *far_queries)

    count = max(1, held // EXCHANGE_PIECES)
    chunks = [(m, first, count) for m in range(1, half) for first in range(0, held, count)]
    arrived = [
        lax.ppermute(
            packed[m * held + first : m * held + first + count], "head", [(i, i ^ m) for i in range(head_size)]
        )
        for m, first, count in chunks
    ]
    return pl.pallas_call(
        functools.partial(place_kernel, half, held, [(0, 0, held)] + chunks),
        out_shape=pltpu.HBM((query_len, held * HD), packed.dtype),
        in_specs=[SMEM] + [ANY] * (1 + len(arrived)),
        out_specs=pl.BlockSpec(memory_space=pltpu.HBM),
        scratch_shapes=[pltpu.SemaphoreType.DMA],
        compiler_params=pltpu.CompilerParams(vmem_limit_bytes=SMALL),
        name="place",
    )(slots, packed, *arrived)


def solution(mesh):
    in_specs = (P("seq", "head"), P("seq", None), P("seq", None), P(), P(), P())
    out_specs = P("seq", "head")
    return jax.shard_map(
        per_device, mesh=mesh, in_specs=in_specs, out_specs=out_specs, check_vma=False
    )
```

```python
import functools
import math

import jax
import jax.numpy as jnp
from jax import lax
from jax.experimental import pallas as pl
from jax.experimental.pallas import tpu as pltpu
from jax.sharding import PartitionSpec as P

HD = 128
QH = 64
KVH = 8
BLK = 64
GROUP = QH // KVH
HEADS_AT_ONCE = 4
LANES = 128

floor_value = -1e30

SMEM = pl.BlockSpec(memory_space=pltpu.SMEM)
VMEM = pl.BlockSpec(memory_space=pltpu.VMEM)
ANY = pl.BlockSpec(memory_space=pl.ANY)
SMALL = 1024 * 1024


def shift_of(size):
    assert size & (size - 1) == 0
    return size.bit_length() - 1


def entry_bits(table):
    bits = jnp.zeros((1, table.shape[1]), jnp.int32)
    for entry in range(table.shape[0]):
        named = table[entry : entry + 1, :]
        bits = bits | jnp.where(named >= 0, jnp.int32(1) << jnp.maximum(named, 0), 0)
    return bits


class Tally:
    def __init__(self, head_size, held):
        self.width = shift_of(held) + 1
        self.per_word = 31 // self.width
        self.words = [jnp.int32(0)] * -(-head_size // self.per_word)

    def rank_and_count(self, owner):
        if len(self.words) == 1:
            at = owner * self.width
            rank = self.words[0] >> at
            self.words[0] = self.words[0] + (jnp.int32(1) << at)
        else:
            word = owner // self.per_word
            at = (owner - word * self.per_word) * self.width
            held_word = self.words[0]
            for index in range(1, len(self.words)):
                held_word = jnp.where(word == index, self.words[index], held_word)
            rank = held_word >> at
            one = jnp.int32(1) << at
            self.words = [w + jnp.where(word == index, one, 0) for index, w in enumerate(self.words)]
        return rank & ((1 << self.width) - 1)

    def count(self, owner):
        word = self.words[owner // self.per_word]
        return (word >> (owner % self.per_word * self.width)) & ((1 << self.width) - 1)


def route_kernel(head_size, held, levels, plan, vertical, slash, send, slots, level, bits):
    own = lax.axis_index("head")
    most = [jnp.int32(0)] * head_size
    for target in range(head_size):
        tally = Tally(head_size, held)
        for t in range(held):
            head = plan[target * held + t]
            owner = head >> shift_of(held)
            rank = tally.rank_and_count(owner)
            send[jnp.where(owner == own, head & (held - 1), held)] = ((owner ^ target) << shift_of(held)) + rank
        for owner in range(head_size):
            most[owner ^ target] = jnp.maximum(most[owner ^ target], tally.count(owner))
    tally = Tally(head_size, held)
    for distance in range(head_size):
        slots[head_size * held + distance] = 0
    for t in range(held):
        owner = plan[own * held + t] >> shift_of(held)
        rank = tally.rank_and_count(owner)
        distance = owner ^ own
        slots[(distance << shift_of(held)) + rank] = t
        slots[head_size * held + distance] = rank + 1
    chosen = jnp.int32(len(levels) - 1)
    for index in reversed(range(len(levels) - 1)):
        fits = most[1] <= levels[index][1]
        for distance in range(2, head_size):
            fits = fits & (most[distance] <= levels[index][distance])
        chosen = jnp.where(fits, index, chosen)
    level[0] = chosen
    bits[0:1, :] = entry_bits(vertical)
    bits[1:2, :] = entry_bits(slash)


def attention_kernel(
    seq_size, held, kv_heads, send, bits, kv_own, kv_other, query_ref, out_ref, send_here, copied
):
    send_copy = pltpu.make_async_copy(send, send_here, copied)
    send_copy.start()
    query_len = query_ref.shape[0]
    key_len = query_len
    own_seq = lax.axis_index("seq")
    own_head = lax.axis_index("head")
    chips = seq_size // 2
    half = chips * key_len

    piece = lax.broadcasted_iota(jnp.int32, (1, 2 * half), 1) // key_len
    core = jnp.where(piece < chips, own_seq & 1, 1 - (own_seq & 1))
    block = ((own_seq >> 1) ^ (piece & (chips - 1))) * 2 + core
    back = own_seq - block
    present = back >= 0
    back_shift = jnp.maximum(back, 0)
    heads = own_head * held + lax.broadcasted_iota(jnp.int32, (held, bits.shape[1]), 0)
    is_head = lax.broadcasted_iota(jnp.int32, (held, bits.shape[1]), 1) == heads
    vertical_bits, slash_bits = (
        jnp.sum(jnp.where(is_head, bits[kind : kind + 1, :], 0), axis=1, keepdims=True) for kind in range(2)
    )
    hit = ((vertical_bits >> block) | (slash_bits >> back_shift)) & 1
    bias = jnp.where((hit == 1) & present, 0.0, floor_value)
    row = lax.broadcasted_iota(jnp.int32, (query_len, LANES), 0)
    column = lax.broadcasted_iota(jnp.int32, (query_len, LANES), 1)
    causal = (column <= row) | (column >= key_len)
    score_scale = HD ** (-0.5) * math.log2(math.e)
    per_kv = held // kv_heads

    def scores_of(lead):
        heads = range(lead, min(lead + HEADS_AT_ONCE, held))
        key_at = lead // per_kv * HD
        key = jnp.concatenate([kv_own[:, key_at : key_at + HD], kv_other[:, key_at : key_at + HD]], axis=0)
        query = jnp.concatenate([query_ref[:, i * HD : (i + 1) * HD] for i in heads], axis=0)
        return lax.dot_general(
            query, key, (((1,), (1,)), ((), ())), preferred_element_type=jnp.float32
        )

    following = scores_of(0)
    for lead in range(0, held, HEADS_AT_ONCE):
        heads = range(lead, min(lead + HEADS_AT_ONCE, held))
        scores = following
        if lead + HEADS_AT_ONCE < held:
            following = scores_of(lead + HEADS_AT_ONCE)
        value_at = (lead // per_kv + kv_heads) * HD
        value = jnp.concatenate(
            [kv_own[:, value_at : value_at + HD], kv_other[:, value_at : value_at + HD]], axis=0
        )
        weights = []
        totals = []
        for at, i in enumerate(heads):
            masked = scores[at * query_len : (at + 1) * query_len] + bias[i : i + 1, :]
            masked = jnp.concatenate(
                [jnp.where(causal, masked[:, :LANES], floor_value), masked[:, LANES:]], axis=1
            )
            row_max = jnp.max(masked, axis=1, keepdims=True)
            weight = jnp.exp2((masked - row_max) * score_scale)
            totals.append(1.0 / jnp.sum(weight, axis=1, keepdims=True))
            weights.append(weight.astype(jnp.bfloat16))
        mixture = jnp.dot(
            jnp.concatenate(weights, axis=0), value, preferred_element_type=jnp.float32
        )
        if lead == 0:
            send_copy.wait()
        for at, i in enumerate(heads):
            mix = mixture[at * query_len : (at + 1) * query_len]
            out_ref[send_here[i]] = (mix * totals[at]).astype(out_ref.dtype)


def place_kernel(head_size, held, sources, slots, *refs):
    out_ref, done = refs[-2:]
    for (distance, capacity), ref in zip(sources, refs):
        arriving = slots[head_size * held + distance]
        for rank in range(capacity):

            @pl.when(rank < arriving)
            def _(ref=ref, rank=rank, distance=distance):
                at = pl.multiple_of(slots[distance * held + rank] * HD, HD)
                pltpu.make_async_copy(ref.at[rank], out_ref.at[:, pl.ds(at, HD)], done).start()

    pltpu.make_async_copy(out_ref, out_ref, done).wait()


def capacity_levels(head_size, held):
    near = max(1, held * 9 // 16)
    steps = sorted({max(1, held * c // 16) for c in (4, 5, 6, 7, 8)})
    even_odd = sorted(((b, c) for b in steps for c in steps), key=sum)
    levels = [
        tuple(near if m < head_size // 2 else far[m % 2] for m in range(head_size)) for far in even_odd
    ]
    return levels + [(max(1, held * 10 // 16),) * head_size, (held,) * head_size]


def exchange(head_size, held, capacities, packed, slots):
    order = sorted(range(1, head_size), key=lambda m: (m >= head_size // 2, -m))
    arrived = [
        lax.ppermute(
            packed[m * held : m * held + capacities[m]], "head", [(i, i ^ m) for i in range(head_size)]
        )
        for m in order
    ]
    return pl.pallas_call(
        functools.partial(place_kernel, head_size, held, [(0, held)] + [(m, capacities[m]) for m in order]),
        out_shape=pltpu.HBM((packed.shape[1], held * HD), packed.dtype),
        in_specs=[SMEM] + [ANY] * head_size,
        out_specs=pl.BlockSpec(memory_space=pltpu.HBM),
        scratch_shapes=[pltpu.SemaphoreType.DMA],
        compiler_params=pltpu.CompilerParams(vmem_limit_bytes=SMALL),
        name="place",
    )(slots, packed, *arrived)


def per_device(queries, keys, values, vertical, slash, plan):
    seq_size = lax.axis_size("seq")
    head_size = lax.axis_size("head")
    query_len = queries.shape[0]
    held = queries.shape[1] // HD
    kv_heads = max(1, held // GROUP)
    chips = seq_size // 2
    assert query_len == BLK and plan.shape[0] == held * head_size and chips & (chips - 1) == 0

    levels = capacity_levels(head_size, held)
    send, slots, level, bits = pl.pallas_call(
        functools.partial(route_kernel, head_size, held, levels),
        out_shape=[
            jax.ShapeDtypeStruct((held + 1,), jnp.int32),
            jax.ShapeDtypeStruct((head_size * held + head_size,), jnp.int32),
            jax.ShapeDtypeStruct((1,), jnp.int32),
            jax.ShapeDtypeStruct((2, vertical.shape[0]), jnp.int32),
        ],
        in_specs=[SMEM, VMEM, VMEM],
        out_specs=[SMEM] * 3 + [VMEM],
        compiler_params=pltpu.CompilerParams(vmem_limit_bytes=SMALL),
        name="route",
    )(plan, vertical.T, slash.T)

    kv_at = lax.axis_index("head") * held // GROUP * HD
    kv = jnp.concatenate(
        [lax.dynamic_slice_in_dim(rows, kv_at, kv_heads * HD, axis=1) for rows in (keys, values)], axis=1
    )
    pieces = [kv]
    for m in range(1, chips):
        pairs = [(i, i ^ (2 * m)) for i in range(seq_size)]
        pieces.append(lax.ppermute(kv, "seq", pairs))
    pieces, send, slots, level, bits = lax.optimization_barrier((pieces, send, slots, level, bits))
    kv_own = jnp.concatenate(pieces, axis=0)
    kv_other = lax.ppermute(kv_own, "seq", [(i, i ^ 1) for i in range(seq_size)])

    packed = pl.pallas_call(
        functools.partial(attention_kernel, seq_size, held, kv_heads),
        out_shape=jax.ShapeDtypeStruct((head_size * held, query_len, HD), jnp.bfloat16),
        in_specs=[ANY] + [VMEM] * 4,
        out_specs=VMEM,
        scratch_shapes=[pltpu.SMEM(send.shape, send.dtype), pltpu.SemaphoreType.DMA],
        compiler_params=pltpu.CompilerParams(vmem_limit_bytes=40 * 1024 * 1024),
        name="attention",
    )(send, bits, kv_own, kv_other, queries)

    return lax.switch(
        level[0],
        [functools.partial(exchange, head_size, held, capacities) for capacities in levels],
        packed,
        slots,
    )


def solution(mesh):
    in_specs = (P("seq", "head"), P("seq", None), P("seq", None), P(), P(), P())
    out_specs = P("seq", "head")
    return jax.shard_map(
        per_device, mesh=mesh, in_specs=in_specs, out_specs=out_specs, check_vma=False
    )
```

```python
import functools
import math

import jax
import jax.numpy as jnp
from jax import lax
from jax.experimental import pallas as pl
from jax.experimental.pallas import tpu as pltpu
from jax.sharding import PartitionSpec as P

HD = 128
QH = 64
KVH = 8
BLK = 64
GROUP = QH // KVH
HEADS_AT_ONCE = 4
LANES = 128

floor_value = -1e30

SMEM = pl.BlockSpec(memory_space=pltpu.SMEM)
VMEM = pl.BlockSpec(memory_space=pltpu.VMEM)
ANY = pl.BlockSpec(memory_space=pl.ANY)
SMALL = 1024 * 1024


def shift_of(size):
    assert size & (size - 1) == 0
    return size.bit_length() - 1


def turned(index, size):
    return ((index << 1) | (index >> (shift_of(size) - 1))) & (size - 1)


def entry_bits(table):
    bits = jnp.zeros((1, table.shape[1]), jnp.int32)
    for entry in range(table.shape[0]):
        named = table[entry : entry + 1, :]
        bits = bits | jnp.where(named >= 0, jnp.int32(1) << jnp.maximum(named, 0), 0)
    return bits


class Tally:
    def __init__(self, head_size, held):
        self.width = shift_of(held) + 1
        self.per_word = 31 // self.width
        self.words = [jnp.int32(0)] * -(-head_size // self.per_word)

    def rank_and_count(self, owner):
        if len(self.words) == 1:
            at = owner * self.width
            rank = self.words[0] >> at
            self.words[0] = self.words[0] + (jnp.int32(1) << at)
        else:
            word = owner // self.per_word
            at = (owner - word * self.per_word) * self.width
            held_word = self.words[0]
            for index in range(1, len(self.words)):
                held_word = jnp.where(word == index, self.words[index], held_word)
            rank = held_word >> at
            one = jnp.int32(1) << at
            self.words = [w + jnp.where(word == index, one, 0) for index, w in enumerate(self.words)]
        return rank & ((1 << self.width) - 1)

    def count(self, owner):
        word = self.words[owner // self.per_word]
        return (word >> (owner % self.per_word * self.width)) & ((1 << self.width) - 1)


def route_kernel(head_size, held, levels, plan, vertical, slash, send, slots, level, bits):
    own = lax.axis_index("head")
    most = [jnp.int32(0)] * head_size
    for target in range(head_size):
        tally = Tally(head_size, held)
        for t in range(held):
            head = plan[target * held + t]
            owner = head >> shift_of(held)
            rank = tally.rank_and_count(owner)
            send[jnp.where(owner == own, head & (held - 1), held)] = ((owner ^ target) << shift_of(held)) + rank
        for owner in range(head_size):
            most[owner ^ target] = jnp.maximum(most[owner ^ target], tally.count(owner))
    tally = Tally(head_size, held)
    for distance in range(head_size):
        slots[head_size * held + distance] = 0
    for t in range(held):
        owner = plan[own * held + t] >> shift_of(held)
        rank = tally.rank_and_count(owner)
        distance = owner ^ own
        slots[(distance << shift_of(held)) + rank] = t
        slots[head_size * held + distance] = rank + 1
    chosen = jnp.int32(len(levels) - 1)
    for index in reversed(range(len(levels) - 1)):
        fits = most[1] <= levels[index][1]
        for distance in range(2, head_size):
            fits = fits & (most[distance] <= levels[index][distance])
        chosen = jnp.where(fits, index, chosen)
    level[0] = chosen
    bits[0:1, :] = entry_bits(vertical)
    bits[1:2, :] = entry_bits(slash)


def attention_kernel(
    seq_size, held, kv_heads, send, bits, kv_own, kv_other, query_ref, out_ref, send_here, copied
):
    send_copy = pltpu.make_async_copy(send, send_here, copied)
    send_copy.start()
    query_len = query_ref.shape[0]
    key_len = query_len
    own_seq = lax.axis_index("seq")
    own_head = lax.axis_index("head")
    chips = seq_size // 2
    half = chips * key_len

    piece = lax.broadcasted_iota(jnp.int32, (1, 2 * half), 1) // key_len
    core = jnp.where(piece < chips, own_seq & 1, 1 - (own_seq & 1))
    flip = piece & (chips - 1)
    flip = jnp.where(core == 0, flip, turned(flip, chips))
    block = ((own_seq >> 1) ^ flip) * 2 + core
    back = own_seq - block
    present = back >= 0
    back_shift = jnp.maximum(back, 0)
    heads = own_head * held + lax.broadcasted_iota(jnp.int32, (held, bits.shape[1]), 0)
    is_head = lax.broadcasted_iota(jnp.int32, (held, bits.shape[1]), 1) == heads
    vertical_bits, slash_bits = (
        jnp.sum(jnp.where(is_head, bits[kind : kind + 1, :], 0), axis=1, keepdims=True) for kind in range(2)
    )
    hit = ((vertical_bits >> block) | (slash_bits >> back_shift)) & 1
    bias = jnp.where((hit == 1) & present, 0.0, floor_value)
    row = lax.broadcasted_iota(jnp.int32, (query_len, LANES), 0)
    column = lax.broadcasted_iota(jnp.int32, (query_len, LANES), 1)
    causal = (column <= row) | (column >= key_len)
    score_scale = HD ** (-0.5) * math.log2(math.e)
    per_kv = held // kv_heads

    def scores_of(lead):
        heads = range(lead, min(lead + HEADS_AT_ONCE, held))
        key_at = lead // per_kv * HD
        key = jnp.concatenate([kv_own[:, key_at : key_at + HD], kv_other[:, key_at : key_at + HD]], axis=0)
        query = jnp.concatenate([query_ref[:, i * HD : (i + 1) * HD] for i in heads], axis=0)
        return lax.dot_general(
            query, key, (((1,), (1,)), ((), ())), preferred_element_type=jnp.float32
        )

    following = scores_of(0)
    for lead in range(0, held, HEADS_AT_ONCE):
        heads = range(lead, min(lead + HEADS_AT_ONCE, held))
        scores = following
        if lead + HEADS_AT_ONCE < held:
            following = scores_of(lead + HEADS_AT_ONCE)
        value_at = (lead // per_kv + kv_heads) * HD
        value = jnp.concatenate(
            [kv_own[:, value_at : value_at + HD], kv_other[:, value_at : value_at + HD]], axis=0
        )
        weights = []
        totals = []
        for at, i in enumerate(heads):
            masked = scores[at * query_len : (at + 1) * query_len] + bias[i : i + 1, :]
            masked = jnp.concatenate(
                [jnp.where(causal, masked[:, :LANES], floor_value), masked[:, LANES:]], axis=1
            )
            row_max = jnp.max(masked, axis=1, keepdims=True)
            weight = jnp.exp2((masked - row_max) * score_scale)
            totals.append(1.0 / jnp.sum(weight, axis=1, keepdims=True))
            weights.append(weight.astype(jnp.bfloat16))
        mixture = jnp.dot(
            jnp.concatenate(weights, axis=0), value, preferred_element_type=jnp.float32
        )
        if lead == 0:
            send_copy.wait()
        for at, i in enumerate(heads):
            mix = mixture[at * query_len : (at + 1) * query_len]
            out_ref[send_here[i]] = (mix * totals[at]).astype(out_ref.dtype)


def place_kernel(head_size, held, ops, slots, *refs):
    out_ref, done = refs[-2:]
    odd = lax.axis_index("seq") & 1
    for (size, parts), ref in zip(ops, refs):
        distance, first, least = (jnp.where(odd == 0, *choice) for choice in zip(*parts))
        arriving = slots[head_size * held + distance]
        for index in range(size):
            rank = first + index

            @pl.when((rank >= least) & (rank < arriving))
            def _(ref=ref, rank=rank, index=index, distance=distance):
                at = pl.multiple_of(slots[distance * held + rank] * HD, HD)
                pltpu.make_async_copy(ref.at[index], out_ref.at[:, pl.ds(at, HD)], done).start()

    pltpu.make_async_copy(out_ref, out_ref, done).wait()


def capacity_levels(head_size, held):
    steps = sorted({max(1, held * c // 16) for c in (4, 5, 6, 7, 8)})
    fars = sorted(((b, c) for b in steps for c in steps), key=sum)
    fars += [(max(1, held * 10 // 16),) * 2, (held,) * 2]
    return [
        tuple(min(held, sum(far)) if m < head_size // 2 else far[m % 2] for m in range(head_size))
        for far in fars
    ]


def exchange_ops(head_size, held, capacities):
    if head_size != 4:
        return [(capacities[m], ((m, 0, 0),) * 2) for m in range(1, head_size)]
    b, c = capacities[2:]
    near, rest = (1, 0, 0), (1, min(b, held - c), b)
    middle, far = (2, 0, 0), (3, 0, 0)
    return [(c, (far, rest)), (b, (middle, near)), (c, (rest, far)), (b, (near, middle))]


def exchange(head_size, held, capacities, packed, slots):
    seq_size = lax.axis_size("seq")
    odd = lax.axis_index("seq") & 1
    ops = exchange_ops(head_size, held, capacities)
    arrived = []
    for size, parts in ops:
        even_at, odd_at = (distance * held + first for distance, first, _ in parts)
        pairs = [
            (i * head_size + z, i * head_size + (z ^ parts[i & 1][0]))
            for i in range(seq_size)
            for z in range(head_size)
        ]
        heads = lax.dynamic_slice_in_dim(packed, jnp.where(odd == 0, even_at, odd_at), size, axis=0)
        arrived.append(lax.ppermute(heads, ("seq", "head"), pairs))
    kept = (held, ((0, 0, 0),) * 2)
    return pl.pallas_call(
        functools.partial(place_kernel, head_size, held, [kept] + ops),
        out_shape=pltpu.HBM((packed.shape[1], held * HD), packed.dtype),
        in_specs=[SMEM] + [ANY] * (1 + len(ops)),
        out_specs=pl.BlockSpec(memory_space=pltpu.HBM),
        scratch_shapes=[pltpu.SemaphoreType.DMA],
        compiler_params=pltpu.CompilerParams(vmem_limit_bytes=SMALL),
        name="place",
    )(slots, packed, *arrived)


def per_device(queries, keys, values, vertical, slash, plan):
    seq_size = lax.axis_size("seq")
    head_size = lax.axis_size("head")
    query_len = queries.shape[0]
    held = queries.shape[1] // HD
    kv_heads = max(1, held // GROUP)
    chips = seq_size // 2
    assert query_len == BLK and plan.shape[0] == held * head_size and chips & (chips - 1) == 0

    levels = capacity_levels(head_size, held)
    send, slots, level, bits = pl.pallas_call(
        functools.partial(route_kernel, head_size, held, levels),
        out_shape=[
            jax.ShapeDtypeStruct((held + 1,), jnp.int32),
            jax.ShapeDtypeStruct((head_size * held + head_size,), jnp.int32),
            jax.ShapeDtypeStruct((1,), jnp.int32),
            jax.ShapeDtypeStruct((2, vertical.shape[0]), jnp.int32),
        ],
        in_specs=[SMEM, VMEM, VMEM],
        out_specs=[SMEM] * 3 + [VMEM],
        compiler_params=pltpu.CompilerParams(vmem_limit_bytes=SMALL),
        name="route",
    )(plan, vertical.T, slash.T)

    kv_at = lax.axis_index("head") * held // GROUP * HD
    kv = jnp.concatenate(
        [lax.dynamic_slice_in_dim(rows, kv_at, kv_heads * HD, axis=1) for rows in (keys, values)], axis=1
    )
    pieces = [kv]
    for m in range(1, chips):
        flips = (2 * m, 2 * turned(m, chips))
        pieces.append(lax.ppermute(kv, "seq", [(i, i ^ flips[i & 1]) for i in range(seq_size)]))
    pieces, send, slots, level, bits = lax.optimization_barrier((pieces, send, slots, level, bits))
    kv_own = jnp.concatenate(pieces, axis=0)
    kv_other = lax.ppermute(kv_own, "seq", [(i, i ^ 1) for i in range(seq_size)])

    packed = pl.pallas_call(
        functools.partial(attention_kernel, seq_size, held, kv_heads),
        out_shape=jax.ShapeDtypeStruct((head_size * held, query_len, HD), jnp.bfloat16),
        in_specs=[ANY] + [VMEM] * 4,
        out_specs=VMEM,
        scratch_shapes=[pltpu.SMEM(send.shape, send.dtype), pltpu.SemaphoreType.DMA],
        compiler_params=pltpu.CompilerParams(vmem_limit_bytes=40 * 1024 * 1024),
        name="attention",
    )(send, bits, kv_own, kv_other, queries)

    return lax.switch(
        level[0],
        [functools.partial(exchange, head_size, held, capacities) for capacities in levels],
        packed,
        slots,
    )


def solution(mesh):
    in_specs = (P("seq", "head"), P("seq", None), P("seq", None), P(), P(), P())
    out_specs = P("seq", "head")
    return jax.shard_map(
        per_device, mesh=mesh, in_specs=in_specs, out_specs=out_specs, check_vma=False
    )
```

```python
import functools
import math

import jax
import jax.numpy as jnp
from jax import lax
from jax.experimental import pallas as pl
from jax.experimental.pallas import tpu as pltpu
from jax.sharding import PartitionSpec as P

HD = 128
QH = 64
KVH = 8
BLK = 64
GROUP = QH // KVH
HEADS_AT_ONCE = 8
LANES = 128

floor_value = -1e30

SMEM = pl.BlockSpec(memory_space=pltpu.SMEM)
VMEM = pl.BlockSpec(memory_space=pltpu.VMEM)
ANY = pl.BlockSpec(memory_space=pl.ANY)
SMALL = 1024 * 1024


def shift_of(size):
    assert size & (size - 1) == 0
    return size.bit_length() - 1


def entry_bits(table):
    bits = jnp.zeros((1, table.shape[1]), jnp.int32)
    for entry in range(table.shape[0]):
        named = table[entry : entry + 1, :]
        bits = bits | jnp.where(named >= 0, jnp.int32(1) << jnp.maximum(named, 0), 0)
    return bits


class Tally:
    def __init__(self, head_size, held):
        self.width = shift_of(held) + 1
        self.per_word = 31 // self.width
        self.words = [jnp.int32(0)] * -(-head_size // self.per_word)

    def rank_and_count(self, owner):
        if len(self.words) == 1:
            at = owner * self.width
            rank = self.words[0] >> at
            self.words[0] = self.words[0] + (jnp.int32(1) << at)
        else:
            word = owner // self.per_word
            at = (owner - word * self.per_word) * self.width
            held_word = self.words[0]
            for index in range(1, len(self.words)):
                held_word = jnp.where(word == index, self.words[index], held_word)
            rank = held_word >> at
            one = jnp.int32(1) << at
            self.words = [w + jnp.where(word == index, one, 0) for index, w in enumerate(self.words)]
        return rank & ((1 << self.width) - 1)

    def count(self, owner):
        word = self.words[owner // self.per_word]
        return (word >> (owner % self.per_word * self.width)) & ((1 << self.width) - 1)


def route_kernel(head_size, held, levels, plan, vertical, slash, send, slots, level, bits):
    own = lax.axis_index("head")
    most = [jnp.int32(0)] * head_size
    for target in range(head_size):
        tally = Tally(head_size, held)
        for t in range(held):
            head = plan[target * held + t]
            owner = head >> shift_of(held)
            rank = tally.rank_and_count(owner)
            send[jnp.where(owner == own, head & (held - 1), held)] = ((owner ^ target) << shift_of(held)) + rank
        for owner in range(head_size):
            most[owner ^ target] = jnp.maximum(most[owner ^ target], tally.count(owner))
    tally = Tally(head_size, held)
    for distance in range(head_size):
        slots[head_size * held + distance] = 0
    for t in range(held):
        owner = plan[own * held + t] >> shift_of(held)
        rank = tally.rank_and_count(owner)
        distance = owner ^ own
        slots[(distance << shift_of(held)) + rank] = t
        slots[head_size * held + distance] = rank + 1
    chosen = jnp.int32(len(levels) - 1)
    for index in reversed(range(len(levels) - 1)):
        fits = most[1] <= levels[index][1]
        for distance in range(2, head_size):
            fits = fits & (most[distance] <= levels[index][distance])
        chosen = jnp.where(fits, index, chosen)
    level[0] = chosen
    bits[0:1, :] = entry_bits(vertical)
    bits[1:2, :] = entry_bits(slash)


def attention_kernel(
    seq_size, held, kv_heads, send, bits, kv_own, kv_other, query_ref, out_ref, send_here, copied
):
    send_copy = pltpu.make_async_copy(send, send_here, copied)
    send_copy.start()
    query_len = query_ref.shape[0]
    key_len = query_len
    own_seq = lax.axis_index("seq")
    own_head = lax.axis_index("head")
    chips = seq_size // 2
    half = chips * key_len

    piece = lax.broadcasted_iota(jnp.int32, (1, 2 * half), 1) // key_len
    core = jnp.where(piece < chips, own_seq & 1, 1 - (own_seq & 1))
    block = ((own_seq >> 1) ^ (piece & (chips - 1))) * 2 + core
    back = own_seq - block
    present = back >= 0
    back_shift = jnp.maximum(back, 0)
    heads = own_head * held + lax.broadcasted_iota(jnp.int32, (held, bits.shape[1]), 0)
    is_head = lax.broadcasted_iota(jnp.int32, (held, bits.shape[1]), 1) == heads
    vertical_bits, slash_bits = (
        jnp.sum(jnp.where(is_head, bits[kind : kind + 1, :], 0), axis=1, keepdims=True) for kind in range(2)
    )
    hit = ((vertical_bits >> block) | (slash_bits >> back_shift)) & 1
    bias = jnp.where((hit == 1) & present, 0.0, floor_value)
    row = lax.broadcasted_iota(jnp.int32, (query_len, LANES), 0)
    column = lax.broadcasted_iota(jnp.int32, (query_len, LANES), 1)
    causal = (column <= row) | (column >= key_len)
    score_scale = HD ** (-0.5) * math.log2(math.e)
    per_kv = held // kv_heads

    def scores_of(lead):
        heads = range(lead, min(lead + HEADS_AT_ONCE, held))
        key_at = lead // per_kv * HD
        key = jnp.concatenate([kv_own[:, key_at : key_at + HD], kv_other[:, key_at : key_at + HD]], axis=0)
        query = jnp.concatenate([query_ref[:, i * HD : (i + 1) * HD] for i in heads], axis=0)
        return lax.dot_general(
            query, key, (((1,), (1,)), ((), ())), preferred_element_type=jnp.float32
        )

    following = scores_of(0)
    for lead in range(0, held, HEADS_AT_ONCE):
        heads = range(lead, min(lead + HEADS_AT_ONCE, held))
        scores = following
        if lead + HEADS_AT_ONCE < held:
            following = scores_of(lead + HEADS_AT_ONCE)
        value_at = (lead // per_kv + kv_heads) * HD
        value = jnp.concatenate(
            [kv_own[:, value_at : value_at + HD], kv_other[:, value_at : value_at + HD]], axis=0
        )
        weights = []
        totals = []
        for at, i in enumerate(heads):
            masked = scores[at * query_len : (at + 1) * query_len] + bias[i : i + 1, :]
            masked = jnp.concatenate(
                [jnp.where(causal, masked[:, :LANES], floor_value), masked[:, LANES:]], axis=1
            )
            row_max = jnp.max(masked, axis=1, keepdims=True)
            weight = jnp.exp2((masked - row_max) * score_scale)
            totals.append(1.0 / jnp.sum(weight, axis=1, keepdims=True))
            weights.append(weight.astype(jnp.bfloat16))
        mixture = jnp.dot(
            jnp.concatenate(weights, axis=0), value, preferred_element_type=jnp.float32
        )
        if lead == 0:
            send_copy.wait()
        for at, i in enumerate(heads):
            mix = mixture[at * query_len : (at + 1) * query_len]
            out_ref[send_here[i]] = (mix * totals[at]).astype(out_ref.dtype)


def place_kernel(head_size, held, sources, slots, *refs):
    out_ref, done = refs[-2:]
    for (distance, capacity), ref in zip(sources, refs):
        arriving = slots[head_size * held + distance]
        for rank in range(capacity):

            @pl.when(rank < arriving)
            def _(ref=ref, rank=rank, distance=distance):
                at = pl.multiple_of(slots[distance * held + rank] * HD, HD)
                pltpu.make_async_copy(ref.at[rank], out_ref.at[:, pl.ds(at, HD)], done).start()

    pltpu.make_async_copy(out_ref, out_ref, done).wait()


def capacity_levels(head_size, held):
    near = max(1, held * 9 // 16)
    steps = sorted({max(1, held * c // 16) for c in (4, 5, 6, 7, 8)})
    even_odd = sorted(((b, c) for b in steps for c in steps), key=sum)
    levels = [
        tuple(near if m < head_size // 2 else far[m % 2] for m in range(head_size)) for far in even_odd
    ]
    return levels + [(max(1, held * 10 // 16),) * head_size, (held,) * head_size]


def exchange(head_size, held, capacities, packed, slots):
    order = range(1, head_size)
    arrived = [
        lax.ppermute(
            packed[m * held : m * held + capacities[m]], "head", [(i, i ^ m) for i in range(head_size)]
        )
        for m in order
    ]
    return pl.pallas_call(
        functools.partial(place_kernel, head_size, held, [(0, held)] + [(m, capacities[m]) for m in order]),
        out_shape=pltpu.HBM((packed.shape[1], held * HD), packed.dtype),
        in_specs=[SMEM] + [ANY] * head_size,
        out_specs=pl.BlockSpec(memory_space=pltpu.HBM),
        scratch_shapes=[pltpu.SemaphoreType.DMA],
        compiler_params=pltpu.CompilerParams(vmem_limit_bytes=SMALL),
        name="place",
    )(slots, packed, *arrived)


def per_device(queries, keys, values, vertical, slash, plan):
    seq_size = lax.axis_size("seq")
    head_size = lax.axis_size("head")
    query_len = queries.shape[0]
    held = queries.shape[1] // HD
    kv_heads = max(1, held // GROUP)
    chips = seq_size // 2
    assert query_len == BLK and plan.shape[0] == held * head_size and chips & (chips - 1) == 0

    levels = capacity_levels(head_size, held)
    send, slots, level, bits = pl.pallas_call(
        functools.partial(route_kernel, head_size, held, levels),
        out_shape=[
            jax.ShapeDtypeStruct((held + 1,), jnp.int32),
            jax.ShapeDtypeStruct((head_size * held + head_size,), jnp.int32),
            jax.ShapeDtypeStruct((1,), jnp.int32),
            jax.ShapeDtypeStruct((2, vertical.shape[0]), jnp.int32),
        ],
        in_specs=[SMEM, VMEM, VMEM],
        out_specs=[SMEM] * 3 + [VMEM],
        compiler_params=pltpu.CompilerParams(vmem_limit_bytes=SMALL),
        name="route",
    )(plan, vertical.T, slash.T)

    kv_at = lax.axis_index("head") * held // GROUP * HD
    kv = jnp.concatenate(
        [lax.dynamic_slice_in_dim(rows, kv_at, kv_heads * HD, axis=1) for rows in (keys, values)], axis=1
    )
    pieces = [kv]
    for m in range(1, chips):
        pairs = [(i, i ^ (2 * m)) for i in range(seq_size)]
        pieces.append(lax.ppermute(kv, "seq", pairs))
    pieces, send, slots, level, bits = lax.optimization_barrier((pieces, send, slots, level, bits))
    kv_own = jnp.concatenate(pieces, axis=0)
    kv_other = lax.ppermute(kv_own, "seq", [(i, i ^ 1) for i in range(seq_size)])

    packed = pl.pallas_call(
        functools.partial(attention_kernel, seq_size, held, kv_heads),
        out_shape=jax.ShapeDtypeStruct((head_size * held, query_len, HD), jnp.bfloat16),
        in_specs=[ANY] + [VMEM] * 4,
        out_specs=VMEM,
        scratch_shapes=[pltpu.SMEM(send.shape, send.dtype), pltpu.SemaphoreType.DMA],
        compiler_params=pltpu.CompilerParams(vmem_limit_bytes=40 * 1024 * 1024),
        name="attention",
    )(send, bits, kv_own, kv_other, queries)

    return lax.switch(
        level[0],
        [functools.partial(exchange, head_size, held, capacities) for capacities in levels],
        packed,
        slots,
    )


def solution(mesh):
    in_specs = (P("seq", "head"), P("seq", None), P("seq", None), P(), P(), P())
    out_specs = P("seq", "head")
    return jax.shard_map(
        per_device, mesh=mesh, in_specs=in_specs, out_specs=out_specs, check_vma=False
    )
```

```python
import functools
import math

import jax
import jax.numpy as jnp
from jax import lax
from jax.experimental import pallas as pl
from jax.experimental.pallas import tpu as pltpu
from jax.sharding import PartitionSpec as P

HD = 128
QH = 64
KVH = 8
BLK = 64
GROUP = QH // KVH
HEADS_AT_ONCE = 4
LANES = 128

floor_value = -1e30

SMEM = pl.BlockSpec(memory_space=pltpu.SMEM)
VMEM = pl.BlockSpec(memory_space=pltpu.VMEM)
ANY = pl.BlockSpec(memory_space=pl.ANY)
SMALL = 1024 * 1024


def shift_of(size):
    assert size & (size - 1) == 0
    return size.bit_length() - 1


def entry_bits(table):
    bits = jnp.zeros((1, table.shape[1]), jnp.int32)
    for entry in range(table.shape[0]):
        named = table[entry : entry + 1, :]
        bits = bits | jnp.where(named >= 0, jnp.int32(1) << jnp.maximum(named, 0), 0)
    return bits


class Tally:
    def __init__(self, head_size, held):
        self.width = shift_of(held) + 1
        self.per_word = 31 // self.width
        self.words = [jnp.int32(0)] * -(-head_size // self.per_word)

    def rank_and_count(self, owner):
        if len(self.words) == 1:
            at = owner * self.width
            rank = self.words[0] >> at
            self.words[0] = self.words[0] + (jnp.int32(1) << at)
        else:
            word = owner // self.per_word
            at = (owner - word * self.per_word) * self.width
            held_word = self.words[0]
            for index in range(1, len(self.words)):
                held_word = jnp.where(word == index, self.words[index], held_word)
            rank = held_word >> at
            one = jnp.int32(1) << at
            self.words = [w + jnp.where(word == index, one, 0) for index, w in enumerate(self.words)]
        return rank & ((1 << self.width) - 1)

    def count(self, owner):
        word = self.words[owner // self.per_word]
        return (word >> (owner % self.per_word * self.width)) & ((1 << self.width) - 1)


def route_kernel(head_size, held, levels, plan, vertical, slash, send, slots, level, bits):
    own = lax.axis_index("head")
    most = [jnp.int32(0)] * head_size
    for target in range(head_size):
        tally = Tally(head_size, held)
        for t in range(held):
            head = plan[target * held + t]
            owner = head >> shift_of(held)
            rank = tally.rank_and_count(owner)
            send[jnp.where(owner == own, head & (held - 1), held)] = ((owner ^ target) << shift_of(held)) + rank
        for owner in range(head_size):
            most[owner ^ target] = jnp.maximum(most[owner ^ target], tally.count(owner))
    tally = Tally(head_size, held)
    for distance in range(head_size):
        slots[head_size * held + distance] = 0
    for t in range(held):
        owner = plan[own * held + t] >> shift_of(held)
        rank = tally.rank_and_count(owner)
        distance = owner ^ own
        slots[(distance << shift_of(held)) + rank] = t
        slots[head_size * held + distance] = rank + 1
    chosen = jnp.int32(len(levels) - 1)
    for index in reversed(range(len(levels) - 1)):
        fits = most[1] <= levels[index][1]
        for distance in range(2, head_size):
            fits = fits & (most[distance] <= levels[index][distance])
        chosen = jnp.where(fits, index, chosen)
    level[0] = chosen
    bits[0:1, :] = entry_bits(vertical)
    bits[1:2, :] = entry_bits(slash)


def attention_kernel(
    seq_size, held, kv_heads, send, bits, kv_own, kv_other, query_ref, out_ref, send_here, copied
):
    send_copy = pltpu.make_async_copy(send, send_here, copied)
    send_copy.start()
    query_len = query_ref.shape[0]
    key_len = query_len
    own_seq = lax.axis_index("seq")
    own_head = lax.axis_index("head")
    chips = seq_size // 2
    half = chips * key_len

    piece = lax.broadcasted_iota(jnp.int32, (1, 2 * half), 1) // key_len
    core = jnp.where(piece < chips, own_seq & 1, 1 - (own_seq & 1))
    block = ((own_seq >> 1) ^ (piece & (chips - 1))) * 2 + core
    back = own_seq - block
    present = back >= 0
    back_shift = jnp.maximum(back, 0)
    heads = own_head * held + lax.broadcasted_iota(jnp.int32, (held, bits.shape[1]), 0)
    is_head = lax.broadcasted_iota(jnp.int32, (held, bits.shape[1]), 1) == heads
    vertical_bits, slash_bits = (
        jnp.sum(jnp.where(is_head, bits[kind : kind + 1, :], 0), axis=1, keepdims=True) for kind in range(2)
    )
    hit = ((vertical_bits >> block) | (slash_bits >> back_shift)) & 1
    bias = jnp.where((hit == 1) & present, 0.0, floor_value)
    row = lax.broadcasted_iota(jnp.int32, (query_len, LANES), 0)
    column = lax.broadcasted_iota(jnp.int32, (query_len, LANES), 1)
    causal = (column <= row) | (column >= key_len)
    score_scale = HD ** (-0.5) * math.log2(math.e)
    per_kv = held // kv_heads

    def scores_of(lead):
        heads = range(lead, min(lead + HEADS_AT_ONCE, held))
        key_at = lead // per_kv * HD
        key = jnp.concatenate([kv_own[:, key_at : key_at + HD], kv_other[:, key_at : key_at + HD]], axis=0)
        query = jnp.concatenate([query_ref[:, i * HD : (i + 1) * HD] for i in heads], axis=0)
        return lax.dot_general(
            query, key, (((1,), (1,)), ((), ())), preferred_element_type=jnp.float32
        )

    following = scores_of(0)
    for lead in range(0, held, HEADS_AT_ONCE):
        heads = range(lead, min(lead + HEADS_AT_ONCE, held))
        scores = following
        if lead + HEADS_AT_ONCE < held:
            following = scores_of(lead + HEADS_AT_ONCE)
        value_at = (lead // per_kv + kv_heads) * HD
        value = jnp.concatenate(
            [kv_own[:, value_at : value_at + HD], kv_other[:, value_at : value_at + HD]], axis=0
        )
        weights = []
        totals = []
        for at, i in enumerate(heads):
            masked = scores[at * query_len : (at + 1) * query_len] + bias[i : i + 1, :]
            masked = jnp.concatenate(
                [jnp.where(causal, masked[:, :LANES], floor_value), masked[:, LANES:]], axis=1
            )
            row_max = jnp.max(masked, axis=1, keepdims=True)
            weight = jnp.exp2((masked - row_max) * score_scale)
            totals.append(1.0 / jnp.sum(weight, axis=1, keepdims=True))
            weights.append(weight.astype(jnp.bfloat16))
        mixture = jnp.dot(
            jnp.concatenate(weights, axis=0), value, preferred_element_type=jnp.float32
        )
        if lead == 0:
            send_copy.wait()
        for at, i in enumerate(heads):
            mix = mixture[at * query_len : (at + 1) * query_len]
            out_ref[send_here[i]] = (mix * totals[at]).astype(out_ref.dtype)


def place_kernel(head_size, held, ops, slots, *refs):
    out_ref, done = refs[-2:]
    odd = lax.axis_index("seq") & 1
    for (size, parts), ref in zip(ops, refs):
        distance, first, least = (jnp.where(odd == 0, *choice) for choice in zip(*parts))
        arriving = slots[head_size * held + distance]
        for index in range(size):
            rank = first + index

            @pl.when((rank >= least) & (rank < arriving))
            def _(ref=ref, rank=rank, index=index, distance=distance):
                at = pl.multiple_of(slots[distance * held + rank] * HD, HD)
                pltpu.make_async_copy(ref.at[index], out_ref.at[:, pl.ds(at, HD)], done).start()

    pltpu.make_async_copy(out_ref, out_ref, done).wait()


def capacity_levels(head_size, held):
    steps = sorted({max(1, held * c // 16) for c in (4, 5, 6, 7, 8)})
    fars = sorted(((b, c) for b in steps for c in steps), key=sum)
    fars += [(max(1, held * 10 // 16),) * 2, (held,) * 2]
    return [
        tuple(min(held, sum(far)) if m < head_size // 2 else far[m % 2] for m in range(head_size))
        for far in fars
    ]


def exchange_ops(head_size, held, capacities):
    if head_size != 4:
        return [(capacities[m], ((m, 0, 0),) * 2) for m in range(1, head_size)]
    b, c = capacities[2:]
    near, rest = (1, 0, 0), (1, min(b, held - c), b)
    middle, far = (2, 0, 0), (3, 0, 0)
    return [(c, (rest, far)), (b, (near, middle)), (c, (far, rest)), (b, (middle, near))]


def exchange(head_size, held, capacities, packed, slots):
    seq_size = lax.axis_size("seq")
    odd = lax.axis_index("seq") & 1
    ops = exchange_ops(head_size, held, capacities)
    arrived = []
    for size, parts in ops:
        even_at, odd_at = (distance * held + first for distance, first, _ in parts)
        pairs = [
            (i * head_size + z, i * head_size + (z ^ parts[i & 1][0]))
            for i in range(seq_size)
            for z in range(head_size)
        ]
        heads = lax.dynamic_slice_in_dim(packed, jnp.where(odd == 0, even_at, odd_at), size, axis=0)
        arrived.append(lax.ppermute(heads, ("seq", "head"), pairs))
    kept = (held, ((0, 0, 0),) * 2)
    return pl.pallas_call(
        functools.partial(place_kernel, head_size, held, [kept] + ops),
        out_shape=pltpu.HBM((packed.shape[1], held * HD), packed.dtype),
        in_specs=[SMEM] + [ANY] * (1 + len(ops)),
        out_specs=pl.BlockSpec(memory_space=pltpu.HBM),
        scratch_shapes=[pltpu.SemaphoreType.DMA],
        compiler_params=pltpu.CompilerParams(vmem_limit_bytes=SMALL),
        name="place",
    )(slots, packed, *arrived)


def per_device(queries, keys, values, vertical, slash, plan):
    seq_size = lax.axis_size("seq")
    head_size = lax.axis_size("head")
    query_len = queries.shape[0]
    held = queries.shape[1] // HD
    kv_heads = max(1, held // GROUP)
    chips = seq_size // 2
    assert query_len == BLK and plan.shape[0] == held * head_size and chips & (chips - 1) == 0

    levels = capacity_levels(head_size, held)
    send, slots, level, bits = pl.pallas_call(
        functools.partial(route_kernel, head_size, held, levels),
        out_shape=[
            jax.ShapeDtypeStruct((held + 1,), jnp.int32),
            jax.ShapeDtypeStruct((head_size * held + head_size,), jnp.int32),
            jax.ShapeDtypeStruct((1,), jnp.int32),
            jax.ShapeDtypeStruct((2, vertical.shape[0]), jnp.int32),
        ],
        in_specs=[SMEM, VMEM, VMEM],
        out_specs=[SMEM] * 3 + [VMEM],
        compiler_params=pltpu.CompilerParams(vmem_limit_bytes=SMALL),
        name="route",
    )(plan, vertical.T, slash.T)

    kv_at = lax.axis_index("head") * held // GROUP * HD
    kv = jnp.concatenate(
        [lax.dynamic_slice_in_dim(rows, kv_at, kv_heads * HD, axis=1) for rows in (keys, values)], axis=1
    )
    pieces = [kv]
    for m in range(1, chips):
        pieces.append(lax.ppermute(kv, "seq", [(i, i ^ (2 * m)) for i in range(seq_size)]))
    pieces, send, slots, level, bits = lax.optimization_barrier((pieces, send, slots, level, bits))
    kv_own = jnp.concatenate(pieces, axis=0)
    kv_other = lax.ppermute(kv_own, "seq", [(i, i ^ 1) for i in range(seq_size)])

    packed = pl.pallas_call(
        functools.partial(attention_kernel, seq_size, held, kv_heads),
        out_shape=jax.ShapeDtypeStruct((head_size * held, query_len, HD), jnp.bfloat16),
        in_specs=[ANY] + [VMEM] * 4,
        out_specs=VMEM,
        scratch_shapes=[pltpu.SMEM(send.shape, send.dtype), pltpu.SemaphoreType.DMA],
        compiler_params=pltpu.CompilerParams(vmem_limit_bytes=40 * 1024 * 1024),
        name="attention",
    )(send, bits, kv_own, kv_other, queries)

    return lax.switch(
        level[0],
        [functools.partial(exchange, head_size, held, capacities) for capacities in levels],
        packed,
        slots,
    )


def solution(mesh):
    in_specs = (P("seq", "head"), P("seq", None), P("seq", None), P(), P(), P())
    out_specs = P("seq", "head")
    return jax.shard_map(
        per_device, mesh=mesh, in_specs=in_specs, out_specs=out_specs, check_vma=False
    )
```

```python
import functools
import math

import jax
import jax.numpy as jnp
from jax import lax
from jax.experimental import pallas as pl
from jax.experimental.pallas import tpu as pltpu
from jax.sharding import PartitionSpec as P

HD = 128
QH = 64
KVH = 8
BLK = 64
GROUP = QH // KVH
HEADS_AT_ONCE = 4
LANES = 128

floor_value = -1e30

SMEM = pl.BlockSpec(memory_space=pltpu.SMEM)
VMEM = pl.BlockSpec(memory_space=pltpu.VMEM)
ANY = pl.BlockSpec(memory_space=pl.ANY)
SMALL = 1024 * 1024


def shift_of(size):
    assert size & (size - 1) == 0
    return size.bit_length() - 1


def entry_bits(table):
    bits = jnp.zeros((1, table.shape[1]), jnp.int32)
    for entry in range(table.shape[0]):
        named = table[entry : entry + 1, :]
        bits = bits | jnp.where(named >= 0, jnp.int32(1) << jnp.maximum(named, 0), 0)
    return bits


class Tally:
    def __init__(self, head_size, held):
        self.width = shift_of(held) + 1
        self.per_word = 31 // self.width
        self.words = [jnp.int32(0)] * -(-head_size // self.per_word)

    def rank_and_count(self, owner):
        if len(self.words) == 1:
            at = owner * self.width
            rank = self.words[0] >> at
            self.words[0] = self.words[0] + (jnp.int32(1) << at)
        else:
            word = owner // self.per_word
            at = (owner - word * self.per_word) * self.width
            held_word = self.words[0]
            for index in range(1, len(self.words)):
                held_word = jnp.where(word == index, self.words[index], held_word)
            rank = held_word >> at
            one = jnp.int32(1) << at
            self.words = [w + jnp.where(word == index, one, 0) for index, w in enumerate(self.words)]
        return rank & ((1 << self.width) - 1)

    def count(self, owner):
        word = self.words[owner // self.per_word]
        return (word >> (owner % self.per_word * self.width)) & ((1 << self.width) - 1)


def route_kernel(head_size, held, levels, plan, vertical, slash, send, slots, level, bits):
    own = lax.axis_index("head")
    most = [jnp.int32(0)] * head_size
    for target in range(head_size):
        tally = Tally(head_size, held)
        for t in range(held):
            head = plan[target * held + t]
            owner = head >> shift_of(held)
            rank = tally.rank_and_count(owner)
            send[jnp.where(owner == own, head & (held - 1), held)] = ((owner ^ target) << shift_of(held)) + rank
        for owner in range(head_size):
            most[owner ^ target] = jnp.maximum(most[owner ^ target], tally.count(owner))
    tally = Tally(head_size, held)
    for distance in range(head_size):
        slots[head_size * held + distance] = 0
    for t in range(held):
        owner = plan[own * held + t] >> shift_of(held)
        rank = tally.rank_and_count(owner)
        distance = owner ^ own
        slots[(distance << shift_of(held)) + rank] = t
        slots[head_size * held + distance] = rank + 1
    chosen = jnp.int32(len(levels) - 1)
    for index in reversed(range(len(levels) - 1)):
        fits = most[1] <= levels[index][1]
        for distance in range(2, head_size):
            fits = fits & (most[distance] <= levels[index][distance])
        chosen = jnp.where(fits, index, chosen)
    level[0] = chosen
    bits[0:1, :] = entry_bits(vertical)
    bits[1:2, :] = entry_bits(slash)


def attention_kernel(
    seq_size, held, kv_heads, send, bits, kv_own, kv_other, query_ref, out_ref, send_here, copied
):
    send_copy = pltpu.make_async_copy(send, send_here, copied)
    send_copy.start()
    query_len = query_ref.shape[0]
    key_len = query_len
    own_seq = lax.axis_index("seq")
    own_head = lax.axis_index("head")
    chips = seq_size // 2
    half = chips * key_len

    piece = lax.broadcasted_iota(jnp.int32, (1, 2 * half), 1) // key_len
    core = jnp.where(piece < chips, own_seq & 1, 1 - (own_seq & 1))
    block = ((own_seq >> 1) ^ (piece & (chips - 1))) * 2 + core
    back = own_seq - block
    present = back >= 0
    back_shift = jnp.maximum(back, 0)
    heads = own_head * held + lax.broadcasted_iota(jnp.int32, (held, bits.shape[1]), 0)
    is_head = lax.broadcasted_iota(jnp.int32, (held, bits.shape[1]), 1) == heads
    vertical_bits, slash_bits = (
        jnp.sum(jnp.where(is_head, bits[kind : kind + 1, :], 0), axis=1, keepdims=True) for kind in range(2)
    )
    hit = ((vertical_bits >> block) | (slash_bits >> back_shift)) & 1
    bias = jnp.where((hit == 1) & present, 0.0, floor_value)
    row = lax.broadcasted_iota(jnp.int32, (query_len, LANES), 0)
    column = lax.broadcasted_iota(jnp.int32, (query_len, LANES), 1)
    causal = (column <= row) | (column >= key_len)
    score_scale = HD ** (-0.5) * math.log2(math.e)
    per_kv = held // kv_heads

    def rows_of(at):
        return jnp.concatenate(
            [
                ref[(own_seq >> 1) ^ m, :, at : at + HD]
                for ref in (kv_own, kv_other)
                for m in range(chips)
            ],
            axis=0,
        )

    def scores_of(lead):
        heads = range(lead, min(lead + HEADS_AT_ONCE, held))
        key = rows_of(lead // per_kv * HD)
        query = jnp.concatenate([query_ref[:, i * HD : (i + 1) * HD] for i in heads], axis=0)
        return lax.dot_general(
            query, key, (((1,), (1,)), ((), ())), preferred_element_type=jnp.float32
        )

    following = scores_of(0)
    for lead in range(0, held, HEADS_AT_ONCE):
        heads = range(lead, min(lead + HEADS_AT_ONCE, held))
        scores = following
        if lead + HEADS_AT_ONCE < held:
            following = scores_of(lead + HEADS_AT_ONCE)
        value = rows_of((lead // per_kv + kv_heads) * HD)
        weights = []
        totals = []
        for at, i in enumerate(heads):
            masked = scores[at * query_len : (at + 1) * query_len] + bias[i : i + 1, :]
            masked = jnp.concatenate(
                [jnp.where(causal, masked[:, :LANES], floor_value), masked[:, LANES:]], axis=1
            )
            row_max = jnp.max(masked, axis=1, keepdims=True)
            weight = jnp.exp2((masked - row_max) * score_scale)
            totals.append(1.0 / jnp.sum(weight, axis=1, keepdims=True))
            weights.append(weight.astype(jnp.bfloat16))
        mixture = jnp.dot(
            jnp.concatenate(weights, axis=0), value, preferred_element_type=jnp.float32
        )
        if lead == 0:
            send_copy.wait()
        for at, i in enumerate(heads):
            mix = mixture[at * query_len : (at + 1) * query_len]
            out_ref[send_here[i]] = (mix * totals[at]).astype(out_ref.dtype)


def place_kernel(head_size, held, sources, slots, *refs):
    out_ref, done = refs[-2:]
    for (distance, capacity), ref in zip(sources, refs):
        arriving = slots[head_size * held + distance]
        for rank in range(capacity):

            @pl.when(rank < arriving)
            def _(ref=ref, rank=rank, distance=distance):
                at = pl.multiple_of(slots[distance * held + rank] * HD, HD)
                pltpu.make_async_copy(ref.at[rank], out_ref.at[:, pl.ds(at, HD)], done).start()

    pltpu.make_async_copy(out_ref, out_ref, done).wait()


def capacity_levels(head_size, held):
    near = max(1, held * 9 // 16)
    steps = sorted({max(1, held * c // 16) for c in (4, 5, 6, 7, 8)})
    even_odd = sorted(((b, c) for b in steps for c in steps), key=sum)
    levels = [
        tuple(near if m < head_size // 2 else far[m % 2] for m in range(head_size)) for far in even_odd
    ]
    return levels + [(max(1, held * 10 // 16),) * head_size, (held,) * head_size]


def exchange(head_size, held, capacities, packed, slots):
    order = sorted(range(1, head_size), key=lambda m: (m >= head_size // 2, -m))
    arrived = [
        lax.ppermute(
            packed[m * held : m * held + capacities[m]], "head", [(i, i ^ m) for i in range(head_size)]
        )
        for m in order
    ]
    return pl.pallas_call(
        functools.partial(place_kernel, head_size, held, [(0, held)] + [(m, capacities[m]) for m in order]),
        out_shape=pltpu.HBM((packed.shape[1], held * HD), packed.dtype),
        in_specs=[SMEM] + [ANY] * head_size,
        out_specs=pl.BlockSpec(memory_space=pltpu.HBM),
        scratch_shapes=[pltpu.SemaphoreType.DMA],
        compiler_params=pltpu.CompilerParams(vmem_limit_bytes=SMALL),
        name="place",
    )(slots, packed, *arrived)


def per_device(queries, keys, values, vertical, slash, plan):
    seq_size = lax.axis_size("seq")
    head_size = lax.axis_size("head")
    query_len = queries.shape[0]
    held = queries.shape[1] // HD
    kv_heads = max(1, held // GROUP)
    chips = seq_size // 2
    assert query_len == BLK and plan.shape[0] == held * head_size and chips & (chips - 1) == 0

    levels = capacity_levels(head_size, held)
    send, slots, level, bits = pl.pallas_call(
        functools.partial(route_kernel, head_size, held, levels),
        out_shape=[
            jax.ShapeDtypeStruct((held + 1,), jnp.int32),
            jax.ShapeDtypeStruct((head_size * held + head_size,), jnp.int32),
            jax.ShapeDtypeStruct((1,), jnp.int32),
            jax.ShapeDtypeStruct((2, vertical.shape[0]), jnp.int32),
        ],
        in_specs=[SMEM, VMEM, VMEM],
        out_specs=[SMEM] * 3 + [VMEM],
        compiler_params=pltpu.CompilerParams(vmem_limit_bytes=SMALL),
        name="route",
    )(plan, vertical.T, slash.T)

    kv_at = lax.axis_index("head") * held // GROUP * HD
    kv = jnp.concatenate(
        [lax.dynamic_slice_in_dim(rows, kv_at, kv_heads * HD, axis=1) for rows in (keys, values)], axis=1
    )
    kv_own = lax.all_to_all(
        jnp.broadcast_to(kv[None], (chips,) + kv.shape),
        "seq",
        0,
        0,
        axis_index_groups=[list(range(core, seq_size, 2)) for core in range(2)],
    )
    kv_own, send, slots, level, bits = lax.optimization_barrier((kv_own, send, slots, level, bits))
    kv_other = lax.ppermute(kv_own, "seq", [(i, i ^ 1) for i in range(seq_size)])

    packed = pl.pallas_call(
        functools.partial(attention_kernel, seq_size, held, kv_heads),
        out_shape=jax.ShapeDtypeStruct((head_size * held, query_len, HD), jnp.bfloat16),
        in_specs=[ANY] + [VMEM] * 4,
        out_specs=VMEM,
        scratch_shapes=[pltpu.SMEM(send.shape, send.dtype), pltpu.SemaphoreType.DMA],
        compiler_params=pltpu.CompilerParams(vmem_limit_bytes=40 * 1024 * 1024),
        name="attention",
    )(send, bits, kv_own, kv_other, queries)

    return lax.switch(
        level[0],
        [functools.partial(exchange, head_size, held, capacities) for capacities in levels],
        packed,
        slots,
    )


def solution(mesh):
    in_specs = (P("seq", "head"), P("seq", None), P("seq", None), P(), P(), P())
    out_specs = P("seq", "head")
    return jax.shard_map(
        per_device, mesh=mesh, in_specs=in_specs, out_specs=out_specs, check_vma=False
    )
```

```python
import functools
import math

import jax
import jax.numpy as jnp
from jax import lax
from jax.experimental import pallas as pl
from jax.experimental.pallas import tpu as pltpu
from jax.sharding import PartitionSpec as P

HD = 128
QH = 64
KVH = 8
BLK = 64
GROUP = QH // KVH
HEADS_AT_ONCE = 4
LANES = 128
EARLY = 7

floor_value = -1e30

SMEM = pl.BlockSpec(memory_space=pltpu.SMEM)
VMEM = pl.BlockSpec(memory_space=pltpu.VMEM)
ANY = pl.BlockSpec(memory_space=pl.ANY)
SMALL = 1024 * 1024


def in_hbm(*arrays):
    return [pltpu.with_memory_space_constraint(array, pltpu.HBM) for array in arrays]


def shift_of(size):
    assert size & (size - 1) == 0
    return size.bit_length() - 1


def entry_bits(table):
    bits = jnp.zeros((1, table.shape[1]), jnp.int32)
    for entry in range(table.shape[0]):
        named = table[entry : entry + 1, :]
        bits = bits | jnp.where(named >= 0, jnp.int32(1) << jnp.maximum(named, 0), 0)
    return bits


class Tally:
    def __init__(self, head_size, held):
        self.width = shift_of(held) + 1
        self.per_word = 31 // self.width
        self.words = [jnp.int32(0)] * -(-head_size // self.per_word)

    def rank_and_count(self, owner):
        if len(self.words) == 1:
            at = owner * self.width
            rank = self.words[0] >> at
            self.words[0] = self.words[0] + (jnp.int32(1) << at)
        else:
            word = owner // self.per_word
            at = (owner - word * self.per_word) * self.width
            held_word = self.words[0]
            for index in range(1, len(self.words)):
                held_word = jnp.where(word == index, self.words[index], held_word)
            rank = held_word >> at
            one = jnp.int32(1) << at
            self.words = [w + jnp.where(word == index, one, 0) for index, w in enumerate(self.words)]
        return rank & ((1 << self.width) - 1)

    def count(self, owner):
        word = self.words[owner // self.per_word]
        return (word >> (owner % self.per_word * self.width)) & ((1 << self.width) - 1)


def pick_kernel(head_size, held, early, widths, keys, values, queries, kv, early_queries, done):
    own = lax.axis_index("head")
    copies = [(queries.at[:, : early * HD], early_queries)]
    at = 0
    for rows in (keys, values):
        for holder, width in zip((own, own ^ (head_size // 2)), widths):
            first = pl.multiple_of(((holder * held) >> shift_of(GROUP)) * HD, HD)
            copies.append((rows.at[:, pl.ds(first, width)], kv.at[:, at : at + width]))
            at += width
    copies = [pltpu.make_async_copy(*ends, done.at[index]) for index, ends in enumerate(copies)]
    for copy in copies[1:] + copies[:1]:
        copy.start()
    for copy in copies:
        copy.wait()


def route_kernel(
    head_size, held, early, levels, plan_in, vertical_in, slash_in, send, slots, level, bits, plan, tables, copied
):
    copies = [
        pltpu.make_async_copy(source, target, copied.at[index])
        for index, (source, target) in enumerate(
            ((plan_in, plan), (vertical_in, tables.at[0]), (slash_in, tables.at[1]))
        )
    ]
    for copy in copies:
        copy.start()
    for copy in copies:
        copy.wait()
    own = lax.axis_index("head")
    half = head_size // 2

    def source_of(head, target):
        owner = head >> shift_of(held)
        swapped = (owner & (half - 1)) | (target & half)
        return owner, jnp.where((head & (held - 1)) < early, swapped, owner)

    for candidate in range(held + early):
        send[candidate] = head_size * held
    most = [jnp.int32(0)] * head_size
    for target in range(head_size):
        tally = Tally(head_size, held)
        for t in range(held):
            head = plan[target * held + t]
            owner, source = source_of(head, target)
            rank = tally.rank_and_count(source)
            candidate = (head & (held - 1)) + jnp.where(owner == own, 0, held)
            candidate = jnp.where(source == own, candidate, held + early)
            send[candidate] = ((source ^ target) << shift_of(held)) + rank
        for source in range(head_size):
            most[source ^ target] = jnp.maximum(most[source ^ target], tally.count(source))
    tally = Tally(head_size, held)
    for distance in range(head_size):
        slots[head_size * held + distance] = 0
    for t in range(held):
        _, source = source_of(plan[own * held + t], own)
        rank = tally.rank_and_count(source)
        distance = source ^ own
        slots[(distance << shift_of(held)) + rank] = t
        slots[head_size * held + distance] = rank + 1
    chosen = jnp.int32(len(levels) - 1)
    for index in reversed(range(len(levels) - 1)):
        fits = most[1] <= levels[index][1]
        for distance in range(2, head_size):
            fits = fits & (most[distance] <= levels[index][distance])
        chosen = jnp.where(fits, index, chosen)
    level[0] = chosen
    for kind in range(2):
        bits[kind : kind + 1, :] = entry_bits(tables[kind])


def attention_kernel(
    seq_size, head_size, held, widths, send, bits, kv_own, kv_other, near, far, out_ref, send_here, copied
):
    send_copy = pltpu.make_async_copy(send, send_here, copied)
    send_copy.start()
    query_len = near.shape[0]
    key_len = query_len
    early = far.shape[1] // HD
    own_seq = lax.axis_index("seq")
    own_head = lax.axis_index("head")
    chips = seq_size // 2
    half = chips * key_len

    piece = lax.broadcasted_iota(jnp.int32, (1, 2 * half), 1) // key_len
    core = jnp.where(piece < chips, own_seq & 1, 1 - (own_seq & 1))
    block = ((own_seq >> 1) ^ (piece & (chips - 1))) * 2 + core
    back = own_seq - block
    present = back >= 0
    back_shift = jnp.maximum(back, 0)
    candidate = lax.broadcasted_iota(jnp.int32, (held + early, bits.shape[1]), 0)
    head = jnp.where(
        candidate < held, own_head * held + candidate, (own_head ^ (head_size // 2)) * held + candidate - held
    )
    is_head = lax.broadcasted_iota(jnp.int32, (held + early, bits.shape[1]), 1) == head
    vertical_bits, slash_bits = (
        jnp.sum(jnp.where(is_head, bits[kind : kind + 1, :], 0), axis=1, keepdims=True) for kind in range(2)
    )
    hit = ((vertical_bits >> block) | (slash_bits >> back_shift)) & 1
    bias = jnp.where((hit == 1) & present, 0.0, floor_value)
    row = lax.broadcasted_iota(jnp.int32, (query_len, LANES), 0)
    column = lax.broadcasted_iota(jnp.int32, (query_len, LANES), 1)
    causal = (column <= row) | (column >= key_len)
    score_scale = HD ** (-0.5) * math.log2(math.e)
    per_kv = held // (widths[0] // HD)
    together = min(HEADS_AT_ONCE, per_kv)
    groups = [(lead, lead + together, lead // per_kv) for lead in range(0, held, together)]
    groups += [
        (held + lead, held + min(lead + together, early), widths[0] // HD + lead // per_kv)
        for lead in range(0, early, together)
    ]

    def rows_of(at):
        return jnp.concatenate([kv_own[:, at : at + HD], kv_other[:, at : at + HD]], axis=0)

    def scores_of(first, last, kv_head):
        query = jnp.concatenate(
            [
                near[:, i * HD : (i + 1) * HD] if i < held else far[:, (i - held) * HD : (i - held + 1) * HD]
                for i in range(first, last)
            ],
            axis=0,
        )
        return lax.dot_general(
            query, rows_of(kv_head * HD), (((1,), (1,)), ((), ())), preferred_element_type=jnp.float32
        )

    following = scores_of(*groups[0])
    for index, (first, last, kv_head) in enumerate(groups):
        scores = following
        if index + 1 < len(groups):
            following = scores_of(*groups[index + 1])
        value = rows_of(kv_head * HD + sum(widths))
        weights = []
        totals = []
        for at, i in enumerate(range(first, last)):
            masked = scores[at * query_len : (at + 1) * query_len] + bias[i : i + 1, :]
            masked = jnp.concatenate(
                [jnp.where(causal, masked[:, :LANES], floor_value), masked[:, LANES:]], axis=1
            )
            row_max = jnp.max(masked, axis=1, keepdims=True)
            weight = jnp.exp2((masked - row_max) * score_scale)
            totals.append(1.0 / jnp.sum(weight, axis=1, keepdims=True))
            weights.append(weight.astype(jnp.bfloat16))
        mixture = jnp.dot(
            jnp.concatenate(weights, axis=0), value, preferred_element_type=jnp.float32
        )
        if index == 0:
            send_copy.wait()
        for at, i in enumerate(range(first, last)):
            mix = mixture[at * query_len : (at + 1) * query_len]
            out_ref[send_here[i]] = (mix * totals[at]).astype(out_ref.dtype)


def place_kernel(head_size, held, sources, slots, *refs):
    out_ref, done = refs[-2:]
    for (distance, capacity), ref in zip(sources, refs):
        arriving = slots[head_size * held + distance]
        for rank in range(capacity):

            @pl.when(rank < arriving)
            def _(ref=ref, rank=rank, distance=distance):
                at = pl.multiple_of(slots[distance * held + rank] * HD, HD)
                pltpu.make_async_copy(ref.at[rank], out_ref.at[:, pl.ds(at, HD)], done).start()

    pltpu.make_async_copy(out_ref, out_ref, done).wait()


def capacity_levels(head_size, held):
    fars = [(b, c) for b in (2, 3, 4, 5) for c in (2, 3, 4, 5) if 5 <= b + c <= 8 and abs(b - c) <= 1]
    shapes = [(near, b, c) for near in (7, 8, 9, 11) for b, c in fars] + [(12, 7, 7)]
    shapes.sort(key=lambda shape: max(sum(shape), 2 * (shape[1] + shape[2])))
    shapes = [tuple(max(1, held * part // 16) for part in shape) for shape in shapes]
    levels = []
    for near, *far in shapes + [(held,) * 3]:
        level = tuple(near if m < head_size // 2 else far[m % 2] for m in range(head_size))
        if level not in levels:
            levels.append(level)
    return levels


def exchange(head_size, held, capacities, packed, slots):
    order = sorted(range(1, head_size), key=lambda m: (m >= head_size // 2, -m))
    arrived = [
        lax.ppermute(
            packed[m * held : m * held + capacities[m]], "head", [(i, i ^ m) for i in range(head_size)]
        )
        for m in order
    ]
    return pl.pallas_call(
        functools.partial(place_kernel, head_size, held, [(0, held)] + [(m, capacities[m]) for m in order]),
        out_shape=pltpu.HBM((packed.shape[1], held * HD), packed.dtype),
        in_specs=[SMEM] + [ANY] * head_size,
        out_specs=pl.BlockSpec(memory_space=pltpu.HBM),
        scratch_shapes=[pltpu.SemaphoreType.DMA],
        compiler_params=pltpu.CompilerParams(vmem_limit_bytes=SMALL),
        name="place",
    )(slots, packed, *arrived)


def per_device(queries, keys, values, vertical, slash, plan):
    seq_size = lax.axis_size("seq")
    head_size = lax.axis_size("head")
    query_len = queries.shape[0]
    held = queries.shape[1] // HD
    early = held * EARLY // 16
    chips = seq_size // 2
    assert query_len == BLK and plan.shape[0] == held * head_size and chips & (chips - 1) == 0
    widths = (max(1, held // GROUP) * HD, -(-early // GROUP) * HD)

    kv, early_queries = pl.pallas_call(
        functools.partial(pick_kernel, head_size, held, early, widths),
        out_shape=[
            jax.ShapeDtypeStruct((query_len, 2 * sum(widths)), jnp.bfloat16),
            jax.ShapeDtypeStruct((query_len, early * HD), jnp.bfloat16),
        ],
        in_specs=[ANY] * 3,
        out_specs=[VMEM] * 2,
        scratch_shapes=[pltpu.SemaphoreType.DMA((5,))],
        compiler_params=pltpu.CompilerParams(vmem_limit_bytes=SMALL),
        name="pick",
    )(*in_hbm(keys, values, queries))
    far_queries = lax.ppermute(early_queries, "head", [(i, i ^ (head_size // 2)) for i in range(head_size)])

    levels = capacity_levels(head_size, held)
    send, slots, level, bits = pl.pallas_call(
        functools.partial(route_kernel, head_size, held, early, levels),
        out_shape=[
            jax.ShapeDtypeStruct((held + early + 1,), jnp.int32),
            jax.ShapeDtypeStruct((head_size * held + head_size,), jnp.int32),
            jax.ShapeDtypeStruct((1,), jnp.int32),
            jax.ShapeDtypeStruct((2, vertical.shape[0]), jnp.int32),
        ],
        in_specs=[ANY] * 3,
        out_specs=[SMEM] * 3 + [VMEM],
        scratch_shapes=[
            pltpu.SMEM(plan.shape, plan.dtype),
            pltpu.VMEM((2,) + vertical.shape[::-1], vertical.dtype),
            pltpu.SemaphoreType.DMA((3,)),
        ],
        compiler_params=pltpu.CompilerParams(vmem_limit_bytes=SMALL),
        name="route",
    )(*in_hbm(plan, vertical.T, slash.T))

    pieces = [kv]
    for m in range(1, chips):
        pieces.append(lax.ppermute(kv, "seq", [(i, i ^ (2 * m)) for i in range(seq_size)]))
    pieces, far_queries, send, slots, level, bits = lax.optimization_barrier(
        (pieces, far_queries, send, slots, level, bits)
    )
    kv_own = jnp.concatenate(pieces, axis=0)
    kv_other = lax.ppermute(kv_own, "seq", [(i, i ^ 1) for i in range(seq_size)])

    packed = pl.pallas_call(
        functools.partial(attention_kernel, seq_size, head_size, held, widths),
        out_shape=jax.ShapeDtypeStruct((head_size * held + 1, query_len, HD), jnp.bfloat16),
        in_specs=[ANY] + [VMEM] * 5,
        out_specs=VMEM,
        scratch_shapes=[pltpu.SMEM(send.shape, send.dtype), pltpu.SemaphoreType.DMA],
        compiler_params=pltpu.CompilerParams(vmem_limit_bytes=40 * 1024 * 1024),
        name="attention",
    )(send, bits, kv_own, kv_other, queries, far_queries)

    return lax.switch(
        level[0],
        [functools.partial(exchange, head_size, held, capacities) for capacities in levels],
        packed,
        slots,
    )


def solution(mesh):
    in_specs = (P("seq", "head"), P("seq", None), P("seq", None), P(), P(), P())
    out_specs = P("seq", "head")
    return jax.shard_map(
        per_device, mesh=mesh, in_specs=in_specs, out_specs=out_specs, check_vma=False
    )
```

```python
import functools
import math

import jax
import jax.numpy as jnp
from jax import lax
from jax.experimental import pallas as pl
from jax.experimental.pallas import tpu as pltpu
from jax.sharding import PartitionSpec as P

HD = 128
QH = 64
KVH = 8
BLK = 64
GROUP = QH // KVH
HEADS_AT_ONCE = 4
LANES = 128

floor_value = -1e30

SMEM = pl.BlockSpec(memory_space=pltpu.SMEM)
VMEM = pl.BlockSpec(memory_space=pltpu.VMEM)
ANY = pl.BlockSpec(memory_space=pl.ANY)
SMALL = 1024 * 1024


def shift_of(size):
    assert size & (size - 1) == 0
    return size.bit_length() - 1


def entry_bits(table):
    bits = jnp.zeros((1, table.shape[1]), jnp.int32)
    for entry in range(table.shape[0]):
        named = table[entry : entry + 1, :]
        bits = bits | jnp.where(named >= 0, jnp.int32(1) << jnp.maximum(named, 0), 0)
    return bits


class Tally:
    def __init__(self, head_size, held):
        self.width = shift_of(held) + 1
        self.per_word = 31 // self.width
        self.words = [jnp.int32(0)] * -(-head_size // self.per_word)

    def rank_and_count(self, owner):
        if len(self.words) == 1:
            at = owner * self.width
            rank = self.words[0] >> at
            self.words[0] = self.words[0] + (jnp.int32(1) << at)
        else:
            word = owner // self.per_word
            at = (owner - word * self.per_word) * self.width
            held_word = self.words[0]
            for index in range(1, len(self.words)):
                held_word = jnp.where(word == index, self.words[index], held_word)
            rank = held_word >> at
            one = jnp.int32(1) << at
            self.words = [w + jnp.where(word == index, one, 0) for index, w in enumerate(self.words)]
        return rank & ((1 << self.width) - 1)

    def count(self, owner):
        word = self.words[owner // self.per_word]
        return (word >> (owner % self.per_word * self.width)) & ((1 << self.width) - 1)


def route_kernel(head_size, held, levels, plan, vertical, slash, send, slots, level, bits):
    own = lax.axis_index("head")
    most = [jnp.int32(0)] * head_size
    for target in range(head_size):
        tally = Tally(head_size, held)
        for t in range(held):
            head = plan[target * held + t]
            owner = head >> shift_of(held)
            rank = tally.rank_and_count(owner)
            send[jnp.where(owner == own, head & (held - 1), held)] = ((owner ^ target) << shift_of(held)) + rank
        for owner in range(head_size):
            most[owner ^ target] = jnp.maximum(most[owner ^ target], tally.count(owner))
    tally = Tally(head_size, held)
    for distance in range(head_size):
        slots[head_size * held + distance] = 0
    for t in range(held):
        owner = plan[own * held + t] >> shift_of(held)
        rank = tally.rank_and_count(owner)
        distance = owner ^ own
        slots[(distance << shift_of(held)) + rank] = t
        slots[head_size * held + distance] = rank + 1
    chosen = jnp.int32(len(levels) - 1)
    for index in reversed(range(len(levels) - 1)):
        fits = most[1] <= levels[index][1]
        for distance in range(2, head_size):
            fits = fits & (most[distance] <= levels[index][distance])
        chosen = jnp.where(fits, index, chosen)
    level[0] = chosen
    bits[0:1, :] = entry_bits(vertical)
    bits[1:2, :] = entry_bits(slash)


def attention_kernel(
    seq_size, held, kv_heads, send, bits, kv_own, kv_other, query_ref, out_ref, send_here, copied
):
    send_copy = pltpu.make_async_copy(send, send_here, copied)
    send_copy.start()
    query_len = query_ref.shape[0]
    key_len = query_len
    own_seq = lax.axis_index("seq")
    own_head = lax.axis_index("head")
    chips = seq_size // 2
    half = chips * key_len

    piece = lax.broadcasted_iota(jnp.int32, (1, 2 * half), 1) // key_len
    core = jnp.where(piece < chips, own_seq & 1, 1 - (own_seq & 1))
    block = ((own_seq >> 1) ^ (piece & (chips - 1))) * 2 + core
    back = own_seq - block
    present = back >= 0
    back_shift = jnp.maximum(back, 0)
    heads = own_head * held + lax.broadcasted_iota(jnp.int32, (held, bits.shape[1]), 0)
    is_head = lax.broadcasted_iota(jnp.int32, (held, bits.shape[1]), 1) == heads
    vertical_bits, slash_bits = (
        jnp.sum(jnp.where(is_head, bits[kind : kind + 1, :], 0), axis=1, keepdims=True) for kind in range(2)
    )
    hit = ((vertical_bits >> block) | (slash_bits >> back_shift)) & 1
    bias = jnp.where((hit == 1) & present, 0.0, floor_value)
    row = lax.broadcasted_iota(jnp.int32, (query_len, LANES), 0)
    column = lax.broadcasted_iota(jnp.int32, (query_len, LANES), 1)
    causal = (column <= row) | (column >= key_len)
    score_scale = HD ** (-0.5) * math.log2(math.e)
    per_kv = held // kv_heads

    def scores_of(lead):
        heads = range(lead, min(lead + HEADS_AT_ONCE, held))
        key_at = lead // per_kv * HD
        key = jnp.concatenate([kv_own[:, key_at : key_at + HD], kv_other[:, key_at : key_at + HD]], axis=0)
        query = jnp.concatenate([query_ref[:, i * HD : (i + 1) * HD] for i in heads], axis=0)
        return lax.dot_general(
            query, key, (((1,), (1,)), ((), ())), preferred_element_type=jnp.float32
        )

    following = scores_of(0)
    for lead in range(0, held, HEADS_AT_ONCE):
        heads = range(lead, min(lead + HEADS_AT_ONCE, held))
        scores = following
        if lead + HEADS_AT_ONCE < held:
            following = scores_of(lead + HEADS_AT_ONCE)
        value_at = (lead // per_kv + kv_heads) * HD
        value = jnp.concatenate(
            [kv_own[:, value_at : value_at + HD], kv_other[:, value_at : value_at + HD]], axis=0
        )
        weights = []
        totals = []
        for at, i in enumerate(heads):
            masked = scores[at * query_len : (at + 1) * query_len] + bias[i : i + 1, :]
            masked = jnp.concatenate(
                [jnp.where(causal, masked[:, :LANES], floor_value), masked[:, LANES:]], axis=1
            )
            row_max = jnp.max(masked, axis=1, keepdims=True)
            weight = jnp.exp2((masked - row_max) * score_scale)
            totals.append(1.0 / jnp.sum(weight, axis=1, keepdims=True))
            weights.append(weight.astype(jnp.bfloat16))
        mixture = jnp.dot(
            jnp.concatenate(weights, axis=0), value, preferred_element_type=jnp.float32
        )
        if lead == 0:
            send_copy.wait()
        for at, i in enumerate(heads):
            mix = mixture[at * query_len : (at + 1) * query_len]
            out_ref[send_here[i]] = (mix * totals[at]).astype(out_ref.dtype)


def place_kernel(head_size, held, sources, slots, *refs):
    out_ref, done = refs[-2:]
    for (distance, capacity), ref in zip(sources, refs):
        arriving = slots[head_size * held + distance]
        for rank in range(capacity):

            @pl.when(rank < arriving)
            def _(ref=ref, rank=rank, distance=distance):
                at = pl.multiple_of(slots[distance * held + rank] * HD, HD)
                pltpu.make_async_copy(ref.at[rank], out_ref.at[:, pl.ds(at, HD)], done).start()

    pltpu.make_async_copy(out_ref, out_ref, done).wait()


def capacity_levels(head_size, held):
    fars = [(b, c) for b in (4, 5, 6, 7) for c in (4, 5, 6, 7) if abs(b - c) <= 2] + [(8, 8)]
    shapes = [(near, b, c) for near in (6, 9) for b, c in fars] + [(11, 11, 11)]
    shapes.sort(key=lambda shape: (2 * (shape[1] + shape[2]), sum(shape)))
    shapes = [tuple(max(1, held * part // 16) for part in shape) for shape in shapes]
    levels = []
    for near, *far in shapes + [(held,) * 3]:
        level = tuple(near if m < head_size // 2 else far[m % 2] for m in range(head_size))
        if level not in levels:
            levels.append(level)
    return levels


def exchange(head_size, held, capacities, packed, slots):
    order = sorted(range(1, head_size), key=lambda m: (m >= head_size // 2, -m))
    arrived = [
        lax.ppermute(
            packed[m * held : m * held + capacities[m]], "head", [(i, i ^ m) for i in range(head_size)]
        )
        for m in order
    ]
    return pl.pallas_call(
        functools.partial(place_kernel, head_size, held, [(0, held)] + [(m, capacities[m]) for m in order]),
        out_shape=pltpu.HBM((packed.shape[1], held * HD), packed.dtype),
        in_specs=[SMEM] + [ANY] * head_size,
        out_specs=pl.BlockSpec(memory_space=pltpu.HBM),
        scratch_shapes=[pltpu.SemaphoreType.DMA],
        compiler_params=pltpu.CompilerParams(vmem_limit_bytes=SMALL),
        name="place",
    )(slots, packed, *arrived)


def per_device(queries, keys, values, vertical, slash, plan):
    seq_size = lax.axis_size("seq")
    head_size = lax.axis_size("head")
    query_len = queries.shape[0]
    held = queries.shape[1] // HD
    kv_heads = max(1, held // GROUP)
    chips = seq_size // 2
    assert query_len == BLK and plan.shape[0] == held * head_size and chips & (chips - 1) == 0

    levels = capacity_levels(head_size, held)
    send, slots, level, bits = pl.pallas_call(
        functools.partial(route_kernel, head_size, held, levels),
        out_shape=[
            jax.ShapeDtypeStruct((held + 1,), jnp.int32),
            jax.ShapeDtypeStruct((head_size * held + head_size,), jnp.int32),
            jax.ShapeDtypeStruct((1,), jnp.int32),
            jax.ShapeDtypeStruct((2, vertical.shape[0]), jnp.int32),
        ],
        in_specs=[SMEM, VMEM, VMEM],
        out_specs=[SMEM] * 3 + [VMEM],
        compiler_params=pltpu.CompilerParams(vmem_limit_bytes=SMALL),
        name="route",
    )(plan, vertical.T, slash.T)

    kv_at = lax.axis_index("head") * held // GROUP * HD
    kv = jnp.concatenate(
        [lax.dynamic_slice_in_dim(rows, kv_at, kv_heads * HD, axis=1) for rows in (keys, values)], axis=1
    )
    pieces = [kv]
    for m in range(1, chips):
        pairs = [(i, i ^ (2 * m)) for i in range(seq_size)]
        pieces.append(lax.ppermute(kv, "seq", pairs))
    pieces, send, slots, level, bits = lax.optimization_barrier((pieces, send, slots, level, bits))
    kv_own = jnp.concatenate(pieces, axis=0)
    kv_other = lax.ppermute(kv_own, "seq", [(i, i ^ 1) for i in range(seq_size)])

    packed = pl.pallas_call(
        functools.partial(attention_kernel, seq_size, held, kv_heads),
        out_shape=jax.ShapeDtypeStruct((head_size * held, query_len, HD), jnp.bfloat16),
        in_specs=[ANY] + [VMEM] * 4,
        out_specs=VMEM,
        scratch_shapes=[pltpu.SMEM(send.shape, send.dtype), pltpu.SemaphoreType.DMA],
        compiler_params=pltpu.CompilerParams(vmem_limit_bytes=40 * 1024 * 1024),
        name="attention",
    )(send, bits, kv_own, kv_other, queries)

    return lax.switch(
        level[0],
        [functools.partial(exchange, head_size, held, capacities) for capacities in levels],
        packed,
        slots,
    )


def solution(mesh):
    in_specs = (P("seq", "head"), P("seq", None), P("seq", None), P(), P(), P())
    out_specs = P("seq", "head")
    return jax.shard_map(
        per_device, mesh=mesh, in_specs=in_specs, out_specs=out_specs, check_vma=False
    )
```

```python
import functools
import math

import jax
import jax.numpy as jnp
from jax import lax
from jax.experimental import pallas as pl
from jax.experimental.pallas import tpu as pltpu
from jax.sharding import PartitionSpec as P

HD = 128
QH = 64
KVH = 8
BLK = 64
GROUP = QH // KVH
HEADS_AT_ONCE = 4
LANES = 128

floor_value = -1e30

SMEM = pl.BlockSpec(memory_space=pltpu.SMEM)
VMEM = pl.BlockSpec(memory_space=pltpu.VMEM)
ANY = pl.BlockSpec(memory_space=pl.ANY)
SMALL = 1024 * 1024


def shift_of(size):
    assert size & (size - 1) == 0
    return size.bit_length() - 1


def entry_bits(table):
    bits = jnp.zeros((1, table.shape[1]), jnp.int32)
    for entry in range(table.shape[0]):
        named = table[entry : entry + 1, :]
        bits = bits | jnp.where(named >= 0, jnp.int32(1) << jnp.maximum(named, 0), 0)
    return bits


class Tally:
    def __init__(self, head_size, held):
        self.width = shift_of(held) + 1
        self.per_word = 31 // self.width
        self.words = [jnp.int32(0)] * -(-head_size // self.per_word)

    def rank_and_count(self, owner):
        if len(self.words) == 1:
            at = owner * self.width
            rank = self.words[0] >> at
            self.words[0] = self.words[0] + (jnp.int32(1) << at)
        else:
            word = owner // self.per_word
            at = (owner - word * self.per_word) * self.width
            held_word = self.words[0]
            for index in range(1, len(self.words)):
                held_word = jnp.where(word == index, self.words[index], held_word)
            rank = held_word >> at
            one = jnp.int32(1) << at
            self.words = [w + jnp.where(word == index, one, 0) for index, w in enumerate(self.words)]
        return rank & ((1 << self.width) - 1)

    def count(self, owner):
        word = self.words[owner // self.per_word]
        return (word >> (owner % self.per_word * self.width)) & ((1 << self.width) - 1)


def route_kernel(head_size, held, levels, plan, vertical, slash, send, slots, level, bits):
    own = lax.axis_index("head")
    most = [jnp.int32(0)] * head_size
    for target in range(head_size):
        tally = Tally(head_size, held)
        for t in range(held):
            head = plan[target * held + t]
            owner = head >> shift_of(held)
            rank = tally.rank_and_count(owner)
            send[jnp.where(owner == own, head & (held - 1), held)] = ((owner ^ target) << shift_of(held)) + rank
        for owner in range(head_size):
            most[owner ^ target] = jnp.maximum(most[owner ^ target], tally.count(owner))
    tally = Tally(head_size, held)
    for distance in range(head_size):
        slots[head_size * held + distance] = 0
    for t in range(held):
        owner = plan[own * held + t] >> shift_of(held)
        rank = tally.rank_and_count(owner)
        distance = owner ^ own
        slots[(distance << shift_of(held)) + rank] = t
        slots[head_size * held + distance] = rank + 1
    chosen = jnp.int32(len(levels) - 1)
    for index in reversed(range(len(levels) - 1)):
        fits = most[1] <= levels[index][1]
        for distance in range(2, head_size):
            fits = fits & (most[distance] <= levels[index][distance])
        chosen = jnp.where(fits, index, chosen)
    level[0] = chosen
    bits[0:1, :] = entry_bits(vertical)
    bits[1:2, :] = entry_bits(slash)


def attention_kernel(
    seq_size, held, kv_heads, send, bits, kv_own, kv_other, query_ref, out_ref, send_here, copied
):
    send_copy = pltpu.make_async_copy(send, send_here, copied)
    send_copy.start()
    own_seq = lax.axis_index("seq")
    rest = (send_copy, bits, kv_own, kv_other, query_ref, out_ref, send_here)

    @pl.when(own_seq < 2)
    def _():
        attend(1, held, kv_heads, *rest)

    @pl.when(own_seq >= 2)
    def _():
        attend(seq_size // 2, held, kv_heads, *rest)


def attend(chips, held, kv_heads, send_copy, bits, kv_own, kv_other, query_ref, out_ref, send_here):
    query_len = query_ref.shape[0]
    key_len = query_len
    own_seq = lax.axis_index("seq")
    own_head = lax.axis_index("head")
    half = chips * key_len

    piece = lax.broadcasted_iota(jnp.int32, (1, 2 * half), 1) // key_len
    core = jnp.where(piece < chips, own_seq & 1, 1 - (own_seq & 1))
    block = ((own_seq >> 1) ^ (piece & (chips - 1))) * 2 + core
    back = own_seq - block
    present = back >= 0
    back_shift = jnp.maximum(back, 0)
    heads = own_head * held + lax.broadcasted_iota(jnp.int32, (held, bits.shape[1]), 0)
    is_head = lax.broadcasted_iota(jnp.int32, (held, bits.shape[1]), 1) == heads
    vertical_bits, slash_bits = (
        jnp.sum(jnp.where(is_head, bits[kind : kind + 1, :], 0), axis=1, keepdims=True) for kind in range(2)
    )
    hit = ((vertical_bits >> block) | (slash_bits >> back_shift)) & 1
    bias = jnp.where((hit == 1) & present, 0.0, floor_value)
    row = lax.broadcasted_iota(jnp.int32, (query_len, LANES), 0)
    column = lax.broadcasted_iota(jnp.int32, (query_len, LANES), 1)
    causal = (column <= row) | (column >= key_len)
    score_scale = HD ** (-0.5) * math.log2(math.e)
    per_kv = held // kv_heads

    def scores_of(lead):
        heads = range(lead, min(lead + HEADS_AT_ONCE, held))
        key_at = lead // per_kv * HD
        key = jnp.concatenate([ref[:half, key_at : key_at + HD] for ref in (kv_own, kv_other)], axis=0)
        query = jnp.concatenate([query_ref[:, i * HD : (i + 1) * HD] for i in heads], axis=0)
        return lax.dot_general(
            query, key, (((1,), (1,)), ((), ())), preferred_element_type=jnp.float32
        )

    following = scores_of(0)
    for lead in range(0, held, HEADS_AT_ONCE):
        heads = range(lead, min(lead + HEADS_AT_ONCE, held))
        scores = following
        if lead + HEADS_AT_ONCE < held:
            following = scores_of(lead + HEADS_AT_ONCE)
        value_at = (lead // per_kv + kv_heads) * HD
        value = jnp.concatenate([ref[:half, value_at : value_at + HD] for ref in (kv_own, kv_other)], axis=0)
        weights = []
        totals = []
        for at, i in enumerate(heads):
            masked = scores[at * query_len : (at + 1) * query_len] + bias[i : i + 1, :]
            own_block = jnp.where(causal, masked[:, :LANES], floor_value)
            masked = own_block if 2 * half == LANES else jnp.concatenate([own_block, masked[:, LANES:]], axis=1)
            row_max = jnp.max(masked, axis=1, keepdims=True)
            weight = jnp.exp2((masked - row_max) * score_scale)
            totals.append(1.0 / jnp.sum(weight, axis=1, keepdims=True))
            weights.append(weight.astype(jnp.bfloat16))
        mixture = jnp.dot(
            jnp.concatenate(weights, axis=0), value, preferred_element_type=jnp.float32
        )
        if lead == 0:
            send_copy.wait()
        for at, i in enumerate(heads):
            mix = mixture[at * query_len : (at + 1) * query_len]
            out_ref[send_here[i]] = (mix * totals[at]).astype(out_ref.dtype)


def place_kernel(head_size, held, sources, slots, *refs):
    out_ref, done = refs[-2:]
    for (distance, capacity), ref in zip(sources, refs):
        arriving = slots[head_size * held + distance]
        for rank in range(capacity):

            @pl.when(rank < arriving)
            def _(ref=ref, rank=rank, distance=distance):
                at = pl.multiple_of(slots[distance * held + rank] * HD, HD)
                pltpu.make_async_copy(ref.at[rank], out_ref.at[:, pl.ds(at, HD)], done).start()

    pltpu.make_async_copy(out_ref, out_ref, done).wait()


def capacity_levels(head_size, held):
    fars = [(b, c) for b in (4, 5, 6, 7) for c in (4, 5, 6, 7) if abs(b - c) <= 2] + [(8, 8)]
    shapes = [(near, b, c) for near in (6, 9) for b, c in fars] + [(11, 11, 11)]
    shapes.sort(key=lambda shape: (2 * (shape[1] + shape[2]), sum(shape)))
    shapes = [tuple(max(1, held * part // 16) for part in shape) for shape in shapes]
    levels = []
    for near, *far in shapes + [(held,) * 3]:
        level = tuple(near if m < head_size // 2 else far[m % 2] for m in range(head_size))
        if level not in levels:
            levels.append(level)
    return levels


def exchange(head_size, held, capacities, packed, slots):
    order = sorted(range(1, head_size), key=lambda m: (m >= head_size // 2, -m))
    arrived = [
        lax.ppermute(
            packed[m * held : m * held + capacities[m]], "head", [(i, i ^ m) for i in range(head_size)]
        )
        for m in order
    ]
    return pl.pallas_call(
        functools.partial(place_kernel, head_size, held, [(0, held)] + [(m, capacities[m]) for m in order]),
        out_shape=pltpu.HBM((packed.shape[1], held * HD), packed.dtype),
        in_specs=[SMEM] + [ANY] * head_size,
        out_specs=pl.BlockSpec(memory_space=pltpu.HBM),
        scratch_shapes=[pltpu.SemaphoreType.DMA],
        compiler_params=pltpu.CompilerParams(vmem_limit_bytes=SMALL),
        name="place",
    )(slots, packed, *arrived)


def per_device(queries, keys, values, vertical, slash, plan):
    seq_size = lax.axis_size("seq")
    head_size = lax.axis_size("head")
    query_len = queries.shape[0]
    held = queries.shape[1] // HD
    kv_heads = max(1, held // GROUP)
    chips = seq_size // 2
    assert query_len == BLK and plan.shape[0] == held * head_size and chips & (chips - 1) == 0

    levels = capacity_levels(head_size, held)
    send, slots, level, bits = pl.pallas_call(
        functools.partial(route_kernel, head_size, held, levels),
        out_shape=[
            jax.ShapeDtypeStruct((held + 1,), jnp.int32),
            jax.ShapeDtypeStruct((head_size * held + head_size,), jnp.int32),
            jax.ShapeDtypeStruct((1,), jnp.int32),
            jax.ShapeDtypeStruct((2, vertical.shape[0]), jnp.int32),
        ],
        in_specs=[SMEM, VMEM, VMEM],
        out_specs=[SMEM] * 3 + [VMEM],
        compiler_params=pltpu.CompilerParams(vmem_limit_bytes=SMALL),
        name="route",
    )(plan, vertical.T, slash.T)

    kv_at = lax.axis_index("head") * held // GROUP * HD
    kv = jnp.concatenate(
        [lax.dynamic_slice_in_dim(rows, kv_at, kv_heads * HD, axis=1) for rows in (keys, values)], axis=1
    )
    pieces = [kv]
    for m in range(1, chips):
        pairs = [(i, i ^ (2 * m)) for i in range(seq_size)]
        pieces.append(lax.ppermute(kv, "seq", pairs))
    pieces, send, slots, level, bits = lax.optimization_barrier((pieces, send, slots, level, bits))
    kv_own = jnp.concatenate(pieces, axis=0)
    kv_other = lax.ppermute(kv_own, "seq", [(i, i ^ 1) for i in range(seq_size)])

    packed = pl.pallas_call(
        functools.partial(attention_kernel, seq_size, held, kv_heads),
        out_shape=jax.ShapeDtypeStruct((head_size * held, query_len, HD), jnp.bfloat16),
        in_specs=[ANY] + [VMEM] * 4,
        out_specs=VMEM,
        scratch_shapes=[pltpu.SMEM(send.shape, send.dtype), pltpu.SemaphoreType.DMA],
        compiler_params=pltpu.CompilerParams(vmem_limit_bytes=40 * 1024 * 1024),
        name="attention",
    )(send, bits, kv_own, kv_other, queries)

    return lax.switch(
        level[0],
        [functools.partial(exchange, head_size, held, capacities) for capacities in levels],
        packed,
        slots,
    )


def solution(mesh):
    in_specs = (P("seq", "head"), P("seq", None), P("seq", None), P(), P(), P())
    out_specs = P("seq", "head")
    return jax.shard_map(
        per_device, mesh=mesh, in_specs=in_specs, out_specs=out_specs, check_vma=False
    )
```

```python
import functools
import math

import jax
import jax.numpy as jnp
from jax import lax
from jax.experimental import pallas as pl
from jax.experimental.pallas import tpu as pltpu
from jax.sharding import PartitionSpec as P

HD = 128
QH = 64
KVH = 8
BLK = 64
GROUP = QH // KVH
HEADS_AT_ONCE = 4
LANES = 128

floor_value = -1e30

SMEM = pl.BlockSpec(memory_space=pltpu.SMEM)
VMEM = pl.BlockSpec(memory_space=pltpu.VMEM)
ANY = pl.BlockSpec(memory_space=pl.ANY)
SMALL = 1024 * 1024


def shift_of(size):
    assert size & (size - 1) == 0
    return size.bit_length() - 1


def entry_bits(table):
    bits = jnp.zeros((1, table.shape[1]), jnp.int32)
    for entry in range(table.shape[0]):
        named = table[entry : entry + 1, :]
        bits = bits | jnp.where(named >= 0, jnp.int32(1) << jnp.maximum(named, 0), 0)
    return bits


class Tally:
    def __init__(self, head_size, held):
        self.width = shift_of(held) + 1
        self.per_word = 31 // self.width
        self.words = [jnp.int32(0)] * -(-head_size // self.per_word)

    def rank_and_count(self, owner):
        if len(self.words) == 1:
            at = owner * self.width
            rank = self.words[0] >> at
            self.words[0] = self.words[0] + (jnp.int32(1) << at)
        else:
            word = owner // self.per_word
            at = (owner - word * self.per_word) * self.width
            held_word = self.words[0]
            for index in range(1, len(self.words)):
                held_word = jnp.where(word == index, self.words[index], held_word)
            rank = held_word >> at
            one = jnp.int32(1) << at
            self.words = [w + jnp.where(word == index, one, 0) for index, w in enumerate(self.words)]
        return rank & ((1 << self.width) - 1)

    def count(self, owner):
        word = self.words[owner // self.per_word]
        return (word >> (owner % self.per_word * self.width)) & ((1 << self.width) - 1)


def route_kernel(head_size, held, levels, plan, vertical, slash, send, slots, level, bits):
    own = lax.axis_index("head")
    most = [jnp.int32(0)] * head_size
    for target in range(head_size):
        tally = Tally(head_size, held)
        for t in range(held):
            head = plan[target * held + t]
            owner = head >> shift_of(held)
            rank = tally.rank_and_count(owner)
            send[jnp.where(owner == own, head & (held - 1), held)] = ((owner ^ target) << shift_of(held)) + rank
        for owner in range(head_size):
            most[owner ^ target] = jnp.maximum(most[owner ^ target], tally.count(owner))
    tally = Tally(head_size, held)
    for distance in range(head_size):
        slots[head_size * held + distance] = 0
    for t in range(held):
        owner = plan[own * held + t] >> shift_of(held)
        rank = tally.rank_and_count(owner)
        distance = owner ^ own
        slots[(distance << shift_of(held)) + rank] = t
        slots[head_size * held + distance] = rank + 1
    chosen = jnp.int32(len(levels) - 1)
    for index in reversed(range(len(levels) - 1)):
        fits = most[1] <= levels[index][1]
        for distance in range(2, head_size):
            fits = fits & (most[distance] <= levels[index][distance])
        chosen = jnp.where(fits, index, chosen)
    level[0] = chosen
    bits[0:1, :] = entry_bits(vertical)
    bits[1:2, :] = entry_bits(slash)


def attention_kernel(
    seq_size, held, kv_heads, send, bits, kv_own, kv_other, query_ref, out_ref, send_here, copied
):
    send_copy = pltpu.make_async_copy(send, send_here, copied)
    send_copy.start()
    own_seq = lax.axis_index("seq")
    rest = (send_copy, bits, kv_own, kv_other, query_ref, out_ref, send_here)

    @pl.when(own_seq < 2)
    def _():
        attend(1, held, kv_heads, *rest)

    @pl.when(own_seq >= 2)
    def _():
        attend(seq_size // 2, held, kv_heads, *rest)


def attend(chips, held, kv_heads, send_copy, bits, kv_own, kv_other, query_ref, out_ref, send_here):
    query_len = query_ref.shape[0]
    key_len = query_len
    own_seq = lax.axis_index("seq")
    own_head = lax.axis_index("head")
    half = chips * key_len

    piece = lax.broadcasted_iota(jnp.int32, (1, 2 * half), 1) // key_len
    core = jnp.where(piece < chips, own_seq & 1, 1 - (own_seq & 1))
    block = ((own_seq >> 1) ^ (piece & (chips - 1))) * 2 + core
    back = own_seq - block
    present = back >= 0
    back_shift = jnp.maximum(back, 0)
    heads = own_head * held + lax.broadcasted_iota(jnp.int32, (held, bits.shape[1]), 0)
    is_head = lax.broadcasted_iota(jnp.int32, (held, bits.shape[1]), 1) == heads
    vertical_bits, slash_bits = (
        jnp.sum(jnp.where(is_head, bits[kind : kind + 1, :], 0), axis=1, keepdims=True) for kind in range(2)
    )
    hit = ((vertical_bits >> block) | (slash_bits >> back_shift)) & 1
    bias = jnp.where((hit == 1) & present, 0.0, floor_value)
    row = lax.broadcasted_iota(jnp.int32, (query_len, LANES), 0)
    column = lax.broadcasted_iota(jnp.int32, (query_len, LANES), 1)
    causal = (column <= row) | (column >= key_len)
    score_scale = HD ** (-0.5) * math.log2(math.e)
    per_kv = held // kv_heads

    def scores_of(lead):
        heads = range(lead, min(lead + HEADS_AT_ONCE, held))
        key_at = lead // per_kv * HD
        key = jnp.concatenate([ref[:half, key_at : key_at + HD] for ref in (kv_own, kv_other)], axis=0)
        query = jnp.concatenate([query_ref[:, i * HD : (i + 1) * HD] for i in heads], axis=0)
        return lax.dot_general(
            query, key, (((1,), (1,)), ((), ())), preferred_element_type=jnp.float32
        )

    following = scores_of(0)
    for lead in range(0, held, HEADS_AT_ONCE):
        heads = range(lead, min(lead + HEADS_AT_ONCE, held))
        scores = following
        if lead + HEADS_AT_ONCE < held:
            following = scores_of(lead + HEADS_AT_ONCE)
        value_at = (lead // per_kv + kv_heads) * HD
        value = jnp.concatenate([ref[:half, value_at : value_at + HD] for ref in (kv_own, kv_other)], axis=0)
        weights = []
        totals = []
        for at, i in enumerate(heads):
            masked = scores[at * query_len : (at + 1) * query_len] + bias[i : i + 1, :]
            own_block = jnp.where(causal, masked[:, :LANES], floor_value)
            masked = own_block if 2 * half == LANES else jnp.concatenate([own_block, masked[:, LANES:]], axis=1)
            row_max = jnp.max(masked, axis=1, keepdims=True)
            weight = jnp.exp2((masked - row_max) * score_scale)
            totals.append(1.0 / jnp.sum(weight, axis=1, keepdims=True))
            weights.append(weight.astype(jnp.bfloat16))
        mixture = jnp.dot(
            jnp.concatenate(weights, axis=0), value, preferred_element_type=jnp.float32
        )
        if lead == 0:
            send_copy.wait()
        for at, i in enumerate(heads):
            mix = mixture[at * query_len : (at + 1) * query_len]
            out_ref[send_here[i]] = (mix * totals[at]).astype(out_ref.dtype)


def place_kernel(head_size, held, sources, slots, *refs):
    out_ref, done = refs[-2:]
    for (distance, capacity), ref in zip(sources, refs):
        arriving = slots[head_size * held + distance]
        for rank in range(capacity):

            @pl.when(rank < arriving)
            def _(ref=ref, rank=rank, distance=distance):
                at = pl.multiple_of(slots[distance * held + rank] * HD, HD)
                pltpu.make_async_copy(ref.at[rank], out_ref.at[:, pl.ds(at, HD)], done).start()

    pltpu.make_async_copy(out_ref, out_ref, done).wait()


SHAPES = (
    (8, 4, 4), (6, 5, 4), (7, 4, 5), (9, 4, 5), (9, 5, 4), (6, 4, 6), (6, 5, 5), (7, 6, 4), (8, 5, 5),
    (6, 6, 5), (7, 5, 6), (7, 6, 5), (8, 4, 7), (8, 7, 4), (6, 6, 6), (7, 5, 7), (7, 7, 5), (8, 6, 6),
    (9, 7, 5), (7, 6, 7), (7, 7, 6), (11, 6, 6), (8, 8, 5), (9, 5, 8), (8, 8, 6), (9, 5, 9), (9, 9, 5),
    (9, 7, 7), (8, 7, 8), (8, 8, 7), (11, 10, 5), (9, 7, 9), (9, 9, 7), (11, 8, 8), (11, 10, 10),
)


def capacity_levels(head_size, held):
    shapes = sorted(SHAPES, key=lambda shape: max(2 * (shape[1] + shape[2]), sum(shape)))
    shapes = [tuple(max(1, held * part // 16) for part in shape) for shape in shapes]
    levels = []
    for near, *far in shapes + [(held,) * 3]:
        level = tuple(near if m < head_size // 2 else far[m % 2] for m in range(head_size))
        if level not in levels:
            levels.append(level)
    return levels


def exchange(head_size, held, capacities, packed, slots):
    order = range(head_size - 1, 0, -1)
    arrived = [
        lax.ppermute(
            packed[m * held : m * held + capacities[m]], "head", [(i, i ^ m) for i in range(head_size)]
        )
        for m in order
    ]
    return pl.pallas_call(
        functools.partial(place_kernel, head_size, held, [(0, held)] + [(m, capacities[m]) for m in order]),
        out_shape=pltpu.HBM((packed.shape[1], held * HD), packed.dtype),
        in_specs=[SMEM] + [ANY] * head_size,
        out_specs=pl.BlockSpec(memory_space=pltpu.HBM),
        scratch_shapes=[pltpu.SemaphoreType.DMA],
        compiler_params=pltpu.CompilerParams(vmem_limit_bytes=SMALL),
        name="place",
    )(slots, packed, *arrived)


def per_device(queries, keys, values, vertical, slash, plan):
    seq_size = lax.axis_size("seq")
    head_size = lax.axis_size("head")
    query_len = queries.shape[0]
    held = queries.shape[1] // HD
    kv_heads = max(1, held // GROUP)
    chips = seq_size // 2
    assert query_len == BLK and plan.shape[0] == held * head_size and chips & (chips - 1) == 0

    levels = capacity_levels(head_size, held)
    send, slots, level, bits = pl.pallas_call(
        functools.partial(route_kernel, head_size, held, levels),
        out_shape=[
            jax.ShapeDtypeStruct((held + 1,), jnp.int32),
            jax.ShapeDtypeStruct((head_size * held + head_size,), jnp.int32),
            jax.ShapeDtypeStruct((1,), jnp.int32),
            jax.ShapeDtypeStruct((2, vertical.shape[0]), jnp.int32),
        ],
        in_specs=[SMEM, VMEM, VMEM],
        out_specs=[SMEM] * 3 + [VMEM],
        compiler_params=pltpu.CompilerParams(vmem_limit_bytes=SMALL),
        name="route",
    )(plan, vertical.T, slash.T)

    kv_at = lax.axis_index("head") * held // GROUP * HD
    kv = jnp.concatenate(
        [lax.dynamic_slice_in_dim(rows, kv_at, kv_heads * HD, axis=1) for rows in (keys, values)], axis=1
    )
    pieces = [kv]
    for m in range(1, chips):
        pairs = [(i, i ^ (2 * m)) for i in range(seq_size)]
        pieces.append(lax.ppermute(kv, "seq", pairs))
    pieces, send, slots, level, bits = lax.optimization_barrier((pieces, send, slots, level, bits))
    kv_own = jnp.concatenate(pieces, axis=0)
    kv_other = lax.ppermute(kv_own, "seq", [(i, i ^ 1) for i in range(seq_size)])

    packed = pl.pallas_call(
        functools.partial(attention_kernel, seq_size, held, kv_heads),
        out_shape=jax.ShapeDtypeStruct((head_size * held, query_len, HD), jnp.bfloat16),
        in_specs=[ANY] + [VMEM] * 4,
        out_specs=VMEM,
        scratch_shapes=[pltpu.SMEM(send.shape, send.dtype), pltpu.SemaphoreType.DMA],
        compiler_params=pltpu.CompilerParams(vmem_limit_bytes=40 * 1024 * 1024),
        name="attention",
    )(send, bits, kv_own, kv_other, queries)

    return lax.switch(
        level[0],
        [functools.partial(exchange, head_size, held, capacities) for capacities in levels],
        packed,
        slots,
    )


def solution(mesh):
    in_specs = (P("seq", "head"), P("seq", None), P("seq", None), P(), P(), P())
    out_specs = P("seq", "head")
    return jax.shard_map(
        per_device, mesh=mesh, in_specs=in_specs, out_specs=out_specs, check_vma=False
    )
```

```python
import functools
import math

import jax
import jax.numpy as jnp
from jax import lax
from jax.experimental import pallas as pl
from jax.experimental.pallas import tpu as pltpu
from jax.sharding import PartitionSpec as P

HD = 128
QH = 64
KVH = 8
BLK = 64
GROUP = QH // KVH
HEADS_AT_ONCE = 4
LANES = 128

floor_value = -1e30

SMEM = pl.BlockSpec(memory_space=pltpu.SMEM)
VMEM = pl.BlockSpec(memory_space=pltpu.VMEM)
ANY = pl.BlockSpec(memory_space=pl.ANY)
SMALL = 1024 * 1024


def shift_of(size):
    assert size & (size - 1) == 0
    return size.bit_length() - 1


def entry_bits(table):
    bits = jnp.zeros((1, table.shape[1]), jnp.int32)
    for entry in range(table.shape[0]):
        named = table[entry : entry + 1, :]
        bits = bits | jnp.where(named >= 0, jnp.int32(1) << jnp.maximum(named, 0), 0)
    return bits


class Tally:
    def __init__(self, head_size, held):
        self.width = shift_of(held) + 1
        self.per_word = 31 // self.width
        self.words = [jnp.int32(0)] * -(-head_size // self.per_word)

    def rank_and_count(self, owner):
        if len(self.words) == 1:
            at = owner * self.width
            rank = self.words[0] >> at
            self.words[0] = self.words[0] + (jnp.int32(1) << at)
        else:
            word = owner // self.per_word
            at = (owner - word * self.per_word) * self.width
            held_word = self.words[0]
            for index in range(1, len(self.words)):
                held_word = jnp.where(word == index, self.words[index], held_word)
            rank = held_word >> at
            one = jnp.int32(1) << at
            self.words = [w + jnp.where(word == index, one, 0) for index, w in enumerate(self.words)]
        return rank & ((1 << self.width) - 1)

    def count(self, owner):
        word = self.words[owner // self.per_word]
        return (word >> (owner % self.per_word * self.width)) & ((1 << self.width) - 1)


def route_kernel(head_size, held, levels, plan, vertical, slash, send, slots, level, bits):
    own = lax.axis_index("head")
    most = [jnp.int32(0)] * head_size
    for target in range(head_size):
        tally = Tally(head_size, held)
        for t in range(held):
            head = plan[target * held + t]
            owner = head >> shift_of(held)
            rank = tally.rank_and_count(owner)
            send[jnp.where(owner == own, head & (held - 1), held)] = ((owner ^ target) << shift_of(held)) + rank
        for owner in range(head_size):
            most[owner ^ target] = jnp.maximum(most[owner ^ target], tally.count(owner))
    tally = Tally(head_size, held)
    for distance in range(head_size):
        slots[head_size * held + distance] = 0
    for t in range(held):
        owner = plan[own * held + t] >> shift_of(held)
        rank = tally.rank_and_count(owner)
        distance = owner ^ own
        slots[(distance << shift_of(held)) + rank] = t
        slots[head_size * held + distance] = rank + 1
    chosen = jnp.int32(len(levels) - 1)
    for index in reversed(range(len(levels) - 1)):
        fits = most[1] <= levels[index][1]
        for distance in range(2, head_size):
            fits = fits & (most[distance] <= levels[index][distance])
        chosen = jnp.where(fits, index, chosen)
    level[0] = chosen
    bits[0:1, :] = entry_bits(vertical)
    bits[1:2, :] = entry_bits(slash)


def attention_kernel(
    seq_size, held, kv_heads, send, bits, kv_own, kv_other, query_ref, out_ref, send_here, copied
):
    send_copy = pltpu.make_async_copy(send, send_here, copied)
    send_copy.start()
    own_seq = lax.axis_index("seq")
    rest = (send_copy, bits, kv_own, kv_other, query_ref, out_ref, send_here)

    @pl.when(own_seq < 2)
    def _():
        attend(1, held, kv_heads, *rest)

    @pl.when(own_seq >= 2)
    def _():
        attend(seq_size // 2, held, kv_heads, *rest)


def attend(chips, held, kv_heads, send_copy, bits, kv_own, kv_other, query_ref, out_ref, send_here):
    query_len = query_ref.shape[0]
    key_len = query_len
    own_seq = lax.axis_index("seq")
    own_head = lax.axis_index("head")
    half = chips * key_len

    piece = lax.broadcasted_iota(jnp.int32, (1, 2 * half), 1) // key_len
    core = jnp.where(piece < chips, own_seq & 1, 1 - (own_seq & 1))
    block = ((own_seq >> 1) ^ (piece & (chips - 1))) * 2 + core
    back = own_seq - block
    present = back >= 0
    back_shift = jnp.maximum(back, 0)
    heads = own_head * held + lax.broadcasted_iota(jnp.int32, (held, bits.shape[1]), 0)
    is_head = lax.broadcasted_iota(jnp.int32, (held, bits.shape[1]), 1) == heads
    vertical_bits, slash_bits = (
        jnp.sum(jnp.where(is_head, bits[kind : kind + 1, :], 0), axis=1, keepdims=True) for kind in range(2)
    )
    hit = ((vertical_bits >> block) | (slash_bits >> back_shift)) & 1
    bias = jnp.where((hit == 1) & present, 0.0, floor_value)
    row = lax.broadcasted_iota(jnp.int32, (query_len, LANES), 0)
    column = lax.broadcasted_iota(jnp.int32, (query_len, LANES), 1)
    causal = (column <= row) | (column >= key_len)
    score_scale = HD ** (-0.5) * math.log2(math.e)
    per_kv = held // kv_heads

    def scores_of(lead):
        heads = range(lead, min(lead + HEADS_AT_ONCE, held))
        key_at = lead // per_kv * HD
        key = jnp.concatenate([ref[:half, key_at : key_at + HD] for ref in (kv_own, kv_other)], axis=0)
        query = jnp.concatenate([query_ref[:, i * HD : (i + 1) * HD] for i in heads], axis=0)
        return lax.dot_general(
            query, key, (((1,), (1,)), ((), ())), preferred_element_type=jnp.float32
        )

    following = scores_of(0)
    for lead in range(0, held, HEADS_AT_ONCE):
        heads = range(lead, min(lead + HEADS_AT_ONCE, held))
        scores = following
        if lead + HEADS_AT_ONCE < held:
            following = scores_of(lead + HEADS_AT_ONCE)
        value_at = (lead // per_kv + kv_heads) * HD
        value = jnp.concatenate([ref[:half, value_at : value_at + HD] for ref in (kv_own, kv_other)], axis=0)
        weights = []
        totals = []
        for at, i in enumerate(heads):
            masked = scores[at * query_len : (at + 1) * query_len] + bias[i : i + 1, :]
            own_block = jnp.where(causal, masked[:, :LANES], floor_value)
            masked = own_block if 2 * half == LANES else jnp.concatenate([own_block, masked[:, LANES:]], axis=1)
            row_max = jnp.max(masked, axis=1, keepdims=True)
            weight = jnp.exp2((masked - row_max) * score_scale)
            totals.append(1.0 / jnp.sum(weight, axis=1, keepdims=True))
            weights.append(weight.astype(jnp.bfloat16))
        mixture = jnp.dot(
            jnp.concatenate(weights, axis=0), value, preferred_element_type=jnp.float32
        )
        if lead == 0:
            send_copy.wait()
        for at, i in enumerate(heads):
            mix = mixture[at * query_len : (at + 1) * query_len]
            out_ref[send_here[i]] = (mix * totals[at]).astype(out_ref.dtype)


def place_kernel(head_size, held, sources, slots, *refs):
    out_ref, done = refs[-2:]
    for (distance, capacity), ref in zip(sources, refs):
        arriving = slots[head_size * held + distance]
        for rank in range(capacity):

            @pl.when(rank < arriving)
            def _(ref=ref, rank=rank, distance=distance):
                at = pl.multiple_of(slots[distance * held + rank] * HD, HD)
                pltpu.make_async_copy(ref.at[rank], out_ref.at[:, pl.ds(at, HD)], done).start()

    pltpu.make_async_copy(out_ref, out_ref, done).wait()


SHAPES = (
    (8, 4, 4), (4, 5, 4), (5, 4, 5), (7, 5, 4), (4, 6, 4), (5, 5, 5), (6, 4, 6), (6, 5, 5), (7, 6, 4), (8, 5, 5),
    (5, 6, 5), (6, 5, 6), (6, 7, 4), (7, 4, 7), (8, 6, 5), (9, 7, 4), (5, 7, 5), (6, 6, 6), (7, 5, 7), (7, 8, 4),
    (8, 7, 5), (8, 4, 8), (9, 6, 6), (5, 8, 5), (6, 7, 6), (7, 6, 7), (8, 5, 8), (6, 8, 6), (7, 7, 7), (7, 6, 8),
    (9, 7, 7), (11, 9, 5), (7, 8, 7), (7, 6, 9), (8, 8, 8), (7, 10, 7), (9, 9, 9), (11, 10, 10),
)


def capacity_levels(head_size, held):
    shapes = [tuple(max(1, held * part // 16) for part in shape) for shape in SHAPES]
    levels = []
    for near, *far in shapes + [(held,) * 3]:
        level = tuple(near if m < head_size // 2 else far[m % 2] for m in range(head_size))
        if level not in levels:
            levels.append(level)
    return levels


def exchange(head_size, held, capacities, packed, slots):
    order = sorted(range(1, head_size), key=lambda m: (m >= head_size // 2, -m))
    arrived = [
        lax.ppermute(
            packed[m * held : m * held + capacities[m]], "head", [(i, i ^ m) for i in range(head_size)]
        )
        for m in order
    ]
    return pl.pallas_call(
        functools.partial(place_kernel, head_size, held, [(0, held)] + [(m, capacities[m]) for m in order]),
        out_shape=pltpu.HBM((packed.shape[1], held * HD), packed.dtype),
        in_specs=[SMEM] + [ANY] * head_size,
        out_specs=pl.BlockSpec(memory_space=pltpu.HBM),
        scratch_shapes=[pltpu.SemaphoreType.DMA],
        compiler_params=pltpu.CompilerParams(vmem_limit_bytes=SMALL),
        name="place",
    )(slots, packed, *arrived)


def per_device(queries, keys, values, vertical, slash, plan):
    seq_size = lax.axis_size("seq")
    head_size = lax.axis_size("head")
    query_len = queries.shape[0]
    held = queries.shape[1] // HD
    kv_heads = max(1, held // GROUP)
    chips = seq_size // 2
    assert query_len == BLK and plan.shape[0] == held * head_size and chips & (chips - 1) == 0

    levels = capacity_levels(head_size, held)
    send, slots, level, bits = pl.pallas_call(
        functools.partial(route_kernel, head_size, held, levels),
        out_shape=[
            jax.ShapeDtypeStruct((held + 1,), jnp.int32),
            jax.ShapeDtypeStruct((head_size * held + head_size,), jnp.int32),
            jax.ShapeDtypeStruct((1,), jnp.int32),
            jax.ShapeDtypeStruct((2, vertical.shape[0]), jnp.int32),
        ],
        in_specs=[SMEM, VMEM, VMEM],
        out_specs=[SMEM] * 3 + [VMEM],
        compiler_params=pltpu.CompilerParams(vmem_limit_bytes=SMALL),
        name="route",
    )(plan, vertical.T, slash.T)

    kv_at = lax.axis_index("head") * held // GROUP * HD
    kv = jnp.concatenate(
        [lax.dynamic_slice_in_dim(rows, kv_at, kv_heads * HD, axis=1) for rows in (keys, values)], axis=1
    )
    pieces = [kv]
    for m in range(1, chips):
        pairs = [(i, i ^ (2 * m)) for i in range(seq_size)]
        pieces.append(lax.ppermute(kv, "seq", pairs))
    pieces, send, slots, level, bits = lax.optimization_barrier((pieces, send, slots, level, bits))
    kv_own = jnp.concatenate(pieces, axis=0)
    kv_other = lax.ppermute(kv_own, "seq", [(i, i ^ 1) for i in range(seq_size)])

    packed = pl.pallas_call(
        functools.partial(attention_kernel, seq_size, held, kv_heads),
        out_shape=jax.ShapeDtypeStruct((head_size * held, query_len, HD), jnp.bfloat16),
        in_specs=[ANY] + [VMEM] * 4,
        out_specs=VMEM,
        scratch_shapes=[pltpu.SMEM(send.shape, send.dtype), pltpu.SemaphoreType.DMA],
        compiler_params=pltpu.CompilerParams(vmem_limit_bytes=40 * 1024 * 1024),
        name="attention",
    )(send, bits, kv_own, kv_other, queries)

    return lax.switch(
        level[0],
        [functools.partial(exchange, head_size, held, capacities) for capacities in levels],
        packed,
        slots,
    )


def solution(mesh):
    in_specs = (P("seq", "head"), P("seq", None), P("seq", None), P(), P(), P())
    out_specs = P("seq", "head")
    return jax.shard_map(
        per_device, mesh=mesh, in_specs=in_specs, out_specs=out_specs, check_vma=False
    )
```

```python
import functools
import math

import jax
import jax.numpy as jnp
from jax import lax
from jax.experimental import pallas as pl
from jax.experimental.pallas import tpu as pltpu
from jax.sharding import PartitionSpec as P

HD = 128
QH = 64
KVH = 8
BLK = 64
GROUP = QH // KVH
HEADS_AT_ONCE = 4
LANES = 128

floor_value = -1e30

SMEM = pl.BlockSpec(memory_space=pltpu.SMEM)
VMEM = pl.BlockSpec(memory_space=pltpu.VMEM)
ANY = pl.BlockSpec(memory_space=pl.ANY)
SMALL = 1024 * 1024


def shift_of(size):
    assert size & (size - 1) == 0
    return size.bit_length() - 1


def piece_flips(chips):
    if chips == 4:
        return (0, 2, 3, 1), (0, 1, 3, 2)
    return (tuple(range(chips)),) * 2


def entry_bits(table):
    bits = jnp.zeros((1, table.shape[1]), jnp.int32)
    for entry in range(table.shape[0]):
        named = table[entry : entry + 1, :]
        bits = bits | jnp.where(named >= 0, jnp.int32(1) << jnp.maximum(named, 0), 0)
    return bits


class Tally:
    def __init__(self, head_size, held):
        self.width = shift_of(held) + 1
        self.per_word = 31 // self.width
        self.words = [jnp.int32(0)] * -(-head_size // self.per_word)

    def rank_and_count(self, owner):
        if len(self.words) == 1:
            at = owner * self.width
            rank = self.words[0] >> at
            self.words[0] = self.words[0] + (jnp.int32(1) << at)
        else:
            word = owner // self.per_word
            at = (owner - word * self.per_word) * self.width
            held_word = self.words[0]
            for index in range(1, len(self.words)):
                held_word = jnp.where(word == index, self.words[index], held_word)
            rank = held_word >> at
            one = jnp.int32(1) << at
            self.words = [w + jnp.where(word == index, one, 0) for index, w in enumerate(self.words)]
        return rank & ((1 << self.width) - 1)

    def count(self, owner):
        word = self.words[owner // self.per_word]
        return (word >> (owner % self.per_word * self.width)) & ((1 << self.width) - 1)


def route_kernel(head_size, held, levels, plan, vertical, slash, send, slots, level, bits):
    own = lax.axis_index("head")
    most = [jnp.int32(0)] * head_size
    for target in range(head_size):
        tally = Tally(head_size, held)
        for t in range(held):
            head = plan[target * held + t]
            owner = head >> shift_of(held)
            rank = tally.rank_and_count(owner)
            send[jnp.where(owner == own, head & (held - 1), held)] = ((owner ^ target) << shift_of(held)) + rank
        for owner in range(head_size):
            most[owner ^ target] = jnp.maximum(most[owner ^ target], tally.count(owner))
    tally = Tally(head_size, held)
    for distance in range(head_size):
        slots[head_size * held + distance] = 0
    for t in range(held):
        owner = plan[own * held + t] >> shift_of(held)
        rank = tally.rank_and_count(owner)
        distance = owner ^ own
        slots[(distance << shift_of(held)) + rank] = t
        slots[head_size * held + distance] = rank + 1
    chosen = jnp.int32(len(levels) - 1)
    for index in reversed(range(len(levels) - 1)):
        fits = most[1] <= levels[index][1]
        for distance in range(2, head_size):
            fits = fits & (most[distance] <= levels[index][distance])
        chosen = jnp.where(fits, index, chosen)
    level[0] = chosen
    bits[0:1, :] = entry_bits(vertical)
    bits[1:2, :] = entry_bits(slash)


def attention_kernel(
    seq_size, held, kv_heads, send, bits, kv_own, kv_other, query_ref, out_ref, send_here, copied
):
    send_copy = pltpu.make_async_copy(send, send_here, copied)
    send_copy.start()
    own_seq = lax.axis_index("seq")
    rest = (send_copy, bits, kv_own, kv_other, query_ref, out_ref, send_here)

    @pl.when(own_seq < 2)
    def _():
        attend(((0,), (0,)), held, kv_heads, *rest)

    @pl.when(own_seq >= 2)
    def _():
        attend(piece_flips(seq_size // 2), held, kv_heads, *rest)


def attend(flips, held, kv_heads, send_copy, bits, kv_own, kv_other, query_ref, out_ref, send_here):
    chips = len(flips[0])
    query_len = query_ref.shape[0]
    key_len = query_len
    own_seq = lax.axis_index("seq")
    own_head = lax.axis_index("head")
    half = chips * key_len

    piece = lax.broadcasted_iota(jnp.int32, (1, 2 * half), 1) // key_len
    core = jnp.where(piece < chips, own_seq & 1, 1 - (own_seq & 1))
    flip = jnp.zeros_like(piece)
    for p, (even, odd) in enumerate(zip(*flips)):
        flip = jnp.where(piece & (chips - 1) == p, jnp.where(core == 0, even, odd), flip)
    block = ((own_seq >> 1) ^ flip) * 2 + core
    back = own_seq - block
    present = back >= 0
    back_shift = jnp.maximum(back, 0)
    heads = own_head * held + lax.broadcasted_iota(jnp.int32, (held, bits.shape[1]), 0)
    is_head = lax.broadcasted_iota(jnp.int32, (held, bits.shape[1]), 1) == heads
    vertical_bits, slash_bits = (
        jnp.sum(jnp.where(is_head, bits[kind : kind + 1, :], 0), axis=1, keepdims=True) for kind in range(2)
    )
    hit = ((vertical_bits >> block) | (slash_bits >> back_shift)) & 1
    bias = jnp.where((hit == 1) & present, 0.0, floor_value)
    row = lax.broadcasted_iota(jnp.int32, (query_len, LANES), 0)
    column = lax.broadcasted_iota(jnp.int32, (query_len, LANES), 1)
    causal = (column <= row) | (column >= key_len)
    score_scale = HD ** (-0.5) * math.log2(math.e)
    per_kv = held // kv_heads

    def scores_of(lead):
        heads = range(lead, min(lead + HEADS_AT_ONCE, held))
        key_at = lead // per_kv * HD
        key = jnp.concatenate([ref[:half, key_at : key_at + HD] for ref in (kv_own, kv_other)], axis=0)
        query = jnp.concatenate([query_ref[:, i * HD : (i + 1) * HD] for i in heads], axis=0)
        return lax.dot_general(
            query, key, (((1,), (1,)), ((), ())), preferred_element_type=jnp.float32
        )

    following = scores_of(0)
    for lead in range(0, held, HEADS_AT_ONCE):
        heads = range(lead, min(lead + HEADS_AT_ONCE, held))
        scores = following
        if lead + HEADS_AT_ONCE < held:
            following = scores_of(lead + HEADS_AT_ONCE)
        value_at = (lead // per_kv + kv_heads) * HD
        value = jnp.concatenate([ref[:half, value_at : value_at + HD] for ref in (kv_own, kv_other)], axis=0)
        weights = []
        totals = []
        for at, i in enumerate(heads):
            masked = scores[at * query_len : (at + 1) * query_len] + bias[i : i + 1, :]
            own_block = jnp.where(causal, masked[:, :LANES], floor_value)
            masked = own_block if 2 * half == LANES else jnp.concatenate([own_block, masked[:, LANES:]], axis=1)
            row_max = jnp.max(masked, axis=1, keepdims=True)
            weight = jnp.exp2((masked - row_max) * score_scale)
            totals.append(1.0 / jnp.sum(weight, axis=1, keepdims=True))
            weights.append(weight.astype(jnp.bfloat16))
        mixture = jnp.dot(
            jnp.concatenate(weights, axis=0), value, preferred_element_type=jnp.float32
        )
        if lead == 0:
            send_copy.wait()
        for at, i in enumerate(heads):
            mix = mixture[at * query_len : (at + 1) * query_len]
            out_ref[send_here[i]] = (mix * totals[at]).astype(out_ref.dtype)


def place_kernel(head_size, held, sources, slots, *refs):
    out_ref, done = refs[-2:]
    for (distance, capacity), ref in zip(sources, refs):
        arriving = slots[head_size * held + distance]
        for rank in range(capacity):

            @pl.when(rank < arriving)
            def _(ref=ref, rank=rank, distance=distance):
                at = pl.multiple_of(slots[distance * held + rank] * HD, HD)
                pltpu.make_async_copy(ref.at[rank], out_ref.at[:, pl.ds(at, HD)], done).start()

    pltpu.make_async_copy(out_ref, out_ref, done).wait()


SHAPES = (
    (8, 4, 4), (4, 5, 4), (5, 4, 5), (7, 5, 4), (4, 6, 4), (5, 5, 5), (6, 4, 6), (6, 5, 5), (7, 6, 4), (8, 5, 5),
    (5, 6, 5), (6, 5, 6), (6, 7, 4), (7, 4, 7), (8, 6, 5), (9, 7, 4), (5, 7, 5), (6, 6, 6), (7, 5, 7), (7, 8, 4),
    (8, 7, 5), (8, 4, 8), (9, 6, 6), (5, 8, 5), (6, 7, 6), (7, 6, 7), (8, 5, 8), (6, 8, 6), (7, 7, 7), (7, 6, 8),
    (9, 7, 7), (11, 9, 5), (7, 8, 7), (7, 6, 9), (8, 8, 8), (7, 10, 7), (9, 9, 9), (11, 10, 10),
)


def capacity_levels(head_size, held):
    shapes = [tuple(max(1, held * part // 16) for part in shape) for shape in SHAPES]
    levels = []
    for near, *far in shapes + [(held,) * 3]:
        level = tuple(near if m < head_size // 2 else far[m % 2] for m in range(head_size))
        if level not in levels:
            levels.append(level)
    return levels


def exchange(head_size, held, capacities, packed, slots):
    order = sorted(range(1, head_size), key=lambda m: (m >= head_size // 2, -m))
    arrived = [
        lax.ppermute(
            packed[m * held : m * held + capacities[m]], "head", [(i, i ^ m) for i in range(head_size)]
        )
        for m in order
    ]
    return pl.pallas_call(
        functools.partial(place_kernel, head_size, held, [(0, held)] + [(m, capacities[m]) for m in order]),
        out_shape=pltpu.HBM((packed.shape[1], held * HD), packed.dtype),
        in_specs=[SMEM] + [ANY] * head_size,
        out_specs=pl.BlockSpec(memory_space=pltpu.HBM),
        scratch_shapes=[pltpu.SemaphoreType.DMA],
        compiler_params=pltpu.CompilerParams(vmem_limit_bytes=SMALL),
        name="place",
    )(slots, packed, *arrived)


def per_device(queries, keys, values, vertical, slash, plan):
    seq_size = lax.axis_size("seq")
    head_size = lax.axis_size("head")
    query_len = queries.shape[0]
    held = queries.shape[1] // HD
    kv_heads = max(1, held // GROUP)
    chips = seq_size // 2
    assert query_len == BLK and plan.shape[0] == held * head_size and chips & (chips - 1) == 0

    levels = capacity_levels(head_size, held)
    send, slots, level, bits = pl.pallas_call(
        functools.partial(route_kernel, head_size, held, levels),
        out_shape=[
            jax.ShapeDtypeStruct((held + 1,), jnp.int32),
            jax.ShapeDtypeStruct((head_size * held + head_size,), jnp.int32),
            jax.ShapeDtypeStruct((1,), jnp.int32),
            jax.ShapeDtypeStruct((2, vertical.shape[0]), jnp.int32),
        ],
        in_specs=[SMEM, VMEM, VMEM],
        out_specs=[SMEM] * 3 + [VMEM],
        compiler_params=pltpu.CompilerParams(vmem_limit_bytes=SMALL),
        name="route",
    )(plan, vertical.T, slash.T)

    kv_at = lax.axis_index("head") * held // GROUP * HD
    kv = jnp.concatenate(
        [lax.dynamic_slice_in_dim(rows, kv_at, kv_heads * HD, axis=1) for rows in (keys, values)], axis=1
    )
    pieces = [kv]
    flips = piece_flips(chips)
    for p in range(1, chips):
        pairs = [(i, i ^ (2 * flips[i & 1][p])) for i in range(seq_size)]
        pieces.append(lax.ppermute(kv, "seq", pairs))
    pieces, send, slots, level, bits = lax.optimization_barrier((pieces, send, slots, level, bits))
    kv_own = jnp.concatenate(pieces, axis=0)
    kv_other = lax.ppermute(kv_own, "seq", [(i, i ^ 1) for i in range(seq_size)])

    packed = pl.pallas_call(
        functools.partial(attention_kernel, seq_size, held, kv_heads),
        out_shape=jax.ShapeDtypeStruct((head_size * held, query_len, HD), jnp.bfloat16),
        in_specs=[ANY] + [VMEM] * 4,
        out_specs=VMEM,
        scratch_shapes=[pltpu.SMEM(send.shape, send.dtype), pltpu.SemaphoreType.DMA],
        compiler_params=pltpu.CompilerParams(vmem_limit_bytes=40 * 1024 * 1024),
        name="attention",
    )(send, bits, kv_own, kv_other, queries)

    return lax.switch(
        level[0],
        [functools.partial(exchange, head_size, held, capacities) for capacities in levels],
        packed,
        slots,
    )


def solution(mesh):
    in_specs = (P("seq", "head"), P("seq", None), P("seq", None), P(), P(), P())
    out_specs = P("seq", "head")
    return jax.shard_map(
        per_device, mesh=mesh, in_specs=in_specs, out_specs=out_specs, check_vma=False
    )
```

```python
import functools
import math

import jax
import jax.numpy as jnp
from jax import lax
from jax.experimental import pallas as pl
from jax.experimental.pallas import tpu as pltpu
from jax.sharding import PartitionSpec as P

HD = 128
QH = 64
KVH = 8
BLK = 64
GROUP = QH // KVH
HEADS_AT_ONCE = 4
LANES = 128

floor_value = -1e30

SMEM = pl.BlockSpec(memory_space=pltpu.SMEM)
VMEM = pl.BlockSpec(memory_space=pltpu.VMEM)
ANY = pl.BlockSpec(memory_space=pl.ANY)
SMALL = 1024 * 1024


def shift_of(size):
    assert size & (size - 1) == 0
    return size.bit_length() - 1


def entry_bits(table):
    bits = jnp.zeros((1, table.shape[1]), jnp.int32)
    for entry in range(table.shape[0]):
        named = table[entry : entry + 1, :]
        bits = bits | jnp.where(named >= 0, jnp.int32(1) << jnp.maximum(named, 0), 0)
    return bits


class Tally:
    def __init__(self, head_size, held):
        self.width = shift_of(held) + 1
        self.per_word = 31 // self.width
        self.words = [jnp.int32(0)] * -(-head_size // self.per_word)

    def rank_and_count(self, owner):
        if len(self.words) == 1:
            at = owner * self.width
            rank = self.words[0] >> at
            self.words[0] = self.words[0] + (jnp.int32(1) << at)
        else:
            word = owner // self.per_word
            at = (owner - word * self.per_word) * self.width
            held_word = self.words[0]
            for index in range(1, len(self.words)):
                held_word = jnp.where(word == index, self.words[index], held_word)
            rank = held_word >> at
            one = jnp.int32(1) << at
            self.words = [w + jnp.where(word == index, one, 0) for index, w in enumerate(self.words)]
        return rank & ((1 << self.width) - 1)

    def count(self, owner):
        word = self.words[owner // self.per_word]
        return (word >> (owner % self.per_word * self.width)) & ((1 << self.width) - 1)


def route_kernel(head_size, held, levels, plan, vertical, slash, send, slots, level, bits):
    own = lax.axis_index("head")
    most = [jnp.int32(0)] * head_size
    for target in range(head_size):
        tally = Tally(head_size, held)
        for t in range(held):
            head = plan[target * held + t]
            owner = head >> shift_of(held)
            rank = tally.rank_and_count(owner)
            send[jnp.where(owner == own, head & (held - 1), held)] = ((owner ^ target) << shift_of(held)) + rank
        for owner in range(head_size):
            most[owner ^ target] = jnp.maximum(most[owner ^ target], tally.count(owner))
    tally = Tally(head_size, held)
    for distance in range(head_size):
        slots[head_size * held + distance] = 0
    for t in range(held):
        owner = plan[own * held + t] >> shift_of(held)
        rank = tally.rank_and_count(owner)
        distance = owner ^ own
        slots[(distance << shift_of(held)) + rank] = t
        slots[head_size * held + distance] = rank + 1
    chosen = jnp.int32(len(levels) - 1)
    for index in reversed(range(len(levels) - 1)):
        fits = most[1] <= levels[index][1]
        for distance in range(2, head_size):
            fits = fits & (most[distance] <= levels[index][distance])
        chosen = jnp.where(fits, index, chosen)
    level[0] = chosen
    bits[0:1, :] = entry_bits(vertical)
    bits[1:2, :] = entry_bits(slash)


def attention_kernel(
    seq_size, held, kv_heads, send, bits, kv_own, kv_other, query_ref, out_ref, send_here, copied
):
    send_copy = pltpu.make_async_copy(send, send_here, copied)
    send_copy.start()
    own_seq = lax.axis_index("seq")
    rest = (send_copy, bits, kv_own, kv_other, query_ref, out_ref, send_here)

    @pl.when(own_seq < 2)
    def _():
        attend(1, held, kv_heads, *rest)

    @pl.when(own_seq >= 2)
    def _():
        attend(seq_size // 2, held, kv_heads, *rest)


def attend(chips, held, kv_heads, send_copy, bits, kv_own, kv_other, query_ref, out_ref, send_here):
    query_len = query_ref.shape[0]
    key_len = query_len
    own_seq = lax.axis_index("seq")
    own_head = lax.axis_index("head")
    half = chips * key_len

    piece = lax.broadcasted_iota(jnp.int32, (1, 2 * half), 1) // key_len
    core = jnp.where(piece < chips, own_seq & 1, 1 - (own_seq & 1))
    block = ((own_seq >> 1) ^ (piece & (chips - 1))) * 2 + core
    back = own_seq - block
    present = back >= 0
    back_shift = jnp.maximum(back, 0)
    heads = own_head * held + lax.broadcasted_iota(jnp.int32, (held, bits.shape[1]), 0)
    is_head = lax.broadcasted_iota(jnp.int32, (held, bits.shape[1]), 1) == heads
    vertical_bits, slash_bits = (
        jnp.sum(jnp.where(is_head, bits[kind : kind + 1, :], 0), axis=1, keepdims=True) for kind in range(2)
    )
    hit = ((vertical_bits >> block) | (slash_bits >> back_shift)) & 1
    bias = jnp.where((hit == 1) & present, 0.0, floor_value)
    row = lax.broadcasted_iota(jnp.int32, (query_len, LANES), 0)
    column = lax.broadcasted_iota(jnp.int32, (query_len, LANES), 1)
    causal = (column <= row) | (column >= key_len)
    score_scale = HD ** (-0.5) * math.log2(math.e)
    per_kv = held // kv_heads

    def scores_of(lead):
        heads = range(lead, min(lead + HEADS_AT_ONCE, held))
        key_at = lead // per_kv * HD
        key = jnp.concatenate([ref[:half, key_at : key_at + HD] for ref in (kv_own, kv_other)], axis=0)
        query = jnp.concatenate([query_ref[:, i * HD : (i + 1) * HD] for i in heads], axis=0)
        return lax.dot_general(
            query, key, (((1,), (1,)), ((), ())), preferred_element_type=jnp.float32
        )

    ready = []
    following = scores_of(0)
    for lead in range(0, held, HEADS_AT_ONCE):
        heads = range(lead, min(lead + HEADS_AT_ONCE, held))
        scores = following
        if lead + HEADS_AT_ONCE < held:
            following = scores_of(lead + HEADS_AT_ONCE)
        value_at = (lead // per_kv + kv_heads) * HD
        value = jnp.concatenate([ref[:half, value_at : value_at + HD] for ref in (kv_own, kv_other)], axis=0)
        weights = []
        totals = []
        for at, i in enumerate(heads):
            masked = scores[at * query_len : (at + 1) * query_len] + bias[i : i + 1, :]
            own_block = jnp.where(causal, masked[:, :LANES], floor_value)
            masked = own_block if 2 * half == LANES else jnp.concatenate([own_block, masked[:, LANES:]], axis=1)
            row_max = jnp.max(masked, axis=1, keepdims=True)
            weight = jnp.exp2((masked - row_max) * score_scale)
            totals.append(1.0 / jnp.sum(weight, axis=1, keepdims=True))
            weights.append(weight.astype(jnp.bfloat16))
        mixture = jnp.dot(
            jnp.concatenate(weights, axis=0), value, preferred_element_type=jnp.float32
        )
        for at, i in enumerate(heads):
            mix = mixture[at * query_len : (at + 1) * query_len]
            ready.append((i, (mix * totals[at]).astype(out_ref.dtype)))
        if chips > 1 or lead + HEADS_AT_ONCE >= held:
            if chips == 1 or lead == 0:
                send_copy.wait()
            for i, rows in ready:
                out_ref[send_here[i]] = rows
            ready = []


def place_kernel(head_size, held, sources, slots, *refs):
    out_ref, done = refs[-2:]
    for (distance, capacity), ref in zip(sources, refs):
        arriving = slots[head_size * held + distance]
        for rank in range(capacity):

            @pl.when(rank < arriving)
            def _(ref=ref, rank=rank, distance=distance):
                at = pl.multiple_of(slots[distance * held + rank] * HD, HD)
                pltpu.make_async_copy(ref.at[rank], out_ref.at[:, pl.ds(at, HD)], done).start()

    pltpu.make_async_copy(out_ref, out_ref, done).wait()


SHAPES = (
    (4, 5, 4), (7, 4, 4), (4, 6, 4), (5, 5, 5), (8, 5, 4), (4, 4, 6), (4, 7, 4), (5, 6, 5), (6, 4, 6), (6, 6, 4),
    (8, 5, 5), (9, 6, 4), (4, 4, 7), (5, 5, 6), (5, 7, 5), (6, 6, 6), (7, 4, 7), (8, 7, 4), (9, 6, 5), (5, 5, 7),
    (5, 8, 5), (6, 7, 6), (7, 5, 7), (8, 4, 8), (9, 7, 5), (11, 6, 6), (6, 6, 7), (5, 9, 5), (6, 8, 6), (7, 7, 7),
    (8, 5, 8), (6, 6, 8), (7, 8, 7), (6, 6, 9), (8, 8, 8), (7, 10, 7), (9, 9, 9), (11, 10, 10),
)


def capacity_levels(head_size, held):
    shapes = [tuple(max(1, held * part // 16) for part in shape) for shape in SHAPES]
    levels = []
    for near, *far in shapes + [(held,) * 3]:
        level = tuple(near if m < head_size // 2 else far[m % 2] for m in range(head_size))
        if level not in levels:
            levels.append(level)
    return levels


def exchange(head_size, held, capacities, packed, slots):
    order = sorted(range(1, head_size), key=lambda m: (m >= head_size // 2, -m))
    arrived = [
        lax.ppermute(
            packed[m * held : m * held + capacities[m]], "head", [(i, i ^ m) for i in range(head_size)]
        )
        for m in order
    ]
    return pl.pallas_call(
        functools.partial(place_kernel, head_size, held, [(0, held)] + [(m, capacities[m]) for m in order]),
        out_shape=pltpu.HBM((packed.shape[1], held * HD), packed.dtype),
        in_specs=[SMEM] + [ANY] * head_size,
        out_specs=pl.BlockSpec(memory_space=pltpu.HBM),
        scratch_shapes=[pltpu.SemaphoreType.DMA],
        compiler_params=pltpu.CompilerParams(vmem_limit_bytes=SMALL),
        name="place",
    )(slots, packed, *arrived)


def per_device(queries, keys, values, vertical, slash, plan):
    seq_size = lax.axis_size("seq")
    head_size = lax.axis_size("head")
    query_len = queries.shape[0]
    held = queries.shape[1] // HD
    kv_heads = max(1, held // GROUP)
    chips = seq_size // 2
    assert query_len == BLK and plan.shape[0] == held * head_size and chips & (chips - 1) == 0

    levels = capacity_levels(head_size, held)
    send, slots, level, bits = pl.pallas_call(
        functools.partial(route_kernel, head_size, held, levels),
        out_shape=[
            jax.ShapeDtypeStruct((held + 1,), jnp.int32),
            jax.ShapeDtypeStruct((head_size * held + head_size,), jnp.int32),
            jax.ShapeDtypeStruct((1,), jnp.int32),
            jax.ShapeDtypeStruct((2, vertical.shape[0]), jnp.int32),
        ],
        in_specs=[SMEM, VMEM, VMEM],
        out_specs=[SMEM] * 3 + [VMEM],
        compiler_params=pltpu.CompilerParams(vmem_limit_bytes=SMALL),
        name="route",
    )(plan, vertical.T, slash.T)

    kv_at = lax.axis_index("head") * held // GROUP * HD
    kv = jnp.concatenate(
        [lax.dynamic_slice_in_dim(rows, kv_at, kv_heads * HD, axis=1) for rows in (keys, values)], axis=1
    )
    pieces = [kv]
    for m in range(1, chips):
        pairs = [(i, i ^ (2 * m)) for i in range(seq_size)]
        pieces.append(lax.ppermute(kv, "seq", pairs))
    pieces, send, slots, level, bits = lax.optimization_barrier((pieces, send, slots, level, bits))
    kv_own = jnp.concatenate(pieces, axis=0)
    kv_other = lax.ppermute(kv_own, "seq", [(i, i ^ 1) for i in range(seq_size)])

    packed = pl.pallas_call(
        functools.partial(attention_kernel, seq_size, held, kv_heads),
        out_shape=jax.ShapeDtypeStruct((head_size * held, query_len, HD), jnp.bfloat16),
        in_specs=[ANY] + [VMEM] * 4,
        out_specs=VMEM,
        scratch_shapes=[pltpu.SMEM(send.shape, send.dtype), pltpu.SemaphoreType.DMA],
        compiler_params=pltpu.CompilerParams(vmem_limit_bytes=40 * 1024 * 1024),
        name="attention",
    )(send, bits, kv_own, kv_other, queries)

    return lax.switch(
        level[0],
        [functools.partial(exchange, head_size, held, capacities) for capacities in levels],
        packed,
        slots,
    )


def solution(mesh):
    in_specs = (P("seq", "head"), P("seq", None), P("seq", None), P(), P(), P())
    out_specs = P("seq", "head")
    return jax.shard_map(
        per_device, mesh=mesh, in_specs=in_specs, out_specs=out_specs, check_vma=False
    )
```

```python
import functools
import math

import jax
import jax.numpy as jnp
from jax import lax
from jax.experimental import pallas as pl
from jax.experimental.pallas import tpu as pltpu
from jax.sharding import PartitionSpec as P

HD = 128
QH = 64
KVH = 8
BLK = 64
GROUP = QH // KVH
HEADS_AT_ONCE = 4
LANES = 128

floor_value = -1e30

SMEM = pl.BlockSpec(memory_space=pltpu.SMEM)
VMEM = pl.BlockSpec(memory_space=pltpu.VMEM)
ANY = pl.BlockSpec(memory_space=pl.ANY)
SMALL = 1024 * 1024


def shift_of(size):
    assert size & (size - 1) == 0
    return size.bit_length() - 1


def entry_bits(table):
    bits = jnp.zeros((1, table.shape[1]), jnp.int32)
    for entry in range(table.shape[0]):
        named = table[entry : entry + 1, :]
        bits = bits | jnp.where(named >= 0, jnp.int32(1) << jnp.maximum(named, 0), 0)
    return bits


class Tally:
    def __init__(self, head_size, held):
        self.width = shift_of(held) + 1
        self.per_word = 31 // self.width
        self.words = [jnp.int32(0)] * -(-head_size // self.per_word)

    def rank_and_count(self, owner):
        if len(self.words) == 1:
            at = owner * self.width
            rank = self.words[0] >> at
            self.words[0] = self.words[0] + (jnp.int32(1) << at)
        else:
            word = owner // self.per_word
            at = (owner - word * self.per_word) * self.width
            held_word = self.words[0]
            for index in range(1, len(self.words)):
                held_word = jnp.where(word == index, self.words[index], held_word)
            rank = held_word >> at
            one = jnp.int32(1) << at
            self.words = [w + jnp.where(word == index, one, 0) for index, w in enumerate(self.words)]
        return rank & ((1 << self.width) - 1)

    def count(self, owner):
        word = self.words[owner // self.per_word]
        return (word >> (owner % self.per_word * self.width)) & ((1 << self.width) - 1)


def route_kernel(head_size, held, levels, plan, vertical, slash, send, slots, level, bits):
    own = lax.axis_index("head")
    most = [jnp.int32(0)] * head_size
    for target in range(head_size):
        tally = Tally(head_size, held)
        for t in range(held):
            head = plan[target * held + t]
            owner = head >> shift_of(held)
            rank = tally.rank_and_count(owner)
            send[jnp.where(owner == own, head & (held - 1), held)] = ((owner ^ target) << shift_of(held)) + rank
        for owner in range(head_size):
            most[owner ^ target] = jnp.maximum(most[owner ^ target], tally.count(owner))
    tally = Tally(head_size, held)
    for distance in range(head_size):
        slots[head_size * held + distance] = 0
    for t in range(held):
        owner = plan[own * held + t] >> shift_of(held)
        rank = tally.rank_and_count(owner)
        distance = owner ^ own
        slots[(distance << shift_of(held)) + rank] = t
        slots[head_size * held + distance] = rank + 1
    chosen = jnp.int32(len(levels) - 1)
    for index in reversed(range(len(levels) - 1)):
        fits = most[1] <= levels[index][1]
        for distance in range(2, head_size):
            fits = fits & (most[distance] <= levels[index][distance])
        chosen = jnp.where(fits, index, chosen)
    level[0] = chosen
    bits[0:1, :] = entry_bits(vertical)
    bits[1:2, :] = entry_bits(slash)


def attention_kernel(
    seq_size, held, kv_heads, send, bits, kv_own, kv_other, query_ref, out_ref, send_here, copied
):
    send_copy = pltpu.make_async_copy(send, send_here, copied)
    send_copy.start()
    own_seq = lax.axis_index("seq")
    rest = (send_copy, bits, kv_own, kv_other, query_ref, out_ref, send_here)
    chips = seq_size // 2

    def pieces_of(chip):
        return tuple(m for m in range(chips) if chip ^ m <= chip)

    if chips == 4:
        cases = [((own_seq >> 1) == chip, pieces_of(chip)) for chip in range(chips)]
    else:
        cases = [(own_seq < 2, (0,)), (own_seq >= 2, tuple(range(chips)))]
    for applies, pieces in cases:

        @pl.when(applies)
        def _(pieces=pieces):
            attend(pieces, held, kv_heads, *rest)


def attend(pieces, held, kv_heads, send_copy, bits, kv_own, kv_other, query_ref, out_ref, send_here):
    query_len = query_ref.shape[0]
    key_len = query_len
    own_seq = lax.axis_index("seq")
    own_head = lax.axis_index("head")
    keys = 2 * len(pieces) * key_len

    place = lax.broadcasted_iota(jnp.int32, (1, keys), 1) // key_len
    own_core = place < len(pieces)
    place = jnp.where(own_core, place, place - len(pieces))
    piece = jnp.zeros_like(place)
    for at, m in enumerate(pieces):
        piece = jnp.where(place == at, m, piece)
    core = jnp.where(own_core, own_seq & 1, 1 - (own_seq & 1))
    block = ((own_seq >> 1) ^ piece) * 2 + core
    back = own_seq - block
    present = back >= 0
    back_shift = jnp.maximum(back, 0)
    heads = own_head * held + lax.broadcasted_iota(jnp.int32, (held, bits.shape[1]), 0)
    is_head = lax.broadcasted_iota(jnp.int32, (held, bits.shape[1]), 1) == heads
    vertical_bits, slash_bits = (
        jnp.sum(jnp.where(is_head, bits[kind : kind + 1, :], 0), axis=1, keepdims=True) for kind in range(2)
    )
    hit = ((vertical_bits >> block) | (slash_bits >> back_shift)) & 1
    bias = jnp.where((hit == 1) & present, 0.0, floor_value)
    row = lax.broadcasted_iota(jnp.int32, (query_len, LANES), 0)
    column = lax.broadcasted_iota(jnp.int32, (query_len, LANES), 1)
    causal = (column <= row) | (column >= key_len)
    score_scale = HD ** (-0.5) * math.log2(math.e)
    per_kv = held // kv_heads

    def rows_of(at):
        runs = []
        for m in pieces:
            if runs and runs[-1][1] == m:
                runs[-1][1] = m + 1
            else:
                runs.append([m, m + 1])
        return jnp.concatenate(
            [
                ref[first * key_len : last * key_len, at : at + HD]
                for ref in (kv_own, kv_other)
                for first, last in runs
            ],
            axis=0,
        )

    def scores_of(lead):
        heads = range(lead, min(lead + HEADS_AT_ONCE, held))
        key = rows_of(lead // per_kv * HD)
        query = jnp.concatenate([query_ref[:, i * HD : (i + 1) * HD] for i in heads], axis=0)
        return lax.dot_general(
            query, key, (((1,), (1,)), ((), ())), preferred_element_type=jnp.float32
        )

    ready = []
    following = scores_of(0)
    for lead in range(0, held, HEADS_AT_ONCE):
        heads = range(lead, min(lead + HEADS_AT_ONCE, held))
        scores = following
        if lead + HEADS_AT_ONCE < held:
            following = scores_of(lead + HEADS_AT_ONCE)
        value = rows_of((lead // per_kv + kv_heads) * HD)
        weights = []
        totals = []
        for at, i in enumerate(heads):
            masked = scores[at * query_len : (at + 1) * query_len] + bias[i : i + 1, :]
            own_block = jnp.where(causal, masked[:, :LANES], floor_value)
            masked = own_block if keys == LANES else jnp.concatenate([own_block, masked[:, LANES:]], axis=1)
            row_max = jnp.max(masked, axis=1, keepdims=True)
            weight = jnp.exp2((masked - row_max) * score_scale)
            totals.append(1.0 / jnp.sum(weight, axis=1, keepdims=True))
            weights.append(weight.astype(jnp.bfloat16))
        mixture = jnp.dot(
            jnp.concatenate(weights, axis=0), value, preferred_element_type=jnp.float32
        )
        for at, i in enumerate(heads):
            mix = mixture[at * query_len : (at + 1) * query_len]
            ready.append((i, (mix * totals[at]).astype(out_ref.dtype)))
        if len(pieces) > 1 or lead + HEADS_AT_ONCE >= held:
            if len(pieces) == 1 or lead == 0:
                send_copy.wait()
            for i, rows in ready:
                out_ref[send_here[i]] = rows
            ready = []


def place_kernel(head_size, held, sources, slots, *refs):
    out_ref, done = refs[-2:]
    for (distance, capacity), ref in zip(sources, refs):
        arriving = slots[head_size * held + distance]
        for rank in range(capacity):

            @pl.when(rank < arriving)
            def _(ref=ref, rank=rank, distance=distance):
                at = pl.multiple_of(slots[distance * held + rank] * HD, HD)
                pltpu.make_async_copy(ref.at[rank], out_ref.at[:, pl.ds(at, HD)], done).start()

    pltpu.make_async_copy(out_ref, out_ref, done).wait()


SHAPES = (
    (4, 5, 4), (7, 4, 4), (4, 6, 4), (5, 5, 5), (8, 5, 4), (4, 4, 6), (4, 7, 4), (5, 6, 5), (6, 4, 6), (6, 6, 4),
    (8, 5, 5), (9, 6, 4), (4, 4, 7), (5, 5, 6), (5, 7, 5), (6, 6, 6), (7, 4, 7), (8, 7, 4), (9, 6, 5), (5, 5, 7),
    (5, 8, 5), (6, 7, 6), (7, 5, 7), (8, 4, 8), (9, 7, 5), (11, 6, 6), (6, 6, 7), (5, 9, 5), (6, 8, 6), (7, 7, 7),
    (8, 5, 8), (6, 6, 8), (7, 8, 7), (6, 6, 9), (8, 8, 8), (7, 10, 7), (9, 9, 9), (11, 10, 10),
)


def capacity_levels(head_size, held):
    shapes = [tuple(max(1, held * part // 16) for part in shape) for shape in SHAPES]
    levels = []
    for near, *far in shapes + [(held,) * 3]:
        level = tuple(near if m < head_size // 2 else far[m % 2] for m in range(head_size))
        if level not in levels:
            levels.append(level)
    return levels


def exchange(head_size, held, capacities, packed, slots):
    order = sorted(range(1, head_size), key=lambda m: (m >= head_size // 2, -m))
    arrived = [
        lax.ppermute(
            packed[m * held : m * held + capacities[m]], "head", [(i, i ^ m) for i in range(head_size)]
        )
        for m in order
    ]
    return pl.pallas_call(
        functools.partial(place_kernel, head_size, held, [(0, held)] + [(m, capacities[m]) for m in order]),
        out_shape=pltpu.HBM((packed.shape[1], held * HD), packed.dtype),
        in_specs=[SMEM] + [ANY] * head_size,
        out_specs=pl.BlockSpec(memory_space=pltpu.HBM),
        scratch_shapes=[pltpu.SemaphoreType.DMA],
        compiler_params=pltpu.CompilerParams(vmem_limit_bytes=SMALL),
        name="place",
    )(slots, packed, *arrived)


def per_device(queries, keys, values, vertical, slash, plan):
    seq_size = lax.axis_size("seq")
    head_size = lax.axis_size("head")
    query_len = queries.shape[0]
    held = queries.shape[1] // HD
    kv_heads = max(1, held // GROUP)
    chips = seq_size // 2
    assert query_len == BLK and plan.shape[0] == held * head_size and chips & (chips - 1) == 0

    levels = capacity_levels(head_size, held)
    send, slots, level, bits = pl.pallas_call(
        functools.partial(route_kernel, head_size, held, levels),
        out_shape=[
            jax.ShapeDtypeStruct((held + 1,), jnp.int32),
            jax.ShapeDtypeStruct((head_size * held + head_size,), jnp.int32),
            jax.ShapeDtypeStruct((1,), jnp.int32),
            jax.ShapeDtypeStruct((2, vertical.shape[0]), jnp.int32),
        ],
        in_specs=[SMEM, VMEM, VMEM],
        out_specs=[SMEM] * 3 + [VMEM],
        compiler_params=pltpu.CompilerParams(vmem_limit_bytes=SMALL),
        name="route",
    )(plan, vertical.T, slash.T)

    kv_at = lax.axis_index("head") * held // GROUP * HD
    kv = jnp.concatenate(
        [lax.dynamic_slice_in_dim(rows, kv_at, kv_heads * HD, axis=1) for rows in (keys, values)], axis=1
    )
    pieces = [kv]
    for m in range(1, chips):
        pairs = [(i, i ^ (2 * m)) for i in range(seq_size)]
        pieces.append(lax.ppermute(kv, "seq", pairs))
    pieces, send, slots, level, bits = lax.optimization_barrier((pieces, send, slots, level, bits))
    kv_own = jnp.concatenate(pieces, axis=0)
    kv_other = lax.ppermute(kv_own, "seq", [(i, i ^ 1) for i in range(seq_size)])

    packed = pl.pallas_call(
        functools.partial(attention_kernel, seq_size, held, kv_heads),
        out_shape=jax.ShapeDtypeStruct((head_size * held, query_len, HD), jnp.bfloat16),
        in_specs=[ANY] + [VMEM] * 4,
        out_specs=VMEM,
        scratch_shapes=[pltpu.SMEM(send.shape, send.dtype), pltpu.SemaphoreType.DMA],
        compiler_params=pltpu.CompilerParams(vmem_limit_bytes=40 * 1024 * 1024),
        name="attention",
    )(send, bits, kv_own, kv_other, queries)

    return lax.switch(
        level[0],
        [functools.partial(exchange, head_size, held, capacities) for capacities in levels],
        packed,
        slots,
    )


def solution(mesh):
    in_specs = (P("seq", "head"), P("seq", None), P("seq", None), P(), P(), P())
    out_specs = P("seq", "head")
    return jax.shard_map(
        per_device, mesh=mesh, in_specs=in_specs, out_specs=out_specs, check_vma=False
    )
```

```python
import functools
import math

import jax
import jax.numpy as jnp
from jax import lax
from jax.experimental import pallas as pl
from jax.experimental.pallas import tpu as pltpu
from jax.sharding import PartitionSpec as P

HD = 128
QH = 64
KVH = 8
BLK = 64
GROUP = QH // KVH
HEADS_AT_ONCE = 4
LANES = 128

floor_value = -1e30

SMEM = pl.BlockSpec(memory_space=pltpu.SMEM)
VMEM = pl.BlockSpec(memory_space=pltpu.VMEM)
ANY = pl.BlockSpec(memory_space=pl.ANY)
SMALL = 1024 * 1024


def shift_of(size):
    assert size & (size - 1) == 0
    return size.bit_length() - 1


def entry_bits(table):
    bits = jnp.zeros((1, table.shape[1]), jnp.int32)
    for entry in range(table.shape[0]):
        named = table[entry : entry + 1, :]
        bits = bits | jnp.where(named >= 0, jnp.int32(1) << jnp.maximum(named, 0), 0)
    return bits


class Tally:
    def __init__(self, head_size, held):
        self.width = shift_of(held) + 1
        self.per_word = 31 // self.width
        self.words = [jnp.int32(0)] * -(-head_size // self.per_word)

    def rank_and_count(self, owner):
        if len(self.words) == 1:
            at = owner * self.width
            rank = self.words[0] >> at
            self.words[0] = self.words[0] + (jnp.int32(1) << at)
        else:
            word = owner // self.per_word
            at = (owner - word * self.per_word) * self.width
            held_word = self.words[0]
            for index in range(1, len(self.words)):
                held_word = jnp.where(word == index, self.words[index], held_word)
            rank = held_word >> at
            one = jnp.int32(1) << at
            self.words = [w + jnp.where(word == index, one, 0) for index, w in enumerate(self.words)]
        return rank & ((1 << self.width) - 1)

    def count(self, owner):
        word = self.words[owner // self.per_word]
        return (word >> (owner % self.per_word * self.width)) & ((1 << self.width) - 1)


def route_kernel(head_size, held, levels, plan, vertical, slash, send, slots, level, bits):
    own = lax.axis_index("head")
    most = [jnp.int32(0)] * head_size
    for target in range(head_size):
        tally = Tally(head_size, held)
        for t in range(held):
            head = plan[target * held + t]
            owner = head >> shift_of(held)
            rank = tally.rank_and_count(owner)
            send[jnp.where(owner == own, head & (held - 1), held)] = ((owner ^ target) << shift_of(held)) + rank
        for owner in range(head_size):
            most[owner ^ target] = jnp.maximum(most[owner ^ target], tally.count(owner))
    tally = Tally(head_size, held)
    for distance in range(head_size):
        slots[head_size * held + distance] = 0
    for t in range(held):
        owner = plan[own * held + t] >> shift_of(held)
        rank = tally.rank_and_count(owner)
        distance = owner ^ own
        slots[(distance << shift_of(held)) + rank] = t
        slots[head_size * held + distance] = rank + 1
    chosen = jnp.int32(len(levels) - 1)
    for index in reversed(range(len(levels) - 1)):
        fits = most[1] <= levels[index][1]
        for distance in range(2, head_size):
            fits = fits & (most[distance] <= levels[index][distance])
        chosen = jnp.where(fits, index, chosen)
    level[0] = chosen
    bits[0:1, :] = entry_bits(vertical)
    bits[1:2, :] = entry_bits(slash)


def attention_kernel(
    seq_size, held, kv_heads, send, bits, kv_own, kv_other, query_ref, out_ref, send_here, copied
):
    send_copy = pltpu.make_async_copy(send, send_here, copied)
    send_copy.start()
    own_seq = lax.axis_index("seq")
    rest = (send_copy, bits, kv_own, kv_other, query_ref, out_ref, send_here)
    chips = seq_size // 2

    def pieces_of(chip):
        return tuple(m for m in range(chips) if chip ^ m <= chip)

    if chips == 4:
        cases = [((own_seq >> 1) == chip, pieces_of(chip)) for chip in range(chips)]
    else:
        cases = [(own_seq < 2, (0,)), (own_seq >= 2, tuple(range(chips)))]
    for applies, pieces in cases:

        @pl.when(applies)
        def _(pieces=pieces):
            attend(pieces, held, kv_heads, *rest)


def attend(pieces, held, kv_heads, send_copy, bits, kv_own, kv_other, query_ref, out_ref, send_here):
    query_len = query_ref.shape[0]
    key_len = query_len
    own_seq = lax.axis_index("seq")
    own_head = lax.axis_index("head")
    keys = 2 * len(pieces) * key_len

    place = lax.broadcasted_iota(jnp.int32, (1, keys), 1) // key_len
    own_core = place < len(pieces)
    place = jnp.where(own_core, place, place - len(pieces))
    piece = jnp.zeros_like(place)
    for at, m in enumerate(pieces):
        piece = jnp.where(place == at, m, piece)
    core = jnp.where(own_core, own_seq & 1, 1 - (own_seq & 1))
    block = ((own_seq >> 1) ^ piece) * 2 + core
    back = own_seq - block
    present = back >= 0
    back_shift = jnp.maximum(back, 0)
    heads = own_head * held + lax.broadcasted_iota(jnp.int32, (held, bits.shape[1]), 0)
    is_head = lax.broadcasted_iota(jnp.int32, (held, bits.shape[1]), 1) == heads
    vertical_bits, slash_bits = (
        jnp.sum(jnp.where(is_head, bits[kind : kind + 1, :], 0), axis=1, keepdims=True) for kind in range(2)
    )
    hit = ((vertical_bits >> block) | (slash_bits >> back_shift)) & 1
    bias = jnp.where((hit == 1) & present, 0.0, floor_value)
    row = lax.broadcasted_iota(jnp.int32, (query_len, LANES), 0)
    column = lax.broadcasted_iota(jnp.int32, (query_len, LANES), 1)
    causal = (column <= row) | (column >= key_len)
    score_scale = HD ** (-0.5) * math.log2(math.e)
    per_kv = held // kv_heads

    def rows_of(at):
        runs = []
        for m in pieces:
            if runs and runs[-1][1] == m:
                runs[-1][1] = m + 1
            else:
                runs.append([m, m + 1])
        return jnp.concatenate(
            [
                ref[first * key_len : last * key_len, at : at + HD]
                for ref in (kv_own, kv_other)
                for first, last in runs
            ],
            axis=0,
        )

    def scores_of(lead):
        heads = range(lead, min(lead + HEADS_AT_ONCE, held))
        key = rows_of(lead // per_kv * HD)
        query = jnp.concatenate([query_ref[:, i * HD : (i + 1) * HD] for i in heads], axis=0)
        return lax.dot_general(
            query, key, (((1,), (1,)), ((), ())), preferred_element_type=jnp.float32
        )

    ready = []
    following = scores_of(0)
    for lead in range(0, held, HEADS_AT_ONCE):
        heads = range(lead, min(lead + HEADS_AT_ONCE, held))
        scores = following
        if lead + HEADS_AT_ONCE < held:
            following = scores_of(lead + HEADS_AT_ONCE)
        value = rows_of((lead // per_kv + kv_heads) * HD)
        weights = []
        totals = []
        for at, i in enumerate(heads):
            masked = scores[at * query_len : (at + 1) * query_len] + bias[i : i + 1, :]
            own_block = jnp.where(causal, masked[:, :LANES], floor_value)
            masked = own_block if keys == LANES else jnp.concatenate([own_block, masked[:, LANES:]], axis=1)
            row_max = jnp.max(masked, axis=1, keepdims=True)
            weight = jnp.exp2((masked - row_max) * score_scale)
            totals.append(1.0 / jnp.sum(weight, axis=1, keepdims=True))
            weights.append(weight.astype(jnp.bfloat16))
        mixture = jnp.dot(
            jnp.concatenate(weights, axis=0), value, preferred_element_type=jnp.float32
        )
        for at, i in enumerate(heads):
            mix = mixture[at * query_len : (at + 1) * query_len]
            ready.append((i, (mix * totals[at]).astype(out_ref.dtype)))
        if len(pieces) > 1 or lead + HEADS_AT_ONCE >= held:
            if len(pieces) == 1 or lead == 0:
                send_copy.wait()
            for i, rows in ready:
                out_ref[send_here[i]] = rows
            ready = []


def place_kernel(head_size, held, distances, slots, *refs):
    out_ref, slots_here, copied, done = refs[-4:]
    slots_copy = pltpu.make_async_copy(slots, slots_here, copied)
    slots_copy.start()
    slots_copy.wait()
    for distance, ref in zip(distances, refs):

        def place(rank, carry, distance=distance, ref=ref):
            at = pl.multiple_of(slots_here[distance * held + rank] * HD, HD)
            pltpu.make_async_copy(ref.at[rank], out_ref.at[:, pl.ds(at, HD)], done).start()
            return carry

        lax.fori_loop(0, slots_here[head_size * held + distance], place, 0)
    pltpu.make_async_copy(out_ref, out_ref, done).wait()


SHAPES = (
    (4, 5, 4), (7, 4, 4), (4, 6, 4), (5, 5, 5), (8, 5, 4), (4, 4, 6), (4, 7, 4), (5, 6, 5), (6, 4, 6), (6, 6, 4),
    (8, 5, 5), (9, 6, 4), (4, 4, 7), (5, 5, 6), (5, 7, 5), (6, 6, 6), (7, 4, 7), (8, 7, 4), (9, 6, 5), (5, 5, 7),
    (5, 8, 5), (6, 7, 6), (7, 5, 7), (8, 4, 8), (9, 7, 5), (11, 6, 6), (6, 6, 7), (5, 9, 5), (6, 8, 6), (7, 7, 7),
    (8, 5, 8), (6, 6, 8), (7, 8, 7), (6, 6, 9), (8, 8, 8), (7, 10, 7), (9, 9, 9), (11, 10, 10),
)


def capacity_levels(head_size, held):
    shapes = [tuple(max(1, held * part // 16) for part in shape) for shape in SHAPES]
    levels = []
    for near, *far in shapes + [(held,) * 3]:
        level = tuple(near if m < head_size // 2 else far[m % 2] for m in range(head_size))
        if level not in levels:
            levels.append(level)
    return levels


def exchange(head_size, held, capacities, packed, slots):
    order = sorted(range(1, head_size), key=lambda m: (m >= head_size // 2, -m))
    arrived = [
        lax.ppermute(
            packed[m * held : m * held + capacities[m]], "head", [(i, i ^ m) for i in range(head_size)]
        )
        for m in order
    ]
    return pl.pallas_call(
        functools.partial(place_kernel, head_size, held, [0, *order]),
        out_shape=pltpu.HBM((packed.shape[1], held * HD), packed.dtype),
        in_specs=[ANY] * (1 + head_size),
        out_specs=pl.BlockSpec(memory_space=pltpu.HBM),
        scratch_shapes=[
            pltpu.SMEM(slots.shape, slots.dtype),
            pltpu.SemaphoreType.DMA,
            pltpu.SemaphoreType.DMA,
        ],
        compiler_params=pltpu.CompilerParams(vmem_limit_bytes=SMALL),
        name="place",
    )(slots, packed, *arrived)


def per_device(queries, keys, values, vertical, slash, plan):
    seq_size = lax.axis_size("seq")
    head_size = lax.axis_size("head")
    query_len = queries.shape[0]
    held = queries.shape[1] // HD
    kv_heads = max(1, held // GROUP)
    chips = seq_size // 2
    assert query_len == BLK and plan.shape[0] == held * head_size and chips & (chips - 1) == 0

    levels = capacity_levels(head_size, held)
    send, slots, level, bits = pl.pallas_call(
        functools.partial(route_kernel, head_size, held, levels),
        out_shape=[
            jax.ShapeDtypeStruct((held + 1,), jnp.int32),
            jax.ShapeDtypeStruct((head_size * held + head_size,), jnp.int32),
            jax.ShapeDtypeStruct((1,), jnp.int32),
            jax.ShapeDtypeStruct((2, vertical.shape[0]), jnp.int32),
        ],
        in_specs=[SMEM, VMEM, VMEM],
        out_specs=[SMEM] * 3 + [VMEM],
        compiler_params=pltpu.CompilerParams(vmem_limit_bytes=SMALL),
        name="route",
    )(plan, vertical.T, slash.T)

    kv_at = lax.axis_index("head") * held // GROUP * HD
    kv = jnp.concatenate(
        [lax.dynamic_slice_in_dim(rows, kv_at, kv_heads * HD, axis=1) for rows in (keys, values)], axis=1
    )
    pieces = [kv]
    for m in range(1, chips):
        pairs = [(i, i ^ (2 * m)) for i in range(seq_size)]
        pieces.append(lax.ppermute(kv, "seq", pairs))
    pieces, send, slots, level, bits = lax.optimization_barrier((pieces, send, slots, level, bits))
    kv_own = jnp.concatenate(pieces, axis=0)
    kv_other = lax.ppermute(kv_own, "seq", [(i, i ^ 1) for i in range(seq_size)])

    packed = pl.pallas_call(
        functools.partial(attention_kernel, seq_size, held, kv_heads),
        out_shape=jax.ShapeDtypeStruct((head_size * held, query_len, HD), jnp.bfloat16),
        in_specs=[ANY] + [VMEM] * 4,
        out_specs=VMEM,
        scratch_shapes=[pltpu.SMEM(send.shape, send.dtype), pltpu.SemaphoreType.DMA],
        compiler_params=pltpu.CompilerParams(vmem_limit_bytes=40 * 1024 * 1024),
        name="attention",
    )(send, bits, kv_own, kv_other, queries)

    return lax.switch(
        level[0],
        [functools.partial(exchange, head_size, held, capacities) for capacities in levels],
        packed,
        slots,
    )


def solution(mesh):
    in_specs = (P("seq", "head"), P("seq", None), P("seq", None), P(), P(), P())
    out_specs = P("seq", "head")
    return jax.shard_map(
        per_device, mesh=mesh, in_specs=in_specs, out_specs=out_specs, check_vma=False
    )
```

```python
import functools
import math

import jax
import jax.numpy as jnp
from jax import lax
from jax.experimental import pallas as pl
from jax.experimental.pallas import tpu as pltpu
from jax.sharding import PartitionSpec as P

HD = 128
QH = 64
KVH = 8
BLK = 64
GROUP = QH // KVH
HEADS_AT_ONCE = 4
LANES = 128

floor_value = -1e30

SMEM = pl.BlockSpec(memory_space=pltpu.SMEM)
VMEM = pl.BlockSpec(memory_space=pltpu.VMEM)
ANY = pl.BlockSpec(memory_space=pl.ANY)
SMALL = 1024 * 1024


def shift_of(size):
    assert size & (size - 1) == 0
    return size.bit_length() - 1


def entry_bits(table):
    bits = jnp.zeros((1, table.shape[1]), jnp.int32)
    for entry in range(table.shape[0]):
        named = table[entry : entry + 1, :]
        bits = bits | jnp.where(named >= 0, jnp.int32(1) << jnp.maximum(named, 0), 0)
    return bits


class Tally:
    def __init__(self, head_size, held):
        self.width = shift_of(held) + 1
        self.per_word = 31 // self.width
        self.words = [jnp.int32(0)] * -(-head_size // self.per_word)

    def rank_and_count(self, owner):
        if len(self.words) == 1:
            at = owner * self.width
            rank = self.words[0] >> at
            self.words[0] = self.words[0] + (jnp.int32(1) << at)
        else:
            word = owner // self.per_word
            at = (owner - word * self.per_word) * self.width
            held_word = self.words[0]
            for index in range(1, len(self.words)):
                held_word = jnp.where(word == index, self.words[index], held_word)
            rank = held_word >> at
            one = jnp.int32(1) << at
            self.words = [w + jnp.where(word == index, one, 0) for index, w in enumerate(self.words)]
        return rank & ((1 << self.width) - 1)

    def count(self, owner):
        word = self.words[owner // self.per_word]
        return (word >> (owner % self.per_word * self.width)) & ((1 << self.width) - 1)


def route_kernel(head_size, held, levels, plan, vertical, slash, send, slots, level, bits):
    own = lax.axis_index("head")
    most = [jnp.int32(0)] * head_size
    for target in range(head_size):
        tally = Tally(head_size, held)
        for t in range(held):
            head = plan[target * held + t]
            owner = head >> shift_of(held)
            rank = tally.rank_and_count(owner)
            send[jnp.where(owner == own, head & (held - 1), held)] = ((owner ^ target) << shift_of(held)) + rank
        for owner in range(head_size):
            most[owner ^ target] = jnp.maximum(most[owner ^ target], tally.count(owner))
    tally = Tally(head_size, held)
    for distance in range(head_size):
        slots[head_size * held + distance] = 0
    for t in range(held):
        owner = plan[own * held + t] >> shift_of(held)
        rank = tally.rank_and_count(owner)
        distance = owner ^ own
        slots[(distance << shift_of(held)) + rank] = t
        slots[head_size * held + distance] = rank + 1
    chosen = jnp.int32(len(levels) - 1)
    for index in reversed(range(len(levels) - 1)):
        fits = most[1] <= levels[index][1]
        for distance in range(2, head_size):
            fits = fits & (most[distance] <= levels[index][distance])
        chosen = jnp.where(fits, index, chosen)
    level[0] = chosen
    bits[0:1, :] = entry_bits(vertical)
    bits[1:2, :] = entry_bits(slash)


def attention_kernel(
    seq_size, held, kv_heads, send, bits, kv_own, kv_other, query_ref, out_ref, send_here, copied
):
    send_copy = pltpu.make_async_copy(send, send_here, copied)
    send_copy.start()
    own_seq = lax.axis_index("seq")
    rest = (send_copy, bits, kv_own, kv_other, query_ref, out_ref, send_here)
    chips = seq_size // 2

    def pieces_of(chip):
        return tuple(m for m in range(chips) if chip ^ m <= chip)

    if chips == 4:
        cases = [((own_seq >> 1) == chip, pieces_of(chip)) for chip in range(chips)]
    else:
        cases = [(own_seq < 2, (0,)), (own_seq >= 2, tuple(range(chips)))]
    for applies, pieces in cases:

        @pl.when(applies)
        def _(pieces=pieces):
            attend(pieces, held, kv_heads, *rest)


def attend(pieces, held, kv_heads, send_copy, bits, kv_own, kv_other, query_ref, out_ref, send_here):
    query_len = query_ref.shape[0]
    key_len = query_len
    own_seq = lax.axis_index("seq")
    own_head = lax.axis_index("head")
    keys = 2 * len(pieces) * key_len

    place = lax.broadcasted_iota(jnp.int32, (1, keys), 1) // key_len
    own_core = place < len(pieces)
    place = jnp.where(own_core, place, place - len(pieces))
    piece = jnp.zeros_like(place)
    for at, m in enumerate(pieces):
        piece = jnp.where(place == at, m, piece)
    core = jnp.where(own_core, own_seq & 1, 1 - (own_seq & 1))
    block = ((own_seq >> 1) ^ piece) * 2 + core
    back = own_seq - block
    present = back >= 0
    back_shift = jnp.maximum(back, 0)
    heads = own_head * held + lax.broadcasted_iota(jnp.int32, (held, bits.shape[1]), 0)
    is_head = lax.broadcasted_iota(jnp.int32, (held, bits.shape[1]), 1) == heads
    vertical_bits, slash_bits = (
        jnp.sum(jnp.where(is_head, bits[kind : kind + 1, :], 0), axis=1, keepdims=True) for kind in range(2)
    )
    hit = ((vertical_bits >> block) | (slash_bits >> back_shift)) & 1
    bias = jnp.where((hit == 1) & present, 0.0, floor_value)
    row = lax.broadcasted_iota(jnp.int32, (query_len, LANES), 0)
    column = lax.broadcasted_iota(jnp.int32, (query_len, LANES), 1)
    causal = (column <= row) | (column >= key_len)
    score_scale = HD ** (-0.5) * math.log2(math.e)
    per_kv = held // kv_heads

    def rows_of(at):
        runs = []
        for m in pieces:
            if runs and runs[-1][1] == m:
                runs[-1][1] = m + 1
            else:
                runs.append([m, m + 1])
        return jnp.concatenate(
            [
                ref[first * key_len : last * key_len, at : at + HD]
                for ref in (kv_own, kv_other)
                for first, last in runs
            ],
            axis=0,
        )

    def scores_of(lead):
        heads = range(lead, min(lead + HEADS_AT_ONCE, held))
        key = rows_of(lead // per_kv * HD)
        query = jnp.concatenate([query_ref[:, i * HD : (i + 1) * HD] for i in heads], axis=0)
        return lax.dot_general(
            query, key, (((1,), (1,)), ((), ())), preferred_element_type=jnp.float32
        )

    ready = []
    following = scores_of(0)
    for lead in range(0, held, HEADS_AT_ONCE):
        heads = range(lead, min(lead + HEADS_AT_ONCE, held))
        scores = following
        if lead + HEADS_AT_ONCE < held:
            following = scores_of(lead + HEADS_AT_ONCE)
        value = rows_of((lead // per_kv + kv_heads) * HD)
        weights = []
        totals = []
        for at, i in enumerate(heads):
            masked = scores[at * query_len : (at + 1) * query_len] + bias[i : i + 1, :]
            own_block = jnp.where(causal, masked[:, :LANES], floor_value)
            masked = own_block if keys == LANES else jnp.concatenate([own_block, masked[:, LANES:]], axis=1)
            row_max = jnp.max(masked, axis=1, keepdims=True)
            weight = jnp.exp2((masked - row_max) * score_scale)
            totals.append(1.0 / jnp.sum(weight, axis=1, keepdims=True))
            weights.append(weight.astype(jnp.bfloat16))
        mixture = jnp.dot(
            jnp.concatenate(weights, axis=0), value, preferred_element_type=jnp.float32
        )
        for at, i in enumerate(heads):
            mix = mixture[at * query_len : (at + 1) * query_len]
            ready.append((i, (mix * totals[at]).astype(out_ref.dtype)))
        if len(pieces) > 1 or lead + HEADS_AT_ONCE >= held:
            if len(pieces) == 1 or lead == 0:
                send_copy.wait()
            for i, rows in ready:
                out_ref[send_here[i]] = rows
            ready = []


def place_kernel(head_size, held, sources, slots, *refs):
    out_ref, done = refs[-2:]
    for (distance, capacity), ref in zip(sources, refs):
        arriving = slots[head_size * held + distance]
        for rank in range(capacity):

            @pl.when(rank < arriving)
            def _(ref=ref, rank=rank, distance=distance):
                at = pl.multiple_of(slots[distance * held + rank] * HD, HD)
                pltpu.make_async_copy(ref.at[rank], out_ref.at[:, pl.ds(at, HD)], done).start()

    pltpu.make_async_copy(out_ref, out_ref, done).wait()


SHAPES = (
    (4, 4, 4), (5, 5, 4), (8, 4, 4), (5, 5, 5), (6, 6, 4), (9, 5, 4), (5, 6, 5), (6, 6, 5), (7, 7, 4), (5, 4, 6),
    (7, 5, 5), (9, 5, 5), (5, 7, 5), (6, 6, 6), (7, 7, 5), (8, 8, 4), (6, 4, 7), (8, 4, 6), (7, 7, 6), (8, 8, 5),
    (6, 5, 7), (7, 4, 8), (11, 6, 6), (7, 7, 7), (8, 8, 6), (9, 9, 5), (7, 5, 8), (8, 4, 9), (8, 8, 7), (9, 10, 5),
    (7, 6, 8), (8, 5, 9), (8, 8, 8), (9, 9, 7), (6, 6, 9), (9, 6, 10), (9, 9, 9), (11, 8, 10),
)


def capacity_levels(head_size, held):
    shapes = [tuple(max(1, held * part // 16) for part in shape) for shape in SHAPES]
    levels = []
    for near, *far in shapes + [(held,) * 3]:
        level = tuple(near if m < head_size // 2 else far[m % 2] for m in range(head_size))
        if level not in levels:
            levels.append(level)
    return levels


def exchange(head_size, held, capacities, packed, slots):
    order = sorted(range(1, head_size), key=lambda m: (m == head_size // 2, -m))
    arrived = [
        lax.ppermute(
            packed[m * held : m * held + capacities[m]], "head", [(i, i ^ m) for i in range(head_size)]
        )
        for m in order
    ]
    return pl.pallas_call(
        functools.partial(place_kernel, head_size, held, [(0, held)] + [(m, capacities[m]) for m in order]),
        out_shape=pltpu.HBM((packed.shape[1], held * HD), packed.dtype),
        in_specs=[SMEM] + [ANY] * head_size,
        out_specs=pl.BlockSpec(memory_space=pltpu.HBM),
        scratch_shapes=[pltpu.SemaphoreType.DMA],
        compiler_params=pltpu.CompilerParams(vmem_limit_bytes=SMALL),
        name="place",
    )(slots, packed, *arrived)


def per_device(queries, keys, values, vertical, slash, plan):
    seq_size = lax.axis_size("seq")
    head_size = lax.axis_size("head")
    query_len = queries.shape[0]
    held = queries.shape[1] // HD
    kv_heads = max(1, held // GROUP)
    chips = seq_size // 2
    assert query_len == BLK and plan.shape[0] == held * head_size and chips & (chips - 1) == 0

    levels = capacity_levels(head_size, held)
    send, slots, level, bits = pl.pallas_call(
        functools.partial(route_kernel, head_size, held, levels),
        out_shape=[
            jax.ShapeDtypeStruct((held + 1,), jnp.int32),
            jax.ShapeDtypeStruct((head_size * held + head_size,), jnp.int32),
            jax.ShapeDtypeStruct((1,), jnp.int32),
            jax.ShapeDtypeStruct((2, vertical.shape[0]), jnp.int32),
        ],
        in_specs=[SMEM, VMEM, VMEM],
        out_specs=[SMEM] * 3 + [VMEM],
        compiler_params=pltpu.CompilerParams(vmem_limit_bytes=SMALL),
        name="route",
    )(plan, vertical.T, slash.T)

    kv_at = lax.axis_index("head") * held // GROUP * HD
    kv = jnp.concatenate(
        [lax.dynamic_slice_in_dim(rows, kv_at, kv_heads * HD, axis=1) for rows in (keys, values)], axis=1
    )
    pieces = [kv]
    for m in range(1, chips):
        pairs = [(i, i ^ (2 * m)) for i in range(seq_size)]
        pieces.append(lax.ppermute(kv, "seq", pairs))
    pieces, send, slots, level, bits = lax.optimization_barrier((pieces, send, slots, level, bits))
    kv_own = jnp.concatenate(pieces, axis=0)
    kv_other = lax.ppermute(kv_own, "seq", [(i, i ^ 1) for i in range(seq_size)])

    packed = pl.pallas_call(
        functools.partial(attention_kernel, seq_size, held, kv_heads),
        out_shape=jax.ShapeDtypeStruct((head_size * held, query_len, HD), jnp.bfloat16),
        in_specs=[ANY] + [VMEM] * 4,
        out_specs=VMEM,
        scratch_shapes=[pltpu.SMEM(send.shape, send.dtype), pltpu.SemaphoreType.DMA],
        compiler_params=pltpu.CompilerParams(vmem_limit_bytes=40 * 1024 * 1024),
        name="attention",
    )(send, bits, kv_own, kv_other, queries)

    return lax.switch(
        level[0],
        [functools.partial(exchange, head_size, held, capacities) for capacities in levels],
        packed,
        slots,
    )


def solution(mesh):
    in_specs = (P("seq", "head"), P("seq", None), P("seq", None), P(), P(), P())
    out_specs = P("seq", "head")
    return jax.shard_map(
        per_device, mesh=mesh, in_specs=in_specs, out_specs=out_specs, check_vma=False
    )
```

```python
import functools
import math

import jax
import jax.numpy as jnp
from jax import lax
from jax.experimental import pallas as pl
from jax.experimental.pallas import tpu as pltpu
from jax.sharding import PartitionSpec as P

HD = 128
QH = 64
KVH = 8
BLK = 64
GROUP = QH // KVH
HEADS_AT_ONCE = 4
LANES = 128

floor_value = -1e30

SMEM = pl.BlockSpec(memory_space=pltpu.SMEM)
VMEM = pl.BlockSpec(memory_space=pltpu.VMEM)
ANY = pl.BlockSpec(memory_space=pl.ANY)
SMALL = 1024 * 1024


def shift_of(size):
    assert size & (size - 1) == 0
    return size.bit_length() - 1


def entry_bits(table):
    bits = jnp.zeros((1, table.shape[1]), jnp.int32)
    for entry in range(table.shape[0]):
        named = table[entry : entry + 1, :]
        bits = bits | jnp.where(named >= 0, jnp.int32(1) << jnp.maximum(named, 0), 0)
    return bits


class Tally:
    def __init__(self, head_size, held):
        self.width = shift_of(held) + 1
        self.per_word = 31 // self.width
        self.words = [jnp.int32(0)] * -(-head_size // self.per_word)

    def rank_and_count(self, owner):
        if len(self.words) == 1:
            at = owner * self.width
            rank = self.words[0] >> at
            self.words[0] = self.words[0] + (jnp.int32(1) << at)
        else:
            word = owner // self.per_word
            at = (owner - word * self.per_word) * self.width
            held_word = self.words[0]
            for index in range(1, len(self.words)):
                held_word = jnp.where(word == index, self.words[index], held_word)
            rank = held_word >> at
            one = jnp.int32(1) << at
            self.words = [w + jnp.where(word == index, one, 0) for index, w in enumerate(self.words)]
        return rank & ((1 << self.width) - 1)

    def count(self, owner):
        word = self.words[owner // self.per_word]
        return (word >> (owner % self.per_word * self.width)) & ((1 << self.width) - 1)


def route_kernel(head_size, held, levels, plan, vertical, slash, send, slots, level, bits):
    own = lax.axis_index("head")
    most = [jnp.int32(0)] * head_size
    for target in range(head_size):
        tally = Tally(head_size, held)
        for t in range(held):
            head = plan[target * held + t]
            owner = head >> shift_of(held)
            rank = tally.rank_and_count(owner)
            send[jnp.where(owner == own, head & (held - 1), held)] = ((owner ^ target) << shift_of(held)) + rank
        for owner in range(head_size):
            most[owner ^ target] = jnp.maximum(most[owner ^ target], tally.count(owner))
    tally = Tally(head_size, held)
    for distance in range(head_size):
        slots[head_size * held + distance] = 0
    for t in range(held):
        owner = plan[own * held + t] >> shift_of(held)
        rank = tally.rank_and_count(owner)
        distance = owner ^ own
        slots[(distance << shift_of(held)) + rank] = t
        slots[head_size * held + distance] = rank + 1
    chosen = jnp.int32(len(levels) - 1)
    for index in reversed(range(len(levels) - 1)):
        fits = most[1] <= levels[index][1]
        for distance in range(2, head_size):
            fits = fits & (most[distance] <= levels[index][distance])
        chosen = jnp.where(fits, index, chosen)
    level[0] = chosen
    bits[0:1, :] = entry_bits(vertical)
    bits[1:2, :] = entry_bits(slash)


def attention_kernel(
    seq_size, held, kv_heads, send, bits, kv_own, kv_other, query_ref, out_ref, send_here, copied
):
    send_copy = pltpu.make_async_copy(send, send_here, copied)
    send_copy.start()
    own_seq = lax.axis_index("seq")
    rest = (send_copy, bits, kv_own, kv_other, query_ref, out_ref, send_here)
    chips = seq_size // 2

    def pieces_of(chip):
        return tuple(m for m in range(chips) if chip ^ m <= chip)

    if chips == 4:
        cases = [((own_seq >> 1) == chip, pieces_of(chip)) for chip in range(chips)]
    else:
        cases = [(own_seq < 2, (0,)), (own_seq >= 2, tuple(range(chips)))]
    for applies, pieces in cases:

        @pl.when(applies)
        def _(pieces=pieces):
            attend(pieces, held, kv_heads, *rest)


def attend(pieces, held, kv_heads, send_copy, bits, kv_own, kv_other, query_ref, out_ref, send_here):
    query_len = query_ref.shape[0]
    key_len = query_len
    own_seq = lax.axis_index("seq")
    own_head = lax.axis_index("head")
    keys = 2 * len(pieces) * key_len

    place = lax.broadcasted_iota(jnp.int32, (1, keys), 1) // key_len
    own_core = place < len(pieces)
    place = jnp.where(own_core, place, place - len(pieces))
    piece = jnp.zeros_like(place)
    for at, m in enumerate(pieces):
        piece = jnp.where(place == at, m, piece)
    core = jnp.where(own_core, own_seq & 1, 1 - (own_seq & 1))
    block = ((own_seq >> 1) ^ piece) * 2 + core
    back = own_seq - block
    present = back >= 0
    back_shift = jnp.maximum(back, 0)
    heads = own_head * held + lax.broadcasted_iota(jnp.int32, (held, bits.shape[1]), 0)
    is_head = lax.broadcasted_iota(jnp.int32, (held, bits.shape[1]), 1) == heads
    vertical_bits, slash_bits = (
        jnp.sum(jnp.where(is_head, bits[kind : kind + 1, :], 0), axis=1, keepdims=True) for kind in range(2)
    )
    hit = ((vertical_bits >> block) | (slash_bits >> back_shift)) & 1
    bias = jnp.where((hit == 1) & present, 0.0, floor_value)
    row = lax.broadcasted_iota(jnp.int32, (query_len, LANES), 0)
    column = lax.broadcasted_iota(jnp.int32, (query_len, LANES), 1)
    causal = (column <= row) | (column >= key_len)
    score_scale = HD ** (-0.5) * math.log2(math.e)
    per_kv = held // kv_heads

    def rows_of(at):
        runs = []
        for m in pieces:
            if runs and runs[-1][1] == m:
                runs[-1][1] = m + 1
            else:
                runs.append([m, m + 1])
        return jnp.concatenate(
            [
                ref[first * key_len : last * key_len, at : at + HD]
                for ref in (kv_own, kv_other)
                for first, last in runs
            ],
            axis=0,
        )

    def scores_of(lead):
        heads = range(lead, min(lead + HEADS_AT_ONCE, held))
        key = rows_of(lead // per_kv * HD)
        query = jnp.concatenate([query_ref[:, i * HD : (i + 1) * HD] for i in heads], axis=0)
        return lax.dot_general(
            query, key, (((1,), (1,)), ((), ())), preferred_element_type=jnp.float32
        )

    ready = []
    following = scores_of(0)
    for lead in range(0, held, HEADS_AT_ONCE):
        heads = range(lead, min(lead + HEADS_AT_ONCE, held))
        scores = following
        if lead + HEADS_AT_ONCE < held:
            following = scores_of(lead + HEADS_AT_ONCE)
        value = rows_of((lead // per_kv + kv_heads) * HD)
        weights = []
        totals = []
        for at, i in enumerate(heads):
            masked = scores[at * query_len : (at + 1) * query_len] + bias[i : i + 1, :]
            own_block = jnp.where(causal, masked[:, :LANES], floor_value)
            masked = own_block if keys == LANES else jnp.concatenate([own_block, masked[:, LANES:]], axis=1)
            row_max = jnp.max(masked, axis=1, keepdims=True)
            weight = jnp.exp2((masked - row_max) * score_scale)
            totals.append(1.0 / jnp.sum(weight, axis=1, keepdims=True))
            weights.append(weight.astype(jnp.bfloat16))
        mixture = jnp.dot(
            jnp.concatenate(weights, axis=0), value, preferred_element_type=jnp.float32
        )
        for at, i in enumerate(heads):
            mix = mixture[at * query_len : (at + 1) * query_len]
            ready.append((i, (mix * totals[at]).astype(out_ref.dtype)))
    send_copy.wait()
    for i, rows in ready:
        out_ref[send_here[i]] = rows


def place_kernel(head_size, held, sources, slots, *refs):
    out_ref, done = refs[-2:]
    for (distance, capacity), ref in zip(sources, refs):
        arriving = slots[head_size * held + distance]
        for rank in range(capacity):

            @pl.when(rank < arriving)
            def _(ref=ref, rank=rank, distance=distance):
                at = pl.multiple_of(slots[distance * held + rank] * HD, HD)
                pltpu.make_async_copy(ref.at[rank], out_ref.at[:, pl.ds(at, HD)], done).start()

    pltpu.make_async_copy(out_ref, out_ref, done).wait()


SHAPES = (
    (4, 4, 4), (5, 5, 4), (8, 4, 4), (5, 5, 5), (6, 6, 4), (9, 5, 4), (5, 6, 5), (6, 6, 5), (7, 7, 4), (5, 4, 6),
    (7, 5, 5), (9, 5, 5), (5, 7, 5), (6, 6, 6), (7, 7, 5), (8, 8, 4), (6, 4, 7), (8, 4, 6), (7, 7, 6), (8, 8, 5),
    (6, 5, 7), (7, 4, 8), (11, 6, 6), (7, 7, 7), (8, 8, 6), (9, 9, 5), (7, 5, 8), (8, 4, 9), (8, 8, 7), (9, 10, 5),
    (7, 6, 8), (8, 5, 9), (8, 8, 8), (9, 9, 7), (6, 6, 9), (9, 6, 10), (9, 9, 9), (11, 8, 10),
)


def capacity_levels(head_size, held):
    shapes = [tuple(max(1, held * part // 16) for part in shape) for shape in SHAPES]
    levels = []
    for near, *far in shapes + [(held,) * 3]:
        level = tuple(near if m < head_size // 2 else far[m % 2] for m in range(head_size))
        if level not in levels:
            levels.append(level)
    return levels


def exchange(head_size, held, capacities, packed, slots):
    order = sorted(range(1, head_size), key=lambda m: (m == head_size // 2, -m))
    arrived = [
        lax.ppermute(
            packed[m * held : m * held + capacities[m]], "head", [(i, i ^ m) for i in range(head_size)]
        )
        for m in order
    ]
    return pl.pallas_call(
        functools.partial(place_kernel, head_size, held, [(0, held)] + [(m, capacities[m]) for m in order]),
        out_shape=pltpu.HBM((packed.shape[1], held * HD), packed.dtype),
        in_specs=[SMEM] + [ANY] * head_size,
        out_specs=pl.BlockSpec(memory_space=pltpu.HBM),
        scratch_shapes=[pltpu.SemaphoreType.DMA],
        compiler_params=pltpu.CompilerParams(vmem_limit_bytes=SMALL),
        name="place",
    )(slots, packed, *arrived)


def per_device(queries, keys, values, vertical, slash, plan):
    seq_size = lax.axis_size("seq")
    head_size = lax.axis_size("head")
    query_len = queries.shape[0]
    held = queries.shape[1] // HD
    kv_heads = max(1, held // GROUP)
    chips = seq_size // 2
    assert query_len == BLK and plan.shape[0] == held * head_size and chips & (chips - 1) == 0

    levels = capacity_levels(head_size, held)
    send, slots, level, bits = pl.pallas_call(
        functools.partial(route_kernel, head_size, held, levels),
        out_shape=[
            jax.ShapeDtypeStruct((held + 1,), jnp.int32),
            jax.ShapeDtypeStruct((head_size * held + head_size,), jnp.int32),
            jax.ShapeDtypeStruct((1,), jnp.int32),
            jax.ShapeDtypeStruct((2, vertical.shape[0]), jnp.int32),
        ],
        in_specs=[SMEM, VMEM, VMEM],
        out_specs=[SMEM] * 3 + [VMEM],
        compiler_params=pltpu.CompilerParams(vmem_limit_bytes=SMALL),
        name="route",
    )(plan, vertical.T, slash.T)

    kv_at = lax.axis_index("head") * held // GROUP * HD
    kv = jnp.concatenate(
        [lax.dynamic_slice_in_dim(rows, kv_at, kv_heads * HD, axis=1) for rows in (keys, values)], axis=1
    )
    pieces = [kv]
    for m in range(1, chips):
        pairs = [(i, i ^ (2 * m)) for i in range(seq_size)]
        pieces.append(lax.ppermute(kv, "seq", pairs))
    pieces, send, slots, level, bits = lax.optimization_barrier((pieces, send, slots, level, bits))
    kv_own = jnp.concatenate(pieces, axis=0)
    kv_other = lax.ppermute(kv_own, "seq", [(i, i ^ 1) for i in range(seq_size)])

    packed = pl.pallas_call(
        functools.partial(attention_kernel, seq_size, held, kv_heads),
        out_shape=jax.ShapeDtypeStruct((head_size * held, query_len, HD), jnp.bfloat16),
        in_specs=[ANY] + [VMEM] * 4,
        out_specs=VMEM,
        scratch_shapes=[pltpu.SMEM(send.shape, send.dtype), pltpu.SemaphoreType.DMA],
        compiler_params=pltpu.CompilerParams(vmem_limit_bytes=40 * 1024 * 1024),
        name="attention",
    )(send, bits, kv_own, kv_other, queries)

    return lax.switch(
        level[0],
        [functools.partial(exchange, head_size, held, capacities) for capacities in levels],
        packed,
        slots,
    )


def solution(mesh):
    in_specs = (P("seq", "head"), P("seq", None), P("seq", None), P(), P(), P())
    out_specs = P("seq", "head")
    return jax.shard_map(
        per_device, mesh=mesh, in_specs=in_specs, out_specs=out_specs, check_vma=False
    )
```

```python
import functools
import math

import jax
import jax.numpy as jnp
from jax import lax
from jax.experimental import pallas as pl
from jax.experimental.pallas import tpu as pltpu
from jax.sharding import PartitionSpec as P

HD = 128
QH = 64
KVH = 8
BLK = 64
GROUP = QH // KVH
HEADS_AT_ONCE = 4
LANES = 128

floor_value = -1e30

SMEM = pl.BlockSpec(memory_space=pltpu.SMEM)
VMEM = pl.BlockSpec(memory_space=pltpu.VMEM)
ANY = pl.BlockSpec(memory_space=pl.ANY)
SMALL = 1024 * 1024


def shift_of(size):
    assert size & (size - 1) == 0
    return size.bit_length() - 1


def entry_bits(table):
    bits = jnp.zeros((1, table.shape[1]), jnp.int32)
    for entry in range(table.shape[0]):
        named = table[entry : entry + 1, :]
        bits = bits | jnp.where(named >= 0, jnp.int32(1) << jnp.maximum(named, 0), 0)
    return bits


class Tally:
    def __init__(self, head_size, held):
        self.width = shift_of(held) + 1
        self.per_word = 31 // self.width
        self.words = [jnp.int32(0)] * -(-head_size // self.per_word)

    def rank_and_count(self, owner):
        if len(self.words) == 1:
            at = owner * self.width
            rank = self.words[0] >> at
            self.words[0] = self.words[0] + (jnp.int32(1) << at)
        else:
            word = owner // self.per_word
            at = (owner - word * self.per_word) * self.width
            held_word = self.words[0]
            for index in range(1, len(self.words)):
                held_word = jnp.where(word == index, self.words[index], held_word)
            rank = held_word >> at
            one = jnp.int32(1) << at
            self.words = [w + jnp.where(word == index, one, 0) for index, w in enumerate(self.words)]
        return rank & ((1 << self.width) - 1)

    def count(self, owner):
        word = self.words[owner // self.per_word]
        return (word >> (owner % self.per_word * self.width)) & ((1 << self.width) - 1)


def route_kernel(head_size, held, levels, plan, vertical, slash, send, slots, level, bits):
    own = lax.axis_index("head")
    most = [jnp.int32(0)] * head_size
    for target in range(head_size):
        tally = Tally(head_size, held)
        for t in range(held):
            head = plan[target * held + t]
            owner = head >> shift_of(held)
            rank = tally.rank_and_count(owner)
            send[jnp.where(owner == own, head & (held - 1), held)] = ((owner ^ target) << shift_of(held)) + rank
        for owner in range(head_size):
            most[owner ^ target] = jnp.maximum(most[owner ^ target], tally.count(owner))
    tally = Tally(head_size, held)
    for distance in range(head_size):
        slots[head_size * held + distance] = 0
    for t in range(held):
        owner = plan[own * held + t] >> shift_of(held)
        rank = tally.rank_and_count(owner)
        distance = owner ^ own
        slots[(distance << shift_of(held)) + rank] = t
        slots[head_size * held + distance] = rank + 1
    chosen = jnp.int32(len(levels) - 1)
    for index in reversed(range(len(levels) - 1)):
        fits = most[1] <= levels[index][1]
        for distance in range(2, head_size):
            fits = fits & (most[distance] <= levels[index][distance])
        chosen = jnp.where(fits, index, chosen)
    level[0] = chosen
    bits[0:1, :] = entry_bits(vertical)
    bits[1:2, :] = entry_bits(slash)


def attention_kernel(
    seq_size, held, kv_heads, send, bits, kv_own, kv_other, query_ref, out_ref, send_here, copied
):
    send_copy = pltpu.make_async_copy(send, send_here, copied)
    send_copy.start()
    own_seq = lax.axis_index("seq")
    rest = (send_copy, bits, kv_own, kv_other, query_ref, out_ref, send_here)
    chips = seq_size // 2

    def pieces_of(chip):
        return tuple(m for m in range(chips) if chip ^ m <= chip)

    if chips == 4:
        cases = [((own_seq >> 1) == chip, pieces_of(chip)) for chip in range(chips)]
    else:
        cases = [(own_seq < 2, (0,)), (own_seq >= 2, tuple(range(chips)))]
    for applies, pieces in cases:

        @pl.when(applies)
        def _(pieces=pieces):
            attend(pieces, held, kv_heads, *rest)


def attend(pieces, held, kv_heads, send_copy, bits, kv_own, kv_other, query_ref, out_ref, send_here):
    query_len = query_ref.shape[0]
    key_len = query_len
    own_seq = lax.axis_index("seq")
    own_head = lax.axis_index("head")
    keys = 2 * len(pieces) * key_len

    place = lax.broadcasted_iota(jnp.int32, (1, keys), 1) // key_len
    own_core = place < len(pieces)
    place = jnp.where(own_core, place, place - len(pieces))
    piece = jnp.zeros_like(place)
    for at, m in enumerate(pieces):
        piece = jnp.where(place == at, m, piece)
    core = jnp.where(own_core, own_seq & 1, 1 - (own_seq & 1))
    block = ((own_seq >> 1) ^ piece) * 2 + core
    back = own_seq - block
    present = back >= 0
    back_shift = jnp.maximum(back, 0)
    heads = own_head * held + lax.broadcasted_iota(jnp.int32, (held, bits.shape[1]), 0)
    is_head = lax.broadcasted_iota(jnp.int32, (held, bits.shape[1]), 1) == heads
    vertical_bits, slash_bits = (
        jnp.sum(jnp.where(is_head, bits[kind : kind + 1, :], 0), axis=1, keepdims=True) for kind in range(2)
    )
    hit = ((vertical_bits >> block) | (slash_bits >> back_shift)) & 1
    bias = jnp.where((hit == 1) & present, 0.0, floor_value)
    row = lax.broadcasted_iota(jnp.int32, (query_len, LANES), 0)
    column = lax.broadcasted_iota(jnp.int32, (query_len, LANES), 1)
    causal = (column <= row) | (column >= key_len)
    score_scale = HD ** (-0.5) * math.log2(math.e)
    per_kv = held // kv_heads
    together = per_kv if len(pieces) == 1 else HEADS_AT_ONCE

    def rows_of(at):
        runs = []
        for m in pieces:
            if runs and runs[-1][1] == m:
                runs[-1][1] = m + 1
            else:
                runs.append([m, m + 1])
        return jnp.concatenate(
            [
                ref[first * key_len : last * key_len, at : at + HD]
                for ref in (kv_own, kv_other)
                for first, last in runs
            ],
            axis=0,
        )

    def scores_of(lead):
        heads = range(lead, min(lead + together, held))
        key = rows_of(lead // per_kv * HD)
        query = jnp.concatenate([query_ref[:, i * HD : (i + 1) * HD] for i in heads], axis=0)
        return lax.dot_general(
            query, key, (((1,), (1,)), ((), ())), preferred_element_type=jnp.float32
        )

    ready = []
    following = scores_of(0)
    for lead in range(0, held, together):
        heads = range(lead, min(lead + together, held))
        scores = following
        if lead + together < held:
            following = scores_of(lead + together)
        value = rows_of((lead // per_kv + kv_heads) * HD)
        weights = []
        totals = []
        for at, i in enumerate(heads):
            masked = scores[at * query_len : (at + 1) * query_len] + bias[i : i + 1, :]
            own_block = jnp.where(causal, masked[:, :LANES], floor_value)
            masked = own_block if keys == LANES else jnp.concatenate([own_block, masked[:, LANES:]], axis=1)
            row_max = jnp.max(masked, axis=1, keepdims=True)
            weight = jnp.exp2((masked - row_max) * score_scale)
            totals.append(1.0 / jnp.sum(weight, axis=1, keepdims=True))
            weights.append(weight.astype(jnp.bfloat16))
        mixture = jnp.dot(
            jnp.concatenate(weights, axis=0), value, preferred_element_type=jnp.float32
        )
        for at, i in enumerate(heads):
            mix = mixture[at * query_len : (at + 1) * query_len]
            ready.append((i, (mix * totals[at]).astype(out_ref.dtype)))
    send_copy.wait()
    for i, rows in ready:
        out_ref[send_here[i]] = rows


def place_kernel(head_size, held, sources, slots, *refs):
    out_ref, done = refs[-2:]
    for (distance, capacity), ref in zip(sources, refs):
        arriving = slots[head_size * held + distance]
        for rank in range(capacity):

            @pl.when(rank < arriving)
            def _(ref=ref, rank=rank, distance=distance):
                at = pl.multiple_of(slots[distance * held + rank] * HD, HD)
                pltpu.make_async_copy(ref.at[rank], out_ref.at[:, pl.ds(at, HD)], done).start()

    pltpu.make_async_copy(out_ref, out_ref, done).wait()


SHAPES = (
    (4, 4, 4), (5, 5, 4), (8, 4, 4), (5, 5, 5), (6, 6, 4), (9, 5, 4), (5, 6, 5), (6, 6, 5), (7, 7, 4), (5, 4, 6),
    (7, 5, 5), (9, 5, 5), (5, 7, 5), (6, 6, 6), (7, 7, 5), (8, 8, 4), (6, 4, 7), (8, 4, 6), (7, 7, 6), (8, 8, 5),
    (6, 5, 7), (7, 4, 8), (11, 6, 6), (7, 7, 7), (8, 8, 6), (9, 9, 5), (7, 5, 8), (8, 4, 9), (8, 8, 7), (9, 10, 5),
    (7, 6, 8), (8, 5, 9), (8, 8, 8), (9, 9, 7), (6, 6, 9), (9, 6, 10), (9, 9, 9), (11, 8, 10),
)


def capacity_levels(head_size, held):
    shapes = [tuple(max(1, held * part // 16) for part in shape) for shape in SHAPES]
    levels = []
    for near, *far in shapes + [(held,) * 3]:
        level = tuple(near if m < head_size // 2 else far[m % 2] for m in range(head_size))
        if level not in levels:
            levels.append(level)
    return levels


def exchange(head_size, held, capacities, packed, slots):
    order = sorted(range(1, head_size), key=lambda m: (m == head_size // 2, -m))
    arrived = [
        lax.ppermute(
            packed[m * held : m * held + capacities[m]], "head", [(i, i ^ m) for i in range(head_size)]
        )
        for m in order
    ]
    return pl.pallas_call(
        functools.partial(place_kernel, head_size, held, [(0, held)] + [(m, capacities[m]) for m in order]),
        out_shape=pltpu.HBM((packed.shape[1], held * HD), packed.dtype),
        in_specs=[SMEM] + [ANY] * head_size,
        out_specs=pl.BlockSpec(memory_space=pltpu.HBM),
        scratch_shapes=[pltpu.SemaphoreType.DMA],
        compiler_params=pltpu.CompilerParams(vmem_limit_bytes=SMALL),
        name="place",
    )(slots, packed, *arrived)


def per_device(queries, keys, values, vertical, slash, plan):
    seq_size = lax.axis_size("seq")
    head_size = lax.axis_size("head")
    query_len = queries.shape[0]
    held = queries.shape[1] // HD
    kv_heads = max(1, held // GROUP)
    chips = seq_size // 2
    assert query_len == BLK and plan.shape[0] == held * head_size and chips & (chips - 1) == 0

    levels = capacity_levels(head_size, held)
    send, slots, level, bits = pl.pallas_call(
        functools.partial(route_kernel, head_size, held, levels),
        out_shape=[
            jax.ShapeDtypeStruct((held + 1,), jnp.int32),
            jax.ShapeDtypeStruct((head_size * held + head_size,), jnp.int32),
            jax.ShapeDtypeStruct((1,), jnp.int32),
            jax.ShapeDtypeStruct((2, vertical.shape[0]), jnp.int32),
        ],
        in_specs=[SMEM, VMEM, VMEM],
        out_specs=[SMEM] * 3 + [VMEM],
        compiler_params=pltpu.CompilerParams(vmem_limit_bytes=SMALL),
        name="route",
    )(plan, vertical.T, slash.T)

    kv_at = lax.axis_index("head") * held // GROUP * HD
    kv = jnp.concatenate(
        [lax.dynamic_slice_in_dim(rows, kv_at, kv_heads * HD, axis=1) for rows in (keys, values)], axis=1
    )
    pieces = [kv]
    for m in range(1, chips):
        pairs = [(i, i ^ (2 * m)) for i in range(seq_size)]
        pieces.append(lax.ppermute(kv, "seq", pairs))
    pieces, send, slots, level, bits = lax.optimization_barrier((pieces, send, slots, level, bits))
    kv_own = jnp.concatenate(pieces, axis=0)
    kv_other = lax.ppermute(kv_own, "seq", [(i, i ^ 1) for i in range(seq_size)])

    packed = pl.pallas_call(
        functools.partial(attention_kernel, seq_size, held, kv_heads),
        out_shape=jax.ShapeDtypeStruct((head_size * held, query_len, HD), jnp.bfloat16),
        in_specs=[ANY] + [VMEM] * 4,
        out_specs=VMEM,
        scratch_shapes=[pltpu.SMEM(send.shape, send.dtype), pltpu.SemaphoreType.DMA],
        compiler_params=pltpu.CompilerParams(vmem_limit_bytes=40 * 1024 * 1024),
        name="attention",
    )(send, bits, kv_own, kv_other, queries)

    return lax.switch(
        level[0],
        [functools.partial(exchange, head_size, held, capacities) for capacities in levels],
        packed,
        slots,
    )


def solution(mesh):
    in_specs = (P("seq", "head"), P("seq", None), P("seq", None), P(), P(), P())
    out_specs = P("seq", "head")
    return jax.shard_map(
        per_device, mesh=mesh, in_specs=in_specs, out_specs=out_specs, check_vma=False
    )
```
